128 devices in a mesh: pool: 2 (over y_lo), seq: 8 (over x, core), mp: 8 (over y_hi, z).
Axes of the slice: x: 4, y: 4 (y_hi: 2, y_lo: 2; y = y_hi * 2 + y_lo), z: 4, core: 2. Of those that a mesh axis runs over, the one named last changes fastest.
Arguments:
- prefill_q: bfloat16 [2, 4096, 128, 128], P('pool', 'seq', 'mp'), may hold values from -400 to 400
- prefill_k: bfloat16 [2, 4096, 8, 128], P('pool', 'seq', 'mp'), may hold values from -6 to 6
- prefill_v: bfloat16 [2, 4096, 8, 128], P('pool', 'seq', 'mp'), may hold values from -6 to 6
- prompt_len: int32 [2, 8], replicated, may hold values from 1 to 2560, 4096 in all within a row
- page_map: int32 [2, 48], replicated, may hold values from 0 to 47, each once within a row
- cache_k: bfloat16 [2, 128, 1024, 8, 128], P('pool', 'seq', None, 'mp'), may hold values from -6 to 6
- cache_v: bfloat16 [2, 128, 1024, 8, 128], P('pool', 'seq', None, 'mp'), may hold values from -6 to 6
- cache_len: int32 [2, 128], P('pool', 'seq'), may hold values from 1 to 1024, as said below
- decode_q: bfloat16 [2, 4, 128, 128, 128], P('pool', None, 'seq', 'mp'), may hold values from -400 to 400
- decode_k: bfloat16 [2, 4, 128, 8, 128], P('pool', None, 'seq', 'mp'), may hold values from -6 to 6
- decode_v: bfloat16 [2, 4, 128, 8, 128], P('pool', None, 'seq', 'mp'), may hold values from -6 to 6
Outputs:
- prefill_out: bfloat16 [2, 4096, 128, 128], P('pool', 'seq', 'mp')
- page_k: bfloat16 [2, 48, 128, 8, 128], P('pool', 'seq', None, 'mp')
- page_v: bfloat16 [2, 48, 128, 8, 128], P('pool', 'seq', None, 'mp')
- decode_out: bfloat16 [2, 4, 128, 128, 128], P('pool', None, 'seq', 'mp')
The draws below stay inside these ranges and needn't reach their ends.
Inputs may be any that keep to these rules, and one draw needn't show every extreme that they name: `prompt_len`: in each group the 8 lengths sum to 4096 and the largest is exactly 2560. `page_map`: each group's row names every page once. `cache_len`: each group has a request with exactly 1024 cached rows.
All inputs are finite; a program needn't handle non-finite values.
Results may differ from the reference program's by a relative error of at most 0.0045.
Values may be sent and summed in bfloat16 or wider, within the bound.
No kernel may reach another device: no remote copies, remote signals or barrier semaphores. Data moves between devices by JAX's collectives and lax.ppermute only.
A program may use at most 128 MiB of HBM per device.

```python
import math
import jax
import jax.numpy as jnp
import numpy as np
from jax import lax

H = 128
KV = 8
HD = 128
SEQ_DEV = 512
NPROMPT = 8
PAGE = 128
CACHE = 1024
STEPS = 4
SPAN = 4096
LONGEST = 2560
PAGES = 48
B = 128


def spiked_queries(key, array_shape, factor_low, factor_high, share):
    base_key, pick_key, size_key = jax.random.split(key, 3)
    values = jax.random.normal(base_key, array_shape, jnp.float32)
    row_shape = array_shape[:-1] + (1,)
    chosen = jax.random.uniform(pick_key, row_shape) < share
    factors = jnp.exp(jax.random.uniform(size_key, row_shape, minval=jnp.log(factor_low), maxval=jnp.log(factor_high)))
    return jnp.clip(values * jnp.where(chosen, factors, 1.0), -400.0, 400.0)


def draw_prefill_q(key, part):
    key = jax.random.fold_in(key, 5)
    values = spiked_queries(key, (2, SPAN, H, HD), 1.0, 1.0001, 0.0)
    return values.astype(jnp.bfloat16)


def draw_decode_q(key, part):
    key = jax.random.fold_in(key, 7)
    values = spiked_queries(key, (2, STEPS, B, H, HD), 1.0, 1.0001, 0.0)
    return values.astype(jnp.bfloat16)


def draw_cache_len(key, part):
    key = jax.random.fold_in(key, 9)
    length_key, place_key = jax.random.split(key)
    lengths = jax.random.randint(length_key, (2, B), 1, CACHE + 1)
    longest_slot = jax.random.randint(place_key, (2, 1), 0, B)
    slot_ids = jnp.arange(B, dtype=jnp.int32)[None, :]
    return jnp.where(slot_ids == longest_slot, CACHE, lengths).astype(jnp.int32)


def steps_of(rng, shape, pieces, low, high):
    def one(position, shards_of):
        draws = jax.random.uniform(jax.random.fold_in(jax.random.fold_in(rng, 6), position), (shards_of,), jnp.float32, low / len(pieces), high / len(pieces))
        return jnp.repeat(jnp.exp(draws), shape[position] // shards_of).reshape((-1,) + (1,) * (len(shape) - position - 1))

    gain = one(*pieces[0])
    for cut in pieces[1:]:
        gain = gain * one(*cut)
    return gain


def split_up(number_of, total, limit, slope):
    loads = [(1 << 20) // math.isqrt(grade ** slope) + 1 for grade in range(2, number_of + 1)]
    rest, holding = total - limit - (number_of - 1), [1] * (number_of - 1)
    while rest > 0:
        free = [i for i in range(number_of - 1) if holding[i] < limit]
        mass, budget = sum([loads[i] for i in free]), rest
        for i in free:
            extra = min(limit - holding[i], max(1, budget * loads[i] // mass), rest)
            holding[i] = holding[i] + extra
            rest = rest - extra
    return np.array([limit] + holding)


def ragged_sizes(stream_key, number_of, total, limit, lean):
    if number_of == 2:
        one = jax.random.randint(stream_key, (), max(1, total - limit), min(limit, total - 1) + 1)
        return jnp.stack([one, total - one])
    sizes = jnp.asarray(split_up(number_of, total, limit, lean), jnp.int32)
    twos = (number_of - 1) // 2
    source_of, sink = sizes[1:1 + 2 * twos:2], sizes[2:2 + 2 * twos:2]
    slack = jnp.minimum(source_of - 1, limit - sink)
    shifted = jax.random.randint(jax.random.fold_in(stream_key, 1), (twos,), 0, 1 << 20) % (slack + 1)
    sizes = sizes.at[1:1 + 2 * twos:2].set(source_of - shifted).at[2:2 + 2 * twos:2].set(sink + shifted)
    return sizes[jax.random.permutation(jax.random.fold_in(stream_key, 2), number_of)]


def scatter_about(rng, shape, spread, bound, pieces=(), kind=jnp.bfloat16):
    drawn = spread * jax.random.normal(rng, shape, jnp.float32)
    if pieces:
        drawn = drawn * steps_of(rng, shape, pieces, -0.22, 0.18)
    return jnp.clip(drawn, -bound, bound).astype(kind)


def setup_inputs(seed: int = 0) -> dict:
    keys = jax.random.split(jax.random.key(seed), 12)
    prefill_q = draw_prefill_q(jax.random.fold_in(keys[11], 71), 0)
    prefill_k = scatter_about(keys[1], (2, SPAN, KV, HD), 1.0, 6.0, ((0, 2), (1, 8), (2, 8)))
    prefill_v = scatter_about(keys[2], (2, SPAN, KV, HD), 1.0, 6.0, ((0, 2), (1, 8), (2, 8)))
    prompt_len = jax.vmap(lambda own: ragged_sizes(own, NPROMPT, SPAN, LONGEST, 2))(jax.random.split(keys[3], 2)).reshape((2, NPROMPT)).astype(jnp.int32)
    page_map = jax.vmap(lambda own: jax.random.permutation(own, PAGES))(jax.random.split(keys[4], 2)).reshape((2, PAGES)).astype(jnp.int32)
    cache_k = scatter_about(keys[5], (2, B, CACHE, KV, HD), 1.0, 6.0, ((0, 2), (1, 8), (3, 8)))
    cache_v = scatter_about(keys[6], (2, B, CACHE, KV, HD), 1.0, 6.0, ((0, 2), (1, 8), (3, 8)))
    cache_len = draw_cache_len(jax.random.fold_in(keys[11], 71), 0)
    decode_q = draw_decode_q(jax.random.fold_in(keys[11], 71), 0)
    decode_k = scatter_about(keys[9], (2, STEPS, B, KV, HD), 1.0, 6.0, ((0, 2), (2, 8), (3, 8)))
    decode_v = scatter_about(keys[10], (2, STEPS, B, KV, HD), 1.0, 6.0, ((0, 2), (2, 8), (3, 8)))
    return {"prefill_q": prefill_q, "prefill_k": prefill_k, "prefill_v": prefill_v, "prompt_len": prompt_len, "page_map": page_map, "cache_k": cache_k, "cache_v": cache_v, "cache_len": cache_len, "decode_q": decode_q, "decode_k": decode_k, "decode_v": decode_v}


NEG = -1.0e30


def segment_of(positions, lengths):
    prompt_ends = jnp.cumsum(lengths).astype(jnp.int32)
    return jnp.sum((positions[:, None] >= prompt_ends[None, :]).astype(jnp.int32), axis=1).astype(jnp.int32)


def page_sources(lengths, mapping, page_ids, page_rows):
    prompts = lengths.shape[0]
    blocks = ((lengths + page_rows - 1) // page_rows).astype(jnp.int32)
    first_block = (jnp.cumsum(blocks) - blocks).astype(jnp.int32)
    starts = (jnp.cumsum(lengths) - lengths).astype(jnp.int32)
    used_blocks = jnp.sum(blocks).astype(jnp.int32)
    slot_ids = jnp.arange(mapping.shape[0], dtype=jnp.int32)
    matches = mapping[None, :] == page_ids[:, None]
    logical = jnp.sum(jnp.where(matches, slot_ids[None, :], 0), axis=1).astype(jnp.int32)
    owners = jnp.sum((first_block[None, :] <= logical[:, None]).astype(jnp.int32), axis=1).astype(jnp.int32) - 1
    chosen = jnp.arange(prompts, dtype=jnp.int32)[None, :] == owners[:, None]
    own_first = jnp.sum(jnp.where(chosen, first_block[None, :], 0), axis=1).astype(jnp.int32)
    own_length = jnp.sum(jnp.where(chosen, lengths[None, :], 0), axis=1).astype(jnp.int32)
    own_start = jnp.sum(jnp.where(chosen, starts[None, :], 0), axis=1).astype(jnp.int32)
    offset = (logical - own_first)[:, None] * page_rows + jnp.arange(page_rows, dtype=jnp.int32)[None, :]
    usable = (logical < used_blocks)[:, None] & (offset < own_length[:, None])
    source = (own_start[:, None] + offset).astype(jnp.int32)
    return source, usable


def prefill_group(queries, key_rows, value_rows, lengths):
    span_rows = queries.shape[0]
    group_size = H // KV
    score_scale = HD ** -0.5
    positions = jnp.arange(span_rows, dtype=jnp.int32)
    segments = segment_of(positions, lengths)
    block_count = span_rows // SEQ_DEV
    q_heads = queries.astype(jnp.float32).reshape(block_count, SEQ_DEV, KV, group_size, HD).transpose(2, 0, 1, 3, 4)
    k_heads = key_rows.astype(jnp.float32).transpose(1, 0, 2)
    v_heads = value_rows.astype(jnp.float32).transpose(1, 0, 2)
    q_pos = positions.reshape(block_count, SEQ_DEV)
    q_seg = segments.reshape(block_count, SEQ_DEV)

    def per_head(inputs):
        q_head, k_head, v_head = inputs

        def per_block(block):
            q_block, block_pos, block_seg = block
            scores = jnp.einsum("qrd,kd->qrk", q_block, k_head) * score_scale
            allowed = (positions[None, :] <= block_pos[:, None]) & (segments[None, :] == block_seg[:, None])
            scores = jnp.where(allowed[:, None, :], scores, NEG)
            highest = jnp.max(scores, axis=2, keepdims=True)
            weights = jnp.where(allowed[:, None, :], jnp.exp(scores - highest), 0.0)
            denominator = jnp.sum(weights, axis=2)
            rounded = lax.optimization_barrier(weights.astype(jnp.bfloat16)).astype(jnp.float32)
            mixed = jnp.einsum("qrk,kd->qrd", rounded, v_head)
            return mixed / denominator[..., None]

        return lax.map(per_block, (q_head, q_pos, q_seg))

    outputs = lax.map(per_head, (q_heads, k_heads, v_heads))
    return outputs.transpose(1, 2, 0, 3, 4).reshape(span_rows, H, HD).astype(jnp.bfloat16)


def decode_group(queries, cache_keys, cache_values, lengths, new_keys, new_values):
    group_size = H // KV
    score_scale = HD ** -0.5
    q_heads = queries.astype(jnp.float32).reshape(STEPS, B, KV, group_size, HD).transpose(2, 0, 1, 3, 4)
    ck_heads = cache_keys.transpose(2, 0, 1, 3)
    cv_heads = cache_values.transpose(2, 0, 1, 3)
    nk_heads = new_keys.transpose(2, 0, 1, 3)
    nv_heads = new_values.transpose(2, 0, 1, 3)
    cache_mask = jnp.arange(CACHE, dtype=jnp.int32)[None, :] < lengths[:, None]
    step_ids = jnp.arange(STEPS, dtype=jnp.int32)
    new_mask = step_ids[None, :] <= step_ids[:, None]

    def per_head(inputs):
        q_head, ck_head, cv_head, nk_head, nv_head = inputs
        old_scores = jnp.einsum("tbrd,bjd->tbrj", q_head, ck_head.astype(jnp.float32)) * score_scale
        old_scores = jnp.where(cache_mask[None, :, None, :], old_scores, NEG)
        new_scores = jnp.einsum("tbrd,ubd->tbru", q_head, nk_head.astype(jnp.float32)) * score_scale
        new_scores = jnp.where(new_mask[:, None, None, :], new_scores, NEG)
        highest = jnp.maximum(jnp.max(old_scores, axis=3), jnp.max(new_scores, axis=3))[..., None]
        old_weights = jnp.where(cache_mask[None, :, None, :], jnp.exp(old_scores - highest), 0.0)
        new_weights = jnp.where(new_mask[:, None, None, :], jnp.exp(new_scores - highest), 0.0)
        denominator = jnp.sum(old_weights, axis=3) + jnp.sum(new_weights, axis=3)
        old_rounded = lax.optimization_barrier(old_weights.astype(jnp.bfloat16)).astype(jnp.float32)
        new_rounded = lax.optimization_barrier(new_weights.astype(jnp.bfloat16)).astype(jnp.float32)
        mixed = jnp.einsum("tbrj,bjd->tbrd", old_rounded, cv_head.astype(jnp.float32))
        mixed = mixed + jnp.einsum("tbru,ubd->tbrd", new_rounded, nv_head.astype(jnp.float32))
        return mixed / denominator[..., None]

    outputs = lax.map(per_head, (q_heads, ck_heads, cv_heads, nk_heads, nv_heads))
    return outputs.transpose(1, 2, 0, 3, 4).reshape(STEPS, B, H, HD).astype(jnp.bfloat16)


def reference(prefill_q, prefill_k, prefill_v, prompt_len, page_map, cache_k, cache_v, cache_len, decode_q, decode_k, decode_v):
    prefill_parts = []
    key_pages = []
    value_pages = []
    decode_parts = []
    for group in range(2):
        prefill_parts.append(prefill_group(prefill_q[group], prefill_k[group], prefill_v[group], prompt_len[group]))
        other = 1 - group
        source, usable = page_sources(prompt_len[other], page_map[other], jnp.arange(PAGES, dtype=jnp.int32), PAGE)
        flat_source = source.reshape(-1)
        flat_usable = usable.reshape(-1)[:, None, None]
        taken_k = jnp.take(prefill_k[other], flat_source, axis=0)
        taken_v = jnp.take(prefill_v[other], flat_source, axis=0)
        key_pages.append(jnp.where(flat_usable, taken_k, jnp.zeros_like(taken_k)).reshape(PAGES, PAGE, KV, HD))
        value_pages.append(jnp.where(flat_usable, taken_v, jnp.zeros_like(taken_v)).reshape(PAGES, PAGE, KV, HD))
        decode_parts.append(decode_group(decode_q[group], cache_k[group], cache_v[group], cache_len[group], decode_k[group], decode_v[group]))
    return (jnp.stack(prefill_parts), jnp.stack(key_pages), jnp.stack(value_pages), jnp.stack(decode_parts))
```

```python
import functools

import jax
import jax.numpy as jnp
from jax import lax
from jax.experimental import pallas as pl
from jax.experimental.pallas import tpu as pltpu
from jax.sharding import PartitionSpec as P

PAGE = 128
PAGES_DEV = 6
NPROMPT = 8
NPAGES = 48
SEQ = 8
ROWS = 512
HEADS = 16
HD = 128
SPAN = SEQ * ROWS
PAD = 512
KB = 512
TILE_POS = 128
TILE = TILE_POS * HEADS
TILES = ROWS // TILE_POS
CHUNK = 512
SLOW_CHUNK = 256
DEC_BLOCK = 4
NEG = -1e30
SCALE = HD ** -0.5
SCALE2 = SCALE * 1.4426950408889634
LOW = 2.0 ** -80
HIGH = 2.0 ** 100
VMEM = 56 * 1024 * 1024

dot_nt = functools.partial(
    lax.dot_general, dimension_numbers=(((1,), (1,)), ((), ())), preferred_element_type=jnp.float32
)
dot_nn = functools.partial(jnp.dot, preferred_element_type=jnp.float32)


def decode_kernel(len_ref, q_ref, ck_ref, cv_ref, nk_ref, nv_ref, o_ref):
    steps, block = q_ref.shape[0], q_ref.shape[1]
    cache = ck_ref.shape[1]
    slots = nk_ref.shape[0] // steps
    rows = steps * HEADS
    first = pl.program_id(0) * block
    new_keys = nk_ref[...]
    new_values = nv_ref[...]
    lane = lax.broadcasted_iota(jnp.int32, (rows, cache), 1)
    new_lane = lax.broadcasted_iota(jnp.int32, (rows, steps * slots), 1)
    step = lax.broadcasted_iota(jnp.int32, (rows, steps * slots), 0) // HEADS
    for i in range(block):
        queries = q_ref[:, i].reshape(rows, HD)
        length = len_ref[0, first + i]
        old_ok = lane < length
        new_ok = (new_lane % slots == first + i) & (new_lane // slots <= step)
        old = jnp.where(old_ok, dot_nt(queries, ck_ref[i]) * SCALE, NEG)
        new = jnp.where(new_ok, dot_nt(queries, new_keys) * SCALE, NEG)
        top = jnp.maximum(jnp.max(old, axis=1, keepdims=True), jnp.max(new, axis=1, keepdims=True))
        old_w = jnp.exp(old - top)
        new_w = jnp.exp(new - top)
        total = jnp.sum(old_w, axis=1, keepdims=True) + jnp.sum(new_w, axis=1, keepdims=True)
        mixed = dot_nn(old_w.astype(jnp.bfloat16), cv_ref[i]) + dot_nn(
            new_w.astype(jnp.bfloat16), new_values
        )
        o_ref[:, i] = (mixed / total).astype(jnp.bfloat16).reshape(steps, HEADS, HD)


def decode_call(lengths, q, ck, cv, nk, nv):
    steps, slots = q.shape[0], q.shape[1]
    cache = ck.shape[1]
    return pl.pallas_call(
        decode_kernel,
        name="decode",
        grid=(slots // DEC_BLOCK,),
        in_specs=[
            pl.BlockSpec(memory_space=pltpu.SMEM),
            pl.BlockSpec((steps, DEC_BLOCK, HEADS, HD), lambda i: (0, i, 0, 0)),
            pl.BlockSpec((DEC_BLOCK, cache, HD), lambda i: (i, 0, 0)),
            pl.BlockSpec((DEC_BLOCK, cache, HD), lambda i: (i, 0, 0)),
            pl.BlockSpec((steps * slots, HD), lambda i: (0, 0)),
            pl.BlockSpec((steps * slots, HD), lambda i: (0, 0)),
        ],
        out_specs=pl.BlockSpec((steps, DEC_BLOCK, HEADS, HD), lambda i: (0, i, 0, 0)),
        out_shape=jax.ShapeDtypeStruct(q.shape, jnp.bfloat16),
        compiler_params=pltpu.CompilerParams(vmem_limit_bytes=VMEM),
        cost_estimate=pl.CostEstimate(
            flops=4 * 64 * 1088 * 128 * 16, bytes_accessed=9 << 20, transcendentals=64 * 1088 * 16
        ),
    )(lengths, q, ck, cv, nk, nv)


def piece_seq(me, chips, swapped):
    core = me ^ 1 if swapped else me
    return (core + 2 * chips + SEQ) % SEQ


PIECES = ((0, False), (-1, False), (1, False), (2, False), (0, True), (-1, True), (1, True), (2, True))


def gather_kernel(len_ref, map_ref, *refs):
    pieces = refs[: len(PIECES)]
    kfull, vturned, pk_ref, pv_ref, vfull, slot_of = refs[len(PIECES) :]
    me = lax.axis_index("seq")
    own = lax.axis_index("pool")
    kfull[:PAD, :] = jnp.zeros((PAD, HD), jnp.bfloat16)
    vturned[:, :PAD] = jnp.zeros((HD, PAD), jnp.bfloat16)
    for (chips, swapped), piece in zip(PIECES, pieces):
        at = pl.multiple_of(piece_seq(me, chips, swapped) * ROWS, ROWS)
        kfull[pl.ds(at + PAD, ROWS), :] = piece[:ROWS, :]
        values = piece[ROWS:, :]
        vfull[pl.ds(at, ROWS), :] = values
        vturned[:, pl.ds(at + PAD, ROWS)] = values.astype(jnp.float32).T.astype(jnp.bfloat16)

    def place(b, _):
        page = map_ref[own, b]

        @pl.when(page // PAGES_DEV == me)
        def _():
            slot_of[page % PAGES_DEV] = b

        return 0

    lax.fori_loop(0, NPAGES, place, 0)
    window = 2 * PAGE
    row = lax.broadcasted_iota(jnp.int32, (PAGE, window), 0)
    col = lax.broadcasted_iota(jnp.int32, (PAGE, window), 1)
    for i in range(PAGES_DEV):
        b = slot_of[i]
        first = jnp.int32(0)
        start = jnp.int32(0)
        source = jnp.int32(0)
        count = jnp.int32(0)
        for prompt in range(NPROMPT):
            length = len_ref[own, prompt]
            blocks = (length + PAGE - 1) // PAGE
            inside = (b >= first) & (b < first + blocks)
            offset = (b - first) * PAGE
            source = jnp.where(inside, start + offset, source)
            count = jnp.where(inside, jnp.minimum(length - offset, PAGE), count)
            first = first + blocks
            start = start + length
        low = pl.multiple_of(jnp.minimum(source // 16 * 16, SPAN - window), 16)
        hit = ((low + col) == (source + row)) & (row < count)
        pick = jnp.where(hit, 1.0, 0.0).astype(jnp.bfloat16)
        here = slice(i * PAGE, (i + 1) * PAGE)
        pk_ref[here, :] = dot_nn(pick, kfull[pl.ds(low + PAD, window), :]).astype(jnp.bfloat16)
        pv_ref[here, :] = dot_nn(pick, vfull[pl.ds(low, window), :]).astype(jnp.bfloat16)


def gather_call(prompt_len, page_map, pieces):
    rows = PAGES_DEV * PAGE
    return pl.pallas_call(
        gather_kernel,
        name="gather_pages",
        in_specs=[pl.BlockSpec(memory_space=pltpu.SMEM)] * 2
        + [pl.BlockSpec(memory_space=pltpu.VMEM)] * len(PIECES),
        out_specs=[pl.BlockSpec(memory_space=pltpu.VMEM)] * 4,
        out_shape=[
            jax.ShapeDtypeStruct((PAD + SPAN, HD), jnp.bfloat16),
            jax.ShapeDtypeStruct((HD, PAD + SPAN), jnp.bfloat16),
            jax.ShapeDtypeStruct((rows, HD), jnp.bfloat16),
            jax.ShapeDtypeStruct((rows, HD), jnp.bfloat16),
        ],
        scratch_shapes=[pltpu.VMEM((SPAN, HD), jnp.bfloat16), pltpu.SMEM((PAGES_DEV,), jnp.int32)],
        compiler_params=pltpu.CompilerParams(vmem_limit_bytes=VMEM),
        cost_estimate=pl.CostEstimate(flops=12 * 2 * 128 * 256 * 128, bytes_accessed=5 << 20, transcendentals=0),
    )(prompt_len, page_map, *pieces)


def prefill_kernel(len_ref, q_hbm, k_ref, v_ref, o_hbm, q_ref, o_ref, acc, total, weights, q_sem, o_sem):
    me = lax.axis_index("seq")
    own = lax.axis_index("pool")
    chunks = TILE // CHUNK

    def q_copy(t):
        at = pl.ds(pl.multiple_of(t * TILE, TILE), TILE)
        return pltpu.make_async_copy(q_hbm.at[at], q_ref.at[at], q_sem.at[t])

    def o_copy(t):
        at = pl.ds(pl.multiple_of(t * TILE, TILE), TILE)
        return pltpu.make_async_copy(o_ref.at[at], o_hbm.at[at], o_sem.at[t])

    for t in range(TILES):
        q_copy(t).start()

    def segment_start(position):
        start = jnp.int32(0)
        end = jnp.int32(0)
        for prompt in range(NPROMPT):
            end = end + len_ref[own, prompt]
            start = jnp.where(end <= position, end, start)
        return start

    def first_position(t):
        return me * ROWS + t * TILE_POS

    def block_count(t):
        low = segment_start(first_position(t))
        return (first_position(t) + TILE_POS - low + KB - 1) // KB

    def block_start(t, j):
        return first_position(t) + TILE_POS - (j + 1) * KB

    def limits(t, c, width):
        lane = lax.broadcasted_iota(jnp.int32, (1, width), 1)
        q_pos = first_position(t) + c * (width // HEADS) + lane // HEADS
        return segment_start(q_pos), q_pos

    def key_at(t, j):
        return pl.ds(pl.multiple_of(block_start(t, j) + PAD, TILE_POS), KB)

    def scores(t, j, c, width):
        at = pl.ds(pl.multiple_of(t * TILE + c * width, width), width)
        return dot_nt(k_ref[key_at(t, j), :], q_ref[at, :]) * SCALE2

    def allowed(t, j, c, width):
        low, high = limits(t, c, width)
        k_pos = block_start(t, j) + lax.broadcasted_iota(jnp.int32, (KB, width), 0)
        return (k_pos >= low) & (k_pos <= high)

    def put(t, j, c, slot, masked):
        at = slice(c * CHUNK, (c + 1) * CHUNK)
        terms = jnp.exp2(scores(t, j, c, CHUNK))
        if masked:
            terms = jnp.where(allowed(t, j, c, CHUNK), terms, 0.0)
        weights[slot, :, at] = terms.astype(jnp.bfloat16)
        return jnp.sum(terms.reshape(KB // 8, 8, CHUNK), axis=0)

    def mix(t, j, c, slot):
        at = slice(c * CHUNK, (c + 1) * CHUNK)
        acc[:, at] += dot_nn(v_ref[:, key_at(t, j)], weights[slot, :, at])

    def slow_tile(t):
        width = SLOW_CHUNK

        def one(c, _):
            def block(j, carried):
                top, below, mixed = carried
                ok = allowed(t, j, c, width)
                here = jnp.where(ok, scores(t, j, c, width), NEG)
                new_top = jnp.maximum(top, jnp.max(here, axis=0, keepdims=True))
                terms = jnp.where(ok, jnp.exp2(here - new_top), 0.0)
                scale = jnp.exp2(top - new_top)
                below = below * scale + jnp.sum(terms, axis=0, keepdims=True)
                mixed = mixed * scale + dot_nn(v_ref[:, key_at(t, j)], terms.astype(jnp.bfloat16))
                return new_top, below, mixed

            _, below, mixed = lax.fori_loop(
                0,
                block_count(t),
                block,
                (
                    jnp.full((1, width), NEG, jnp.float32),
                    jnp.zeros((1, width), jnp.float32),
                    jnp.zeros((HD, width), jnp.float32),
                ),
            )
            at = pl.ds(pl.multiple_of(t * TILE + c * width, width), width)
            o_ref[at, :] = (mixed / below).T.astype(jnp.bfloat16)
            return 0

        lax.fori_loop(0, TILE // width, one, 0)

    def finish(t):
        below = jnp.sum(total[...], axis=0, keepdims=True)
        at = pl.ds(pl.multiple_of(t * TILE, TILE), TILE)
        o_ref[at, :] = (acc[...] / below).T.astype(jnp.bfloat16)
        acc[...] = jnp.zeros_like(acc)
        bad = jnp.max(jnp.where((below >= LOW) & (below <= HIGH), 0.0, 1.0))

        @pl.when(bad > 0.0)
        def _():
            slow_tile(t)

        o_copy(t).start()

    def step(t, j, count, slot, last):
        wrap = j + 1 == count
        t2 = jnp.where(wrap, t + 1, t)
        j2 = jnp.where(wrap, 0, j + 1)
        t2c = jnp.minimum(t2, TILES - 1)
        masked = (j2 == 0) | (segment_start(first_position(t2c) + TILE_POS - 1) > block_start(t2c, j2))

        @pl.when(wrap & jnp.logical_not(last))
        def _():
            q_copy(t2c).wait()

        def both(is_masked):
            sums = []
            for c in range(chunks):
                sums.append(put(t2c, j2, c, 1 - slot, is_masked))
                mix(t, j, c, slot)
            return sums

        def run(is_masked):
            sums = both(is_masked)

            @pl.when(wrap)
            def _():
                finish(t)
                total[...] = jnp.zeros_like(total)

            for c in range(chunks):
                total[:, c * CHUNK : (c + 1) * CHUNK] += sums[c]

        @pl.when(masked & jnp.logical_not(last))
        def _():
            run(True)

        @pl.when(jnp.logical_not(masked | last))
        def _():
            run(False)

        @pl.when(last)
        def _():
            for c in range(chunks):
                mix(t, j, c, slot)
            finish(t)

        return t2, j2, jnp.where(wrap, block_count(t2c), count)

    items = jnp.int32(0)
    for t in range(TILES):
        items = items + block_count(t)
    q_copy(0).wait()
    acc[...] = jnp.zeros_like(acc)
    for c in range(chunks):
        total[:, c * CHUNK : (c + 1) * CHUNK] = put(0, 0, c, 0, True)

    def pair(i, state):
        state = step(*state, 0, 2 * i + 1 == items)

        def second(state):
            return step(*state, 1, 2 * i + 2 == items)

        return lax.cond(2 * i + 1 < items, second, lambda s: s, state)

    lax.fori_loop(0, (items + 1) // 2, pair, (jnp.int32(0), jnp.int32(0), block_count(0)))
    for t in range(TILES):
        o_copy(t).wait()


def prefill_call(prompt_len, q, keys, values):
    return pl.pallas_call(
        prefill_kernel,
        name="prefill",
        in_specs=[
            pl.BlockSpec(memory_space=pltpu.SMEM),
            pl.BlockSpec(memory_space=pl.ANY),
            pl.BlockSpec(memory_space=pltpu.VMEM),
            pl.BlockSpec(memory_space=pltpu.VMEM),
        ],
        out_specs=pl.BlockSpec(memory_space=pl.ANY),
        out_shape=jax.ShapeDtypeStruct(q.shape, jnp.bfloat16),
        scratch_shapes=[
            pltpu.VMEM((TILES * TILE, HD), jnp.bfloat16),
            pltpu.VMEM((TILES * TILE, HD), jnp.bfloat16),
            pltpu.VMEM((HD, TILE), jnp.float32),
            pltpu.VMEM((8, TILE), jnp.float32),
            pltpu.VMEM((2, KB, TILE), jnp.bfloat16),
            pltpu.SemaphoreType.DMA((TILES,)),
            pltpu.SemaphoreType.DMA((TILES,)),
        ],
        compiler_params=pltpu.CompilerParams(vmem_limit_bytes=VMEM),
        cost_estimate=pl.CostEstimate(
            flops=4 * 8192 * 2304 * 128, bytes_accessed=6 << 20, transcendentals=8192 * 2304
        ),
    )(prompt_len, q, keys, values)


def on_device(
    prefill_q,
    prefill_k,
    prefill_v,
    prompt_len,
    page_map,
    cache_k,
    cache_v,
    cache_len,
    decode_q,
    decode_k,
    decode_v,
):
    def chip_shift(x, chips):
        return lax.ppermute(x, "seq", [(j, (j + 2 * chips) % SEQ) for j in range(SEQ)])

    def core_swap(x):
        return lax.ppermute(x, "seq", [(j, j ^ 1) for j in range(SEQ)])

    own = jnp.concatenate([prefill_k[0, :, 0], prefill_v[0, :, 0]], axis=0)
    right = chip_shift(own, 1)
    left = chip_shift(own, -1)
    far = chip_shift(own, 2)
    straight = [own, right, left, far]
    pieces = straight + [core_swap(x) for x in straight]
    steps, slots = decode_q.shape[1], decode_q.shape[2]
    decode_out = decode_call(
        cache_len,
        decode_q[0],
        cache_k[0, :, :, 0],
        cache_v[0, :, :, 0],
        decode_k[0, :, :, 0].reshape(steps * slots, HD),
        decode_v[0, :, :, 0].reshape(steps * slots, HD),
    )
    keys, values, pk, pv = gather_call(prompt_len, page_map, pieces)
    page_k = lax.ppermute(pk, "pool", [(0, 1), (1, 0)])
    page_v = lax.ppermute(pv, "pool", [(0, 1), (1, 0)])
    prefill_out = prefill_call(prompt_len, prefill_q[0].reshape(ROWS * HEADS, HD), keys, values)
    return (
        prefill_out.reshape(prefill_q.shape),
        page_k.reshape(1, PAGES_DEV, PAGE, 1, HD),
        page_v.reshape(1, PAGES_DEV, PAGE, 1, HD),
        decode_out[None],
    )


def solution(mesh):
    placed = (
        P("pool", "seq", "mp", None),
        P("pool", "seq", "mp", None),
        P("pool", "seq", "mp", None),
        P(),
        P(),
        P("pool", "seq", None, "mp", None),
        P("pool", "seq", None, "mp", None),
        P("pool", "seq"),
        P("pool", None, "seq", "mp", None),
        P("pool", None, "seq", "mp", None),
        P("pool", None, "seq", "mp", None),
    )
    return jax.shard_map(
        on_device,
        mesh=mesh,
        in_specs=placed,
        out_specs=(
            P("pool", "seq", "mp", None),
            P("pool", "seq", None, "mp", None),
            P("pool", "seq", None, "mp", None),
            P("pool", None, "seq", "mp", None),
        ),
        check_vma=False,
    )
```

```python
import functools

import jax
import jax.numpy as jnp
from jax import lax
from jax.experimental import pallas as pl
from jax.experimental.pallas import tpu as pltpu
from jax.sharding import PartitionSpec as P

PAGE = 128
PAGES_DEV = 6
NPROMPT = 8
NPAGES = 48
SEQ = 8
ROWS = 512
HEADS = 16
HD = 128
SPAN = SEQ * ROWS
BLOCKS = ROWS // PAGE
PAD_BLOCKS = 4
KB = 512
TILE_POS = 128
TILE = TILE_POS * HEADS
TILES = ROWS // TILE_POS
CHUNK = 512
SLOW_CHUNK = 256
DEC_BLOCK = 4
PLACES = ((0, False), (0, True), (-1, False), (-1, True), (1, False), (1, True), (2, False), (2, True))
PIECES = PLACES
NEG = -1e30
SCALE = HD ** -0.5
SCALE2 = SCALE * 1.4426950408889634
LOW = 2.0 ** -80
HIGH = 2.0 ** 100
VMEM = 56 * 1024 * 1024

dot_nt = functools.partial(
    lax.dot_general, dimension_numbers=(((1,), (1,)), ((), ())), preferred_element_type=jnp.float32
)
dot_nn = functools.partial(jnp.dot, preferred_element_type=jnp.float32)


def decode_kernel(len_ref, q_ref, ck_ref, cv_ref, nk_ref, nv_ref, o_ref):
    steps, block = q_ref.shape[0], q_ref.shape[1]
    cache = ck_ref.shape[1]
    slots = nk_ref.shape[0] // steps
    rows = steps * HEADS
    first = pl.program_id(0) * block
    new_keys = nk_ref[...]
    new_values = nv_ref[...]
    lane = lax.broadcasted_iota(jnp.int32, (rows, cache), 1)
    new_lane = lax.broadcasted_iota(jnp.int32, (rows, steps * slots), 1)
    step = lax.broadcasted_iota(jnp.int32, (rows, steps * slots), 0) // HEADS
    each = range(block)
    queries = [q_ref[:, i].reshape(rows, HD) for i in each]
    old = [dot_nt(queries[i], ck_ref[i]) * SCALE for i in each]
    new = [dot_nt(queries[i], new_keys) * SCALE for i in each]
    old_w, new_w, total = [], [], []
    for i in each:
        old_i = jnp.where(lane < len_ref[0, first + i], old[i], NEG)
        new_ok = (new_lane % slots == first + i) & (new_lane // slots <= step)
        new_i = jnp.where(new_ok, new[i], NEG)
        top = jnp.maximum(
            jnp.max(old_i, axis=1, keepdims=True), jnp.max(new_i, axis=1, keepdims=True)
        )
        old_e = jnp.exp(old_i - top)
        new_e = jnp.exp(new_i - top)
        total.append(jnp.sum(old_e, axis=1, keepdims=True) + jnp.sum(new_e, axis=1, keepdims=True))
        old_w.append(old_e.astype(jnp.bfloat16))
        new_w.append(new_e.astype(jnp.bfloat16))
    for i in each:
        mixed = dot_nn(old_w[i], cv_ref[i]) + dot_nn(new_w[i], new_values)
        o_ref[:, i] = (mixed / total[i]).astype(jnp.bfloat16).reshape(steps, HEADS, HD)


def decode_call(lengths, q, ck, cv, nk, nv):
    steps, slots = q.shape[0], q.shape[1]
    cache = ck.shape[1]
    return pl.pallas_call(
        decode_kernel,
        name="decode",
        grid=(slots // DEC_BLOCK,),
        in_specs=[
            pl.BlockSpec(memory_space=pltpu.SMEM),
            pl.BlockSpec((steps, DEC_BLOCK, HEADS, HD), lambda i: (0, i, 0, 0)),
            pl.BlockSpec((DEC_BLOCK, cache, HD), lambda i: (i, 0, 0)),
            pl.BlockSpec((DEC_BLOCK, cache, HD), lambda i: (i, 0, 0)),
            pl.BlockSpec((steps * slots, HD), lambda i: (0, 0)),
            pl.BlockSpec((steps * slots, HD), lambda i: (0, 0)),
        ],
        out_specs=pl.BlockSpec((steps, DEC_BLOCK, HEADS, HD), lambda i: (0, i, 0, 0)),
        out_shape=jax.ShapeDtypeStruct(q.shape, jnp.bfloat16),
        compiler_params=pltpu.CompilerParams(vmem_limit_bytes=VMEM),
        cost_estimate=pl.CostEstimate(
            flops=4 * 64 * 1088 * 128 * 16, bytes_accessed=9 << 20, transcendentals=64 * 1088 * 16
        ),
    )(lengths, q, ck, cv, nk, nv)


def prepare_kernel(k_ref, v_ref, o_ref):
    o_ref[:BLOCKS] = k_ref[...].reshape(BLOCKS, PAGE, HD)
    for i in range(BLOCKS):
        values = v_ref[i * PAGE : (i + 1) * PAGE, :].astype(jnp.float32)
        o_ref[BLOCKS + i] = values.T.astype(jnp.bfloat16)


def prepare_call(keys, values):
    return pl.pallas_call(
        prepare_kernel,
        name="prepare",
        out_shape=jax.ShapeDtypeStruct((2 * BLOCKS, PAGE, HD), jnp.bfloat16),
        cost_estimate=pl.CostEstimate(flops=0, bytes_accessed=1 << 19, transcendentals=0),
    )(keys, values)


def piece_seq(me, chips, swapped):
    core = me ^ 1 if swapped else me
    return (core + 2 * chips + SEQ) % SEQ


def piece_copies(places, pieces, k_buf, v_buf, sem):
    me = lax.axis_index("seq")
    copies = []
    for i, ((chips, swapped), piece) in enumerate(zip(places, pieces)):
        at = pl.ds(piece_seq(me, chips, swapped) * BLOCKS + PAD_BLOCKS, BLOCKS)
        copies.append(pltpu.make_async_copy(piece.at[pl.ds(0, BLOCKS)], k_buf.at[at], sem.at[2 * i]))
        copies.append(
            pltpu.make_async_copy(piece.at[pl.ds(BLOCKS, BLOCKS)], v_buf.at[at], sem.at[2 * i + 1])
        )
    return copies


def gather_kernel(len_ref, map_ref, *refs):
    pieces = refs[: len(PIECES)]
    pk_ref, pv_ref, k_buf, v_buf, slot_of, sem = refs[len(PIECES) :]
    me = lax.axis_index("seq")
    own = lax.axis_index("pool")
    copies = piece_copies(PIECES, pieces, k_buf, v_buf, sem)
    for copy in copies:
        copy.start()

    def place(b, _):
        page = map_ref[own, b]

        @pl.when(page // PAGES_DEV == me)
        def _():
            slot_of[page % PAGES_DEV] = b

        return 0

    lax.fori_loop(0, NPAGES, place, 0)
    window = 2 * PAGE
    row = lax.broadcasted_iota(jnp.int32, (PAGE, window), 0)
    col = lax.broadcasted_iota(jnp.int32, (PAGE, window), 1)
    picks, lows = [], []
    for i in range(PAGES_DEV):
        b = slot_of[i]
        first = jnp.int32(0)
        start = jnp.int32(0)
        source = jnp.int32(0)
        count = jnp.int32(0)
        for prompt in range(NPROMPT):
            length = len_ref[own, prompt]
            blocks = (length + PAGE - 1) // PAGE
            inside = (b >= first) & (b < first + blocks)
            offset = (b - first) * PAGE
            source = jnp.where(inside, start + offset, source)
            count = jnp.where(inside, jnp.minimum(length - offset, PAGE), count)
            first = first + blocks
            start = start + length
        low = jnp.minimum(source // PAGE, SPAN // PAGE - 2)
        hit = ((low * PAGE + col) == (source + row)) & (row < count)
        picks.append(jnp.where(hit, 1.0, 0.0).astype(jnp.bfloat16))
        lows.append(low + PAD_BLOCKS)
    for copy in copies:
        copy.wait()
    for i in range(PAGES_DEV):
        here = slice(i * PAGE, (i + 1) * PAGE)
        at = pl.ds(lows[i], 2)
        keys = k_buf[at].reshape(window, HD)
        values = jnp.concatenate([v_buf[lows[i]], v_buf[lows[i] + 1]], axis=1)
        pk_ref[here, :] = dot_nn(picks[i], keys).astype(jnp.bfloat16)
        pv_ref[here, :] = dot_nt(picks[i], values).astype(jnp.bfloat16)


def gather_call(prompt_len, page_map, pieces):
    rows = PAGES_DEV * PAGE
    return pl.pallas_call(
        gather_kernel,
        name="cut_pages",
        in_specs=[pl.BlockSpec(memory_space=pltpu.SMEM)] * 2
        + [pl.BlockSpec(memory_space=pl.ANY)] * len(PIECES),
        out_specs=[pl.BlockSpec(memory_space=pltpu.VMEM)] * 2,
        out_shape=[jax.ShapeDtypeStruct((rows, HD), jnp.bfloat16)] * 2,
        scratch_shapes=[
            pltpu.VMEM((PAD_BLOCKS + SEQ * BLOCKS, PAGE, HD), jnp.bfloat16),
            pltpu.VMEM((PAD_BLOCKS + SEQ * BLOCKS, PAGE, HD), jnp.bfloat16),
            pltpu.SMEM((PAGES_DEV,), jnp.int32),
            pltpu.SemaphoreType.DMA((2 * len(PIECES),)),
        ],
        compiler_params=pltpu.CompilerParams(vmem_limit_bytes=VMEM),
        cost_estimate=pl.CostEstimate(
            flops=12 * 2 * 128 * 256 * 128, bytes_accessed=5 << 20, transcendentals=0
        ),
    )(prompt_len, page_map, *pieces)


def prefill_kernel(stage, places, len_ref, q_hbm, *refs):
    pieces, refs = refs[: len(places)], refs[len(places) :]
    near = stage == "near"
    if near:
        acc_hbm, sum_hbm = refs[:2]
        refs = refs[2:]
    else:
        acc_hbm, sum_hbm, o_hbm, o_ref, o_sem = refs[:5]
        refs = refs[5:]
    q_ref, k_buf, v_buf, acc, total, weights, q_sem, acc_sem, sum_sem, kv_sem = refs
    me = lax.axis_index("seq")
    own = lax.axis_index("pool")
    chunks = TILE // CHUNK

    def tile_at(t):
        return pl.ds(pl.multiple_of(t * TILE, TILE), TILE)

    def q_copy(t):
        return pltpu.make_async_copy(q_hbm.at[tile_at(t)], q_ref.at[tile_at(t)], q_sem.at[t])

    def o_copy(t):
        return pltpu.make_async_copy(o_ref.at[tile_at(t)], o_hbm.at[tile_at(t)], o_sem.at[t])

    def carry_copies(t):
        pairs = ((acc_hbm, acc, acc_sem), (sum_hbm, total, sum_sem))
        if near:
            return [pltpu.make_async_copy(v.at[t], h.at[t], s.at[t]) for h, v, s in pairs]
        return [pltpu.make_async_copy(h.at[t], v.at[t], s.at[t]) for h, v, s in pairs]

    kv_copies = piece_copies(places, pieces, k_buf, v_buf, kv_sem)
    q_copy(0).start()
    for copy in kv_copies:
        copy.start()
    for t in range(1, TILES):
        q_copy(t).start()
    if near:
        acc[...] = jnp.zeros_like(acc)
        total[...] = jnp.zeros_like(total)
    else:
        for t in range(TILES):
            for copy in carry_copies(t):
                copy.start()
    k_buf[:PAD_BLOCKS] = jnp.zeros((PAD_BLOCKS, PAGE, HD), jnp.bfloat16)
    v_buf[:PAD_BLOCKS] = jnp.zeros((PAD_BLOCKS, PAGE, HD), jnp.bfloat16)
    if near:
        other = (me // 2 * 2 + SEQ - 2) % SEQ * BLOCKS + PAD_BLOCKS
        k_buf[pl.ds(other, 2 * BLOCKS)] = jnp.zeros((2 * BLOCKS, PAGE, HD), jnp.bfloat16)
        v_buf[pl.ds(other, 2 * BLOCKS)] = jnp.zeros((2 * BLOCKS, PAGE, HD), jnp.bfloat16)

    def segment_start(position):
        start = jnp.int32(0)
        end = jnp.int32(0)
        for prompt in range(NPROMPT):
            end = end + len_ref[own, prompt]
            start = jnp.where(end <= position, end, start)
        return start

    chip_start = me // 2 * (2 * ROWS)

    def first_position(t):
        return me * ROWS + t * TILE_POS

    def tile_end(t):
        return first_position(t) + TILE_POS

    def tile_low(t):
        return segment_start(first_position(t))

    def block_count(t):
        if near:
            low = jnp.maximum(tile_low(t), chip_start)
            return (tile_end(t) - low + KB - 1) // KB
        return jnp.maximum((chip_start - tile_low(t) + KB - 1) // KB, 1)

    def block_start(t, j):
        return (tile_end(t) if near else chip_start) - (j + 1) * KB

    def keys_at(start):
        at = pl.ds(start // PAGE + PAD_BLOCKS, KB // PAGE)
        return k_buf[at].reshape(KB, HD)

    def values_at(start):
        block = start // PAGE + PAD_BLOCKS
        return jnp.concatenate([v_buf[block + i] for i in range(KB // PAGE)], axis=1)

    def scores(start, t, c, width):
        at = pl.ds(pl.multiple_of(t * TILE + c * width, width), width)
        return dot_nt(keys_at(start), q_ref[at, :]) * SCALE2

    def allowed(start, t, c, width):
        lane = lax.broadcasted_iota(jnp.int32, (1, width), 1)
        high = first_position(t) + c * (width // HEADS) + lane // HEADS
        low = segment_start(high)
        if near:
            low = jnp.maximum(low, chip_start)
        k_pos = start + lax.broadcasted_iota(jnp.int32, (KB, width), 0)
        return (k_pos >= low) & (k_pos <= high)

    def put(t, j, c, slot, masked):
        at = slice(c * CHUNK, (c + 1) * CHUNK)
        start = block_start(t, j)
        terms = jnp.exp2(scores(start, t, c, CHUNK))
        if masked:
            terms = jnp.where(allowed(start, t, c, CHUNK), terms, 0.0)
        weights[slot, :, at] = terms.astype(jnp.bfloat16)
        total[t, :, at] += jnp.sum(terms.reshape(KB // 8, 8, CHUNK), axis=0)

    def mix(t, j, c, slot):
        at = slice(c * CHUNK, (c + 1) * CHUNK)
        acc[t, :, at] += dot_nn(values_at(block_start(t, j)), weights[slot, :, at])

    def slow_tile(t):
        width = SLOW_CHUNK

        def one(c, _):
            def block(j, carried):
                top, below, mixed = carried
                start = tile_end(t) - (j + 1) * KB
                ok = allowed(start, t, c, width)
                here = jnp.where(ok, scores(start, t, c, width), NEG)
                new_top = jnp.maximum(top, jnp.max(here, axis=0, keepdims=True))
                terms = jnp.where(ok, jnp.exp2(here - new_top), 0.0)
                scale = jnp.exp2(top - new_top)
                below = below * scale + jnp.sum(terms, axis=0, keepdims=True)
                mixed = mixed * scale + dot_nn(values_at(start), terms.astype(jnp.bfloat16))
                return new_top, below, mixed

            _, below, mixed = lax.fori_loop(
                0,
                (tile_end(t) - tile_low(t) + KB - 1) // KB,
                block,
                (
                    jnp.full((1, width), NEG, jnp.float32),
                    jnp.zeros((1, width), jnp.float32),
                    jnp.zeros((HD, width), jnp.float32),
                ),
            )
            at = pl.ds(pl.multiple_of(t * TILE + c * width, width), width)
            o_ref[at, :] = (mixed / below).T.astype(jnp.bfloat16)
            return 0

        lax.fori_loop(0, TILE // width, one, 0)

    def finish(t):
        if near:
            for copy in carry_copies(t):
                copy.start()
            return
        below = jnp.sum(total[t], axis=0, keepdims=True)
        o_ref[tile_at(t), :] = (acc[t] / below).T.astype(jnp.bfloat16)
        bad = jnp.max(jnp.where((below >= LOW) & (below <= HIGH), 0.0, 1.0))

        @pl.when(bad > 0.0)
        def _():
            slow_tile(t)

        o_copy(t).start()

    def begin(t):
        q_copy(t).wait()
        if not near:
            for copy in carry_copies(t):
                copy.wait()

    def step(t, j, count, slot, last):
        wrap = j + 1 == count
        t2 = jnp.where(wrap, t + 1, t)
        j2 = jnp.where(wrap, 0, j + 1)
        t2 = jnp.minimum(t2, TILES - 1)
        masked = segment_start(tile_end(t2) - 1) > block_start(t2, j2)
        if near:
            masked = masked | (j2 == 0) | (chip_start > block_start(t2, j2))

        @pl.when(wrap & jnp.logical_not(last))
        def _():
            begin(t2)

        def both(is_masked):
            for c in range(chunks):
                put(t2, j2, c, 1 - slot, is_masked)
                mix(t, j, c, slot)

        @pl.when(masked & jnp.logical_not(last))
        def _():
            both(True)

        @pl.when(jnp.logical_not(masked | last))
        def _():
            both(False)

        @pl.when(last)
        def _():
            for c in range(chunks):
                mix(t, j, c, slot)

        @pl.when(wrap)
        def _():
            finish(t)

        return t2, j2, jnp.where(wrap, block_count(t2), count)

    items = jnp.int32(0)
    for t in range(TILES):
        items = items + block_count(t)
    begin(0)
    for copy in kv_copies:
        copy.wait()
    for c in range(chunks):
        put(0, 0, c, 0, True)

    def pair(i, state):
        state = step(*state, 0, 2 * i + 1 == items)

        def second(state):
            return step(*state, 1, 2 * i + 2 == items)

        return lax.cond(2 * i + 1 < items, second, lambda s: s, state)

    lax.fori_loop(0, (items + 1) // 2, pair, (jnp.int32(0), jnp.int32(0), block_count(0)))
    for t in range(TILES):
        if near:
            for copy in carry_copies(t):
                copy.wait()
        else:
            o_copy(t).wait()


CARRY = (
    jax.ShapeDtypeStruct((TILES, HD, TILE), jnp.float32),
    jax.ShapeDtypeStruct((TILES, 8, TILE), jnp.float32),
)


def prefill_call(stage, places, prompt_len, q, pieces, carry=()):
    near = stage == "near"
    outs = CARRY if near else (jax.ShapeDtypeStruct(q.shape, jnp.bfloat16),)
    out_scratch = (
        []
        if near
        else [pltpu.VMEM((TILES * TILE, HD), jnp.bfloat16), pltpu.SemaphoreType.DMA((TILES,))]
    )
    buf = pltpu.VMEM((PAD_BLOCKS + SEQ * BLOCKS, PAGE, HD), jnp.bfloat16)
    keys = 640 if near else 1664
    return pl.pallas_call(
        functools.partial(prefill_kernel, stage, places),
        name="prefill_" + stage,
        in_specs=[pl.BlockSpec(memory_space=pltpu.SMEM)]
        + [pl.BlockSpec(memory_space=pl.ANY)] * (1 + len(pieces) + len(carry)),
        out_specs=[pl.BlockSpec(memory_space=pl.ANY)] * len(outs),
        out_shape=outs,
        scratch_shapes=out_scratch
        + [
            pltpu.VMEM((TILES * TILE, HD), jnp.bfloat16),
            buf,
            buf,
            pltpu.VMEM(CARRY[0].shape, jnp.float32),
            pltpu.VMEM(CARRY[1].shape, jnp.float32),
            pltpu.VMEM((2, KB, TILE), jnp.bfloat16),
            pltpu.SemaphoreType.DMA((TILES,)),
            pltpu.SemaphoreType.DMA((TILES,)),
            pltpu.SemaphoreType.DMA((TILES,)),
            pltpu.SemaphoreType.DMA((2 * len(pieces),)),
        ],
        compiler_params=pltpu.CompilerParams(vmem_limit_bytes=VMEM),
        cost_estimate=pl.CostEstimate(
            flops=4 * 8192 * keys * 128, bytes_accessed=8 << 20, transcendentals=8192 * keys
        ),
    )(prompt_len, q, *pieces, *carry)


def on_device(
    prefill_q,
    prefill_k,
    prefill_v,
    prompt_len,
    page_map,
    cache_k,
    cache_v,
    cache_len,
    decode_q,
    decode_k,
    decode_v,
):
    def chip_shift(x, chips):
        return lax.ppermute(x, "seq", [(j, (j + 2 * chips) % SEQ) for j in range(SEQ)])

    def core_swap(x):
        return lax.ppermute(x, "seq", [(j, j ^ 1) for j in range(SEQ)])

    q = prefill_q[0].reshape(ROWS * HEADS, HD)
    steps, slots = decode_q.shape[1], decode_q.shape[2]
    own = prepare_call(prefill_k[0, :, 0], prefill_v[0, :, 0])
    right = chip_shift(own, 1)
    left = chip_shift(own, -1)
    far = chip_shift(own, 2)
    pair = core_swap(own)
    decode_out = decode_call(
        cache_len,
        decode_q[0],
        cache_k[0, :, :, 0],
        cache_v[0, :, :, 0],
        decode_k[0, :, :, 0].reshape(steps * slots, HD),
        decode_v[0, :, :, 0].reshape(steps * slots, HD),
    )
    right, left, decode_out = lax.optimization_barrier((right, left, decode_out))
    right_swap, left_swap = core_swap(right), core_swap(left)
    carry = prefill_call("near", PLACES[:2], prompt_len, q, (own, pair))
    far, *carry = lax.optimization_barrier((far, *carry))
    pieces = (own, pair, right, right_swap, left, left_swap, far, core_swap(far))
    pk, pv = gather_call(prompt_len, page_map, pieces)
    page_k = lax.ppermute(pk, "pool", [(0, 1), (1, 0)])
    page_v = lax.ppermute(pv, "pool", [(0, 1), (1, 0)])
    (prefill_out,) = prefill_call("rest", PLACES, prompt_len, q, pieces, tuple(carry))
    return (
        prefill_out.reshape(prefill_q.shape),
        page_k.reshape(1, PAGES_DEV, PAGE, 1, HD),
        page_v.reshape(1, PAGES_DEV, PAGE, 1, HD),
        decode_out[None],
    )


def solution(mesh):
    placed = (
        P("pool", "seq", "mp", None),
        P("pool", "seq", "mp", None),
        P("pool", "seq", "mp", None),
        P(),
        P(),
        P("pool", "seq", None, "mp", None),
        P("pool", "seq", None, "mp", None),
        P("pool", "seq"),
        P("pool", None, "seq", "mp", None),
        P("pool", None, "seq", "mp", None),
        P("pool", None, "seq", "mp", None),
    )
    return jax.shard_map(
        on_device,
        mesh=mesh,
        in_specs=placed,
        out_specs=(
            P("pool", "seq", "mp", None),
            P("pool", "seq", None, "mp", None),
            P("pool", "seq", None, "mp", None),
            P("pool", None, "seq", "mp", None),
        ),
        check_vma=False,
    )
```

```python
import functools

import jax
import jax.numpy as jnp
from jax import lax
from jax.experimental import pallas as pl
from jax.experimental.pallas import tpu as pltpu
from jax.sharding import PartitionSpec as P

PAGE = 128
PAGES_DEV = 6
NPROMPT = 8
NPAGES = 48
SEQ = 8
ROWS = 512
HEADS = 16
HD = 128
SPAN = SEQ * ROWS
BLOCKS = ROWS // PAGE
PAD_BLOCKS = 4
KB = 512
TILE_POS = 128
TILE = TILE_POS * HEADS
TILES = ROWS // TILE_POS
CHUNK = 256
SLOW_CHUNK = 256
DEC_BLOCK = 4
PLACES = ((0, False), (0, True), (-1, False), (-1, True), (1, False), (1, True), (2, False), (2, True))
PIECES = PLACES
NEG = -1e30
SCALE = HD ** -0.5
SCALE2 = SCALE * 1.4426950408889634
LOW = 2.0 ** -80
HIGH = 2.0 ** 100
VMEM = 56 * 1024 * 1024

dot_nt = functools.partial(
    lax.dot_general, dimension_numbers=(((1,), (1,)), ((), ())), preferred_element_type=jnp.float32
)
dot_nn = functools.partial(jnp.dot, preferred_element_type=jnp.float32)


def decode_kernel(len_ref, q_ref, ck_ref, cv_ref, nk_ref, nv_ref, o_ref):
    steps, block = q_ref.shape[0], q_ref.shape[1]
    cache = ck_ref.shape[1]
    slots = nk_ref.shape[0] // steps
    rows = steps * HEADS
    first = pl.program_id(0) * block
    new_keys = nk_ref[...]
    new_values = nv_ref[...]
    lane = lax.broadcasted_iota(jnp.int32, (rows, cache), 1)
    new_lane = lax.broadcasted_iota(jnp.int32, (rows, steps * slots), 1)
    step = lax.broadcasted_iota(jnp.int32, (rows, steps * slots), 0) // HEADS
    each = range(block)
    queries = [q_ref[:, i].reshape(rows, HD) for i in each]
    old = [dot_nt(queries[i], ck_ref[i]) * SCALE for i in each]
    new = [dot_nt(queries[i], new_keys) * SCALE for i in each]
    old_w, new_w, total = [], [], []
    for i in each:
        old_i = jnp.where(lane < len_ref[0, first + i], old[i], NEG)
        new_ok = (new_lane % slots == first + i) & (new_lane // slots <= step)
        new_i = jnp.where(new_ok, new[i], NEG)
        top = jnp.maximum(
            jnp.max(old_i, axis=1, keepdims=True), jnp.max(new_i, axis=1, keepdims=True)
        )
        old_e = jnp.exp(old_i - top)
        new_e = jnp.exp(new_i - top)
        total.append(jnp.sum(old_e, axis=1, keepdims=True) + jnp.sum(new_e, axis=1, keepdims=True))
        old_w.append(old_e.astype(jnp.bfloat16))
        new_w.append(new_e.astype(jnp.bfloat16))
    for i in each:
        mixed = dot_nn(old_w[i], cv_ref[i]) + dot_nn(new_w[i], new_values)
        o_ref[:, i] = (mixed / total[i]).astype(jnp.bfloat16).reshape(steps, HEADS, HD)


def decode_call(lengths, q, ck, cv, nk, nv):
    steps, slots = q.shape[0], q.shape[1]
    cache = ck.shape[1]
    return pl.pallas_call(
        decode_kernel,
        name="decode",
        grid=(slots // DEC_BLOCK,),
        in_specs=[
            pl.BlockSpec(memory_space=pltpu.SMEM),
            pl.BlockSpec((steps, DEC_BLOCK, HEADS, HD), lambda i: (0, i, 0, 0)),
            pl.BlockSpec((DEC_BLOCK, cache, HD), lambda i: (i, 0, 0)),
            pl.BlockSpec((DEC_BLOCK, cache, HD), lambda i: (i, 0, 0)),
            pl.BlockSpec((steps * slots, HD), lambda i: (0, 0)),
            pl.BlockSpec((steps * slots, HD), lambda i: (0, 0)),
        ],
        out_specs=pl.BlockSpec((steps, DEC_BLOCK, HEADS, HD), lambda i: (0, i, 0, 0)),
        out_shape=jax.ShapeDtypeStruct(q.shape, jnp.bfloat16),
        compiler_params=pltpu.CompilerParams(vmem_limit_bytes=VMEM),
        cost_estimate=pl.CostEstimate(
            flops=4 * 64 * 1088 * 128 * 16, bytes_accessed=9 << 20, transcendentals=64 * 1088 * 16
        ),
    )(lengths, q, ck, cv, nk, nv)


def prepare_kernel(k_ref, v_ref, o_ref):
    o_ref[:BLOCKS] = k_ref[...].reshape(BLOCKS, PAGE, HD)
    for i in range(BLOCKS):
        values = v_ref[i * PAGE : (i + 1) * PAGE, :].astype(jnp.float32)
        o_ref[BLOCKS + i] = values.T.astype(jnp.bfloat16)


def prepare_call(keys, values):
    return pl.pallas_call(
        prepare_kernel,
        name="prepare",
        out_shape=jax.ShapeDtypeStruct((2 * BLOCKS, PAGE, HD), jnp.bfloat16),
        cost_estimate=pl.CostEstimate(flops=0, bytes_accessed=1 << 19, transcendentals=0),
    )(keys, values)


def piece_seq(me, chips, swapped):
    core = me ^ 1 if swapped else me
    return (core + 2 * chips + SEQ) % SEQ


def piece_copies(places, pieces, k_buf, v_buf, sem):
    me = lax.axis_index("seq")
    copies = []
    for i, ((chips, swapped), piece) in enumerate(zip(places, pieces)):
        at = pl.ds(piece_seq(me, chips, swapped) * BLOCKS + PAD_BLOCKS, BLOCKS)
        copies.append(pltpu.make_async_copy(piece.at[pl.ds(0, BLOCKS)], k_buf.at[at], sem.at[2 * i]))
        copies.append(
            pltpu.make_async_copy(piece.at[pl.ds(BLOCKS, BLOCKS)], v_buf.at[at], sem.at[2 * i + 1])
        )
    return copies


def gather_kernel(len_ref, map_ref, *refs):
    pieces = refs[: len(PIECES)]
    pk_ref, pv_ref, k_buf, v_buf, slot_of, sem = refs[len(PIECES) :]
    me = lax.axis_index("seq")
    own = lax.axis_index("pool")
    copies = piece_copies(PIECES, pieces, k_buf, v_buf, sem)
    for copy in copies:
        copy.start()

    def place(b, _):
        page = map_ref[own, b]

        @pl.when(page // PAGES_DEV == me)
        def _():
            slot_of[page % PAGES_DEV] = b

        return 0

    lax.fori_loop(0, NPAGES, place, 0)
    window = 2 * PAGE
    row = lax.broadcasted_iota(jnp.int32, (PAGE, window), 0)
    col = lax.broadcasted_iota(jnp.int32, (PAGE, window), 1)
    picks, lows = [], []
    for i in range(PAGES_DEV):
        b = slot_of[i]
        first = jnp.int32(0)
        start = jnp.int32(0)
        source = jnp.int32(0)
        count = jnp.int32(0)
        for prompt in range(NPROMPT):
            length = len_ref[own, prompt]
            blocks = (length + PAGE - 1) // PAGE
            inside = (b >= first) & (b < first + blocks)
            offset = (b - first) * PAGE
            source = jnp.where(inside, start + offset, source)
            count = jnp.where(inside, jnp.minimum(length - offset, PAGE), count)
            first = first + blocks
            start = start + length
        low = jnp.minimum(source // PAGE, SPAN // PAGE - 2)
        hit = ((low * PAGE + col) == (source + row)) & (row < count)
        picks.append(jnp.where(hit, 1.0, 0.0).astype(jnp.bfloat16))
        lows.append(low + PAD_BLOCKS)
    for copy in copies:
        copy.wait()
    for i in range(PAGES_DEV):
        here = slice(i * PAGE, (i + 1) * PAGE)
        at = pl.ds(lows[i], 2)
        keys = k_buf[at].reshape(window, HD)
        values = jnp.concatenate([v_buf[lows[i]], v_buf[lows[i] + 1]], axis=1)
        pk_ref[here, :] = dot_nn(picks[i], keys).astype(jnp.bfloat16)
        pv_ref[here, :] = dot_nt(picks[i], values).astype(jnp.bfloat16)


def gather_call(prompt_len, page_map, pieces):
    rows = PAGES_DEV * PAGE
    return pl.pallas_call(
        gather_kernel,
        name="cut_pages",
        in_specs=[pl.BlockSpec(memory_space=pltpu.SMEM)] * 2
        + [pl.BlockSpec(memory_space=pl.ANY)] * len(PIECES),
        out_specs=[pl.BlockSpec(memory_space=pltpu.VMEM)] * 2,
        out_shape=[jax.ShapeDtypeStruct((rows, HD), jnp.bfloat16)] * 2,
        scratch_shapes=[
            pltpu.VMEM((PAD_BLOCKS + SEQ * BLOCKS, PAGE, HD), jnp.bfloat16),
            pltpu.VMEM((PAD_BLOCKS + SEQ * BLOCKS, PAGE, HD), jnp.bfloat16),
            pltpu.SMEM((PAGES_DEV,), jnp.int32),
            pltpu.SemaphoreType.DMA((2 * len(PIECES),)),
        ],
        compiler_params=pltpu.CompilerParams(vmem_limit_bytes=VMEM),
        cost_estimate=pl.CostEstimate(
            flops=12 * 2 * 128 * 256 * 128, bytes_accessed=5 << 20, transcendentals=0
        ),
    )(prompt_len, page_map, *pieces)


def prefill_kernel(len_ref, q_hbm, *refs):
    pieces, refs = refs[: len(PLACES)], refs[len(PLACES) :]
    o_hbm, o_ref, q_ref, k_buf, v_buf, acc, total, weights, q_sem, o_sem, kv_sem = refs
    me = lax.axis_index("seq")
    own = lax.axis_index("pool")
    chunks = TILE // CHUNK

    def tile_at(t):
        return pl.ds(pl.multiple_of(t * TILE, TILE), TILE)

    def q_copy(t):
        return pltpu.make_async_copy(q_hbm.at[tile_at(t)], q_ref.at[tile_at(t)], q_sem.at[t])

    def o_copy(t):
        return pltpu.make_async_copy(o_ref.at[tile_at(t)], o_hbm.at[tile_at(t)], o_sem.at[t])

    kv_copies = piece_copies(PLACES, pieces, k_buf, v_buf, kv_sem)
    q_copy(0).start()
    for copy in kv_copies:
        copy.start()
    for t in range(1, TILES):
        q_copy(t).start()
    acc[...] = jnp.zeros_like(acc)
    total[...] = jnp.zeros_like(total)
    k_buf[:PAD_BLOCKS] = jnp.zeros((PAD_BLOCKS, PAGE, HD), jnp.bfloat16)
    v_buf[:PAD_BLOCKS] = jnp.zeros((PAD_BLOCKS, PAGE, HD), jnp.bfloat16)

    def segment_start(position):
        start = jnp.int32(0)
        end = jnp.int32(0)
        for prompt in range(NPROMPT):
            end = end + len_ref[own, prompt]
            start = jnp.where(end <= position, end, start)
        return start

    def first_position(t):
        return me * ROWS + t * TILE_POS

    def tile_end(t):
        return first_position(t) + TILE_POS

    def tile_low(t):
        return segment_start(first_position(t))

    def block_count(t):
        return (tile_end(t) - tile_low(t) + KB - 1) // KB

    def block_start(t, j):
        return tile_end(t) - (j + 1) * KB

    def keys_at(start):
        at = pl.ds(start // PAGE + PAD_BLOCKS, KB // PAGE)
        return k_buf[at].reshape(KB, HD)

    def values_at(start):
        block = start // PAGE + PAD_BLOCKS
        return jnp.concatenate([v_buf[block + i] for i in range(KB // PAGE)], axis=1)

    def scores(start, t, c, width):
        at = pl.ds(pl.multiple_of(t * TILE + c * width, width), width)
        return dot_nt(keys_at(start), q_ref[at, :]) * SCALE2

    def allowed(start, t, c, width):
        lane = lax.broadcasted_iota(jnp.int32, (1, width), 1)
        high = first_position(t) + c * (width // HEADS) + lane // HEADS
        low = segment_start(high)
        k_pos = start + lax.broadcasted_iota(jnp.int32, (KB, width), 0)
        return (k_pos >= low) & (k_pos <= high)

    def put(t, j, c, slot, mode):
        at = slice(c * CHUNK, (c + 1) * CHUNK)
        start = block_start(t, j)
        terms = jnp.exp2(scores(start, t, c, CHUNK))
        if mode != "none":
            terms = clear(terms, start, t, c, mode)
        weights[slot, :, at] = terms.astype(jnp.bfloat16)
        total[t, :, at] += jnp.sum(terms.reshape(KB // 8, 8, CHUNK), axis=0)

    def mix(t, j, c, slot):
        at = slice(c * CHUNK, (c + 1) * CHUNK)
        acc[t, :, at] += dot_nn(values_at(block_start(t, j)), weights[slot, :, at])

    def clear(terms, start, t, c, mode):
        lane = lax.broadcasted_iota(jnp.int32, (1, CHUNK), 1)
        high = first_position(t) + c * (CHUNK // HEADS) + lane // HEADS
        if mode == "both":
            low = segment_start(high) - start
            terms = jnp.where(lax.broadcasted_iota(jnp.int32, (KB, CHUNK), 0) >= low, terms, 0.0)
        cut = KB - TILE_POS
        k_pos = lax.broadcasted_iota(jnp.int32, (TILE_POS, CHUNK), 0)
        end = jnp.where(k_pos <= high - (start + cut), terms[cut:], 0.0)
        return jnp.concatenate([terms[:cut], end], axis=0)

    def slow_tile(t):
        width = SLOW_CHUNK

        def one(c, _):
            def block(j, carried):
                top, below, mixed = carried
                start = block_start(t, j)
                ok = allowed(start, t, c, width)
                here = jnp.where(ok, scores(start, t, c, width), NEG)
                new_top = jnp.maximum(top, jnp.max(here, axis=0, keepdims=True))
                terms = jnp.where(ok, jnp.exp2(here - new_top), 0.0)
                scale = jnp.exp2(top - new_top)
                below = below * scale + jnp.sum(terms, axis=0, keepdims=True)
                mixed = mixed * scale + dot_nn(values_at(start), terms.astype(jnp.bfloat16))
                return new_top, below, mixed

            _, below, mixed = lax.fori_loop(
                0,
                block_count(t),
                block,
                (
                    jnp.full((1, width), NEG, jnp.float32),
                    jnp.zeros((1, width), jnp.float32),
                    jnp.zeros((HD, width), jnp.float32),
                ),
            )
            at = pl.ds(pl.multiple_of(t * TILE + c * width, width), width)
            o_ref[at, :] = (mixed / below).T.astype(jnp.bfloat16)
            return 0

        lax.fori_loop(0, TILE // width, one, 0)

    def finish(t):
        below = jnp.sum(total[t], axis=0, keepdims=True)
        o_ref[tile_at(t), :] = (acc[t] / below).T.astype(jnp.bfloat16)
        bad = jnp.max(jnp.where((below >= LOW) & (below <= HIGH), 0.0, 1.0))

        @pl.when(bad > 0.0)
        def _():
            slow_tile(t)

        o_copy(t).start()

    def step(t, j, count, slot, last):
        wrap = j + 1 == count
        t2 = jnp.where(wrap, t + 1, t)
        j2 = jnp.where(wrap, 0, j + 1)
        t2 = jnp.minimum(t2, TILES - 1)
        both = segment_start(tile_end(t2) - 1) > block_start(t2, j2)
        edge = (j2 == 0) & jnp.logical_not(both)
        inner = (j2 > 0) & jnp.logical_not(both)

        @pl.when(wrap & jnp.logical_not(last))
        def _():
            q_copy(t2).wait()

        for mode, chosen in (("both", both), ("edge", edge), ("none", inner)):

            @pl.when(chosen & jnp.logical_not(last))
            def _():
                for c in range(chunks):
                    put(t2, j2, c, 1 - slot, mode)
                    mix(t, j, c, slot)

        @pl.when(last)
        def _():
            for c in range(chunks):
                mix(t, j, c, slot)

        @pl.when(wrap)
        def _():
            finish(t)

        return t2, j2, jnp.where(wrap, block_count(t2), count)

    items = jnp.int32(0)
    for t in range(TILES):
        items = items + block_count(t)
    q_copy(0).wait()
    for copy in kv_copies:
        copy.wait()
    for c in range(chunks):
        put(0, 0, c, 0, "both")

    def pair(i, state):
        state = step(*state, 0, 2 * i + 1 == items)

        def second(state):
            return step(*state, 1, 2 * i + 2 == items)

        return lax.cond(2 * i + 1 < items, second, lambda s: s, state)

    lax.fori_loop(0, (items + 1) // 2, pair, (jnp.int32(0), jnp.int32(0), block_count(0)))
    for t in range(TILES):
        o_copy(t).wait()


def prefill_call(prompt_len, q, pieces):
    buf = pltpu.VMEM((PAD_BLOCKS + SEQ * BLOCKS, PAGE, HD), jnp.bfloat16)
    return pl.pallas_call(
        prefill_kernel,
        name="prefill",
        in_specs=[pl.BlockSpec(memory_space=pltpu.SMEM)]
        + [pl.BlockSpec(memory_space=pl.ANY)] * (1 + len(pieces)),
        out_specs=pl.BlockSpec(memory_space=pl.ANY),
        out_shape=jax.ShapeDtypeStruct(q.shape, jnp.bfloat16),
        scratch_shapes=[
            pltpu.VMEM((TILES * TILE, HD), jnp.bfloat16),
            pltpu.VMEM((TILES * TILE, HD), jnp.bfloat16),
            buf,
            buf,
            pltpu.VMEM((TILES, HD, TILE), jnp.float32),
            pltpu.VMEM((TILES, 8, TILE), jnp.float32),
            pltpu.VMEM((2, KB, TILE), jnp.bfloat16),
            pltpu.SemaphoreType.DMA((TILES,)),
            pltpu.SemaphoreType.DMA((TILES,)),
            pltpu.SemaphoreType.DMA((2 * len(pieces),)),
        ],
        compiler_params=pltpu.CompilerParams(vmem_limit_bytes=VMEM),
        cost_estimate=pl.CostEstimate(
            flops=4 * 8192 * 2304 * 128, bytes_accessed=8 << 20, transcendentals=8192 * 2304
        ),
    )(prompt_len, q, *pieces)


def on_device(
    prefill_q,
    prefill_k,
    prefill_v,
    prompt_len,
    page_map,
    cache_k,
    cache_v,
    cache_len,
    decode_q,
    decode_k,
    decode_v,
):
    def chip_shift(x, chips):
        return lax.ppermute(x, "seq", [(j, (j + 2 * chips) % SEQ) for j in range(SEQ)])

    def core_swap(x):
        return lax.ppermute(x, "seq", [(j, j ^ 1) for j in range(SEQ)])

    q = prefill_q[0].reshape(ROWS * HEADS, HD)
    steps, slots = decode_q.shape[1], decode_q.shape[2]
    own = prepare_call(prefill_k[0, :, 0], prefill_v[0, :, 0])
    right = chip_shift(own, 1)
    left = chip_shift(own, -1)
    far = chip_shift(own, 2)
    pair = core_swap(own)
    decode_out = decode_call(
        cache_len,
        decode_q[0],
        cache_k[0, :, :, 0],
        cache_v[0, :, :, 0],
        decode_k[0, :, :, 0].reshape(steps * slots, HD),
        decode_v[0, :, :, 0].reshape(steps * slots, HD),
    )
    right, left, decode_out = lax.optimization_barrier((right, left, decode_out))
    right_swap, left_swap = core_swap(right), core_swap(left)
    pieces = (own, pair, right, right_swap, left, left_swap, far, core_swap(far))
    pk, pv = gather_call(prompt_len, page_map, pieces)
    page_k = lax.ppermute(pk, "pool", [(0, 1), (1, 0)])
    page_v = lax.ppermute(pv, "pool", [(0, 1), (1, 0)])
    prefill_out = prefill_call(prompt_len, q, pieces)
    return (
        prefill_out.reshape(prefill_q.shape),
        page_k.reshape(1, PAGES_DEV, PAGE, 1, HD),
        page_v.reshape(1, PAGES_DEV, PAGE, 1, HD),
        decode_out[None],
    )


def solution(mesh):
    placed = (
        P("pool", "seq", "mp", None),
        P("pool", "seq", "mp", None),
        P("pool", "seq", "mp", None),
        P(),
        P(),
        P("pool", "seq", None, "mp", None),
        P("pool", "seq", None, "mp", None),
        P("pool", "seq"),
        P("pool", None, "seq", "mp", None),
        P("pool", None, "seq", "mp", None),
        P("pool", None, "seq", "mp", None),
    )
    return jax.shard_map(
        on_device,
        mesh=mesh,
        in_specs=placed,
        out_specs=(
            P("pool", "seq", "mp", None),
            P("pool", "seq", None, "mp", None),
            P("pool", "seq", None, "mp", None),
            P("pool", None, "seq", "mp", None),
        ),
        check_vma=False,
    )
```

```python
import functools

import jax
import jax.numpy as jnp
from jax import lax
from jax.experimental import pallas as pl
from jax.experimental.pallas import tpu as pltpu
from jax.sharding import PartitionSpec as P

PAGE = 128
PAGES_DEV = 6
NPROMPT = 8
NPAGES = 48
SEQ = 8
ROWS = 512
HEADS = 16
HD = 128
SPAN = SEQ * ROWS
BLOCKS = ROWS // PAGE
PAD_BLOCKS = 4
KB = 512
TILE_POS = 128
TILE = TILE_POS * HEADS
TILES = ROWS // TILE_POS
CHUNK = 256
SLOW_CHUNK = 256
DEC_BLOCK = 4
PLACES = ((0, False), (0, True), (-1, False), (-1, True), (1, False), (1, True), (2, False), (2, True))
PIECES = PLACES
NEG = -1e30
SCALE = HD ** -0.5
SCALE2 = SCALE * 1.4426950408889634
LOW = 2.0 ** -80
HIGH = 2.0 ** 100
VMEM = 36 * 1024 * 1024
CUT_VMEM = 16 * 1024 * 1024

dot_nt = functools.partial(
    lax.dot_general, dimension_numbers=(((1,), (1,)), ((), ())), preferred_element_type=jnp.float32
)
dot_nn = functools.partial(jnp.dot, preferred_element_type=jnp.float32)


def decode_kernel(len_ref, q_ref, ck_ref, cv_ref, nk_ref, nv_ref, o_ref):
    steps, block = q_ref.shape[0], q_ref.shape[1]
    cache = ck_ref.shape[1]
    slots = nk_ref.shape[0] // steps
    rows = steps * HEADS
    first = pl.program_id(0) * block
    new_keys = nk_ref[...]
    new_values = nv_ref[...]
    lane = lax.broadcasted_iota(jnp.int32, (rows, cache), 1)
    new_lane = lax.broadcasted_iota(jnp.int32, (rows, steps * slots), 1)
    step = lax.broadcasted_iota(jnp.int32, (rows, steps * slots), 0) // HEADS
    each = range(block)
    queries = [q_ref[:, i].reshape(rows, HD) for i in each]
    old = [dot_nt(queries[i], ck_ref[i]) * SCALE for i in each]
    new = [dot_nt(queries[i], new_keys) * SCALE for i in each]
    old_w, new_w, total = [], [], []
    for i in each:
        old_i = jnp.where(lane < len_ref[0, first + i], old[i], NEG)
        new_ok = (new_lane % slots == first + i) & (new_lane // slots <= step)
        new_i = jnp.where(new_ok, new[i], NEG)
        top = jnp.maximum(
            jnp.max(old_i, axis=1, keepdims=True), jnp.max(new_i, axis=1, keepdims=True)
        )
        old_e = jnp.exp(old_i - top)
        new_e = jnp.exp(new_i - top)
        total.append(jnp.sum(old_e, axis=1, keepdims=True) + jnp.sum(new_e, axis=1, keepdims=True))
        old_w.append(old_e.astype(jnp.bfloat16))
        new_w.append(new_e.astype(jnp.bfloat16))
    for i in each:
        mixed = dot_nn(old_w[i], cv_ref[i]) + dot_nn(new_w[i], new_values)
        o_ref[:, i] = (mixed / total[i]).astype(jnp.bfloat16).reshape(steps, HEADS, HD)


def decode_call(lengths, q, ck, cv, nk, nv):
    steps, slots = q.shape[0], q.shape[1]
    cache = ck.shape[1]
    return pl.pallas_call(
        decode_kernel,
        name="decode",
        grid=(slots // DEC_BLOCK,),
        in_specs=[
            pl.BlockSpec(memory_space=pltpu.SMEM),
            pl.BlockSpec((steps, DEC_BLOCK, HEADS, HD), lambda i: (0, i, 0, 0)),
            pl.BlockSpec((DEC_BLOCK, cache, HD), lambda i: (i, 0, 0)),
            pl.BlockSpec((DEC_BLOCK, cache, HD), lambda i: (i, 0, 0)),
            pl.BlockSpec((steps * slots, HD), lambda i: (0, 0)),
            pl.BlockSpec((steps * slots, HD), lambda i: (0, 0)),
        ],
        out_specs=pl.BlockSpec((steps, DEC_BLOCK, HEADS, HD), lambda i: (0, i, 0, 0)),
        out_shape=jax.ShapeDtypeStruct(q.shape, jnp.bfloat16),
        compiler_params=pltpu.CompilerParams(vmem_limit_bytes=VMEM),
        cost_estimate=pl.CostEstimate(
            flops=4 * 64 * 1088 * 128 * 16, bytes_accessed=9 << 20, transcendentals=64 * 1088 * 16
        ),
    )(lengths, q, ck, cv, nk, nv)


def prepare_kernel(k_ref, v_ref, o_ref):
    o_ref[:BLOCKS] = k_ref[...].reshape(BLOCKS, PAGE, HD)
    for i in range(BLOCKS):
        values = v_ref[i * PAGE : (i + 1) * PAGE, :].astype(jnp.float32)
        o_ref[BLOCKS + i] = values.T.astype(jnp.bfloat16)


def prepare_call(keys, values):
    return pl.pallas_call(
        prepare_kernel,
        name="prepare",
        out_shape=jax.ShapeDtypeStruct((2 * BLOCKS, PAGE, HD), jnp.bfloat16),
        cost_estimate=pl.CostEstimate(flops=0, bytes_accessed=1 << 19, transcendentals=0),
    )(keys, values)


def piece_seq(me, chips, swapped):
    core = me ^ 1 if swapped else me
    return (core + 2 * chips + SEQ) % SEQ


def gather_kernel(len_ref, map_ref, *refs):
    pieces = refs[: len(PIECES)]
    k_buf, v_buf, pk_ref, pv_ref, slot_of = refs[len(PIECES) :]
    me = lax.axis_index("seq")
    own = lax.axis_index("pool")
    k_buf[:PAD_BLOCKS] = jnp.zeros((PAD_BLOCKS, PAGE, HD), jnp.bfloat16)
    v_buf[:PAD_BLOCKS] = jnp.zeros((PAD_BLOCKS, PAGE, HD), jnp.bfloat16)
    for (chips, swapped), piece in zip(PIECES, pieces):
        at = pl.ds(piece_seq(me, chips, swapped) * BLOCKS + PAD_BLOCKS, BLOCKS)
        k_buf[at] = piece[:BLOCKS]
        v_buf[at] = piece[BLOCKS:]

    def place(b, _):
        page = map_ref[own, b]

        @pl.when(page // PAGES_DEV == me)
        def _():
            slot_of[page % PAGES_DEV] = b

        return 0

    lax.fori_loop(0, NPAGES, place, 0)
    window = 2 * PAGE
    row = lax.broadcasted_iota(jnp.int32, (PAGE, window), 0)
    col = lax.broadcasted_iota(jnp.int32, (PAGE, window), 1)
    for i in range(PAGES_DEV):
        b = slot_of[i]
        first = jnp.int32(0)
        start = jnp.int32(0)
        source = jnp.int32(0)
        count = jnp.int32(0)
        for prompt in range(NPROMPT):
            length = len_ref[own, prompt]
            blocks = (length + PAGE - 1) // PAGE
            inside = (b >= first) & (b < first + blocks)
            offset = (b - first) * PAGE
            source = jnp.where(inside, start + offset, source)
            count = jnp.where(inside, jnp.minimum(length - offset, PAGE), count)
            first = first + blocks
            start = start + length
        low = jnp.minimum(source // PAGE, SPAN // PAGE - 2)
        hit = ((low * PAGE + col) == (source + row)) & (row < count)
        pick = jnp.where(hit, 1.0, 0.0).astype(jnp.bfloat16)
        here = slice(i * PAGE, (i + 1) * PAGE)
        at = low + PAD_BLOCKS
        keys = k_buf[pl.ds(at, 2)].reshape(window, HD)
        values = jnp.concatenate([v_buf[at], v_buf[at + 1]], axis=1)
        pk_ref[here, :] = dot_nn(pick, keys).astype(jnp.bfloat16)
        pv_ref[here, :] = dot_nt(pick, values).astype(jnp.bfloat16)


def gather_call(prompt_len, page_map, pieces):
    rows = PAGES_DEV * PAGE
    return pl.pallas_call(
        gather_kernel,
        name="cut_pages",
        in_specs=[pl.BlockSpec(memory_space=pltpu.SMEM)] * 2
        + [pl.BlockSpec(memory_space=pltpu.VMEM)] * len(PIECES),
        out_specs=[pl.BlockSpec(memory_space=pltpu.VMEM)] * 4,
        out_shape=[jax.ShapeDtypeStruct((PAD_BLOCKS + SEQ * BLOCKS, PAGE, HD), jnp.bfloat16)] * 2
        + [jax.ShapeDtypeStruct((rows, HD), jnp.bfloat16)] * 2,
        scratch_shapes=[pltpu.SMEM((PAGES_DEV,), jnp.int32)],
        compiler_params=pltpu.CompilerParams(vmem_limit_bytes=CUT_VMEM),
        cost_estimate=pl.CostEstimate(
            flops=12 * 2 * 128 * 256 * 128, bytes_accessed=5 << 20, transcendentals=0
        ),
    )(prompt_len, page_map, *pieces)


def prefill_kernel(len_ref, q_ref, k_buf, v_buf, o_hbm, o_ref, acc, total, weights, o_sem):
    me = lax.axis_index("seq")
    own = lax.axis_index("pool")
    chunks = TILE // CHUNK

    def tile_at(t):
        return pl.ds(pl.multiple_of(t * TILE, TILE), TILE)

    def o_copy(t):
        return pltpu.make_async_copy(o_ref.at[tile_at(t)], o_hbm.at[tile_at(t)], o_sem.at[t])

    acc[...] = jnp.zeros_like(acc)
    total[...] = jnp.zeros_like(total)

    def segment_start(position):
        start = jnp.int32(0)
        end = jnp.int32(0)
        for prompt in range(NPROMPT):
            end = end + len_ref[own, prompt]
            start = jnp.where(end <= position, end, start)
        return start

    def first_position(t):
        return me * ROWS + t * TILE_POS

    def tile_end(t):
        return first_position(t) + TILE_POS

    def tile_low(t):
        return segment_start(first_position(t))

    def block_count(t):
        return (tile_end(t) - tile_low(t) + KB - 1) // KB

    def block_start(t, j):
        return tile_end(t) - (j + 1) * KB

    def keys_at(start):
        at = pl.ds(start // PAGE + PAD_BLOCKS, KB // PAGE)
        return k_buf[at].reshape(KB, HD)

    def values_at(start):
        block = start // PAGE + PAD_BLOCKS
        return jnp.concatenate([v_buf[block + i] for i in range(KB // PAGE)], axis=1)

    def scores(start, t, c, width):
        at = pl.ds(pl.multiple_of(t * TILE + c * width, width), width)
        return dot_nt(keys_at(start), q_ref[at, :]) * SCALE2

    def allowed(start, t, c, width):
        lane = lax.broadcasted_iota(jnp.int32, (1, width), 1)
        high = first_position(t) + c * (width // HEADS) + lane // HEADS
        low = segment_start(high)
        k_pos = start + lax.broadcasted_iota(jnp.int32, (KB, width), 0)
        return (k_pos >= low) & (k_pos <= high)

    def put(t, j, c, slot, mode):
        at = slice(c * CHUNK, (c + 1) * CHUNK)
        start = block_start(t, j)
        if mode == "half":
            half = KB // 2
            blocks = half // PAGE
            keys = k_buf[pl.ds((start + half) // PAGE + PAD_BLOCKS, blocks)].reshape(half, HD)
            q_at = pl.ds(pl.multiple_of(t * TILE + c * CHUNK, CHUNK), CHUNK)
            terms = jnp.exp2(dot_nt(keys, q_ref[q_at, :]) * SCALE2)
            low = row_limits(t, c)[0] - (start + half)
            k_pos = lax.broadcasted_iota(jnp.int32, (half, CHUNK), 0)
            terms = jnp.where(k_pos >= low, terms, 0.0)
            weights[slot, :half, at] = jnp.zeros((half, CHUNK), jnp.bfloat16)
            weights[slot, half:, at] = terms.astype(jnp.bfloat16)
            total[t, :, at] += jnp.sum(terms.reshape(half // 8, 8, CHUNK), axis=0)
            return
        terms = jnp.exp2(scores(start, t, c, CHUNK))
        if mode != "none":
            terms = clear(terms, start, t, c, mode)
        weights[slot, :, at] = terms.astype(jnp.bfloat16)
        total[t, :, at] += jnp.sum(terms.reshape(KB // 8, 8, CHUNK), axis=0)

    def mix(t, j, c, slot):
        at = slice(c * CHUNK, (c + 1) * CHUNK)
        acc[t, :, at] += dot_nn(values_at(block_start(t, j)), weights[slot, :, at])

    def row_limits(t, c):
        lane = lax.broadcasted_iota(jnp.int32, (1, CHUNK), 1)
        high = first_position(t) + c * (CHUNK // HEADS) + lane // HEADS
        return segment_start(high), high

    def clear(terms, start, t, c, mode):
        low, high = row_limits(t, c)
        if mode == "both":
            low = low - start
            terms = jnp.where(lax.broadcasted_iota(jnp.int32, (KB, CHUNK), 0) >= low, terms, 0.0)
        cut = KB - TILE_POS
        k_pos = lax.broadcasted_iota(jnp.int32, (TILE_POS, CHUNK), 0)
        end = jnp.where(k_pos <= high - (start + cut), terms[cut:], 0.0)
        return jnp.concatenate([terms[:cut], end], axis=0)

    def slow_tile(t):
        width = SLOW_CHUNK

        def one(c, _):
            def block(j, carried):
                top, below, mixed = carried
                start = block_start(t, j)
                ok = allowed(start, t, c, width)
                here = jnp.where(ok, scores(start, t, c, width), NEG)
                new_top = jnp.maximum(top, jnp.max(here, axis=0, keepdims=True))
                terms = jnp.where(ok, jnp.exp2(here - new_top), 0.0)
                scale = jnp.exp2(top - new_top)
                below = below * scale + jnp.sum(terms, axis=0, keepdims=True)
                mixed = mixed * scale + dot_nn(values_at(start), terms.astype(jnp.bfloat16))
                return new_top, below, mixed

            _, below, mixed = lax.fori_loop(
                0,
                block_count(t),
                block,
                (
                    jnp.full((1, width), NEG, jnp.float32),
                    jnp.zeros((1, width), jnp.float32),
                    jnp.zeros((HD, width), jnp.float32),
                ),
            )
            at = pl.ds(pl.multiple_of(t * TILE + c * width, width), width)
            o_ref[at, :] = (mixed / below).T.astype(jnp.bfloat16)
            return 0

        lax.fori_loop(0, TILE // width, one, 0)

    def finish(t):
        below = jnp.sum(total[t], axis=0, keepdims=True)
        o_ref[tile_at(t), :] = (acc[t] / below).T.astype(jnp.bfloat16)
        bad = jnp.max(jnp.where((below >= LOW) & (below <= HIGH), 0.0, 1.0))

        @pl.when(bad > 0.0)
        def _():
            slow_tile(t)

        o_copy(t).start()

    def step(t, j, count, slot, last):
        wrap = j + 1 == count
        t2 = jnp.where(wrap, t + 1, t)
        j2 = jnp.where(wrap, 0, j + 1)
        t2 = jnp.minimum(t2, TILES - 1)
        start = block_start(t2, j2)
        bounded = segment_start(tile_end(t2) - 1) > start
        half = (j2 > 0) & (tile_low(t2) >= start + KB // 2)
        both = bounded & jnp.logical_not(half)
        edge = (j2 == 0) & jnp.logical_not(bounded)
        inner = (j2 > 0) & jnp.logical_not(bounded)

        for mode, chosen in (("both", both), ("half", half), ("edge", edge), ("none", inner)):

            @pl.when(chosen & jnp.logical_not(last))
            def _():
                for c in range(chunks):
                    put(t2, j2, c, 1 - slot, mode)
                    mix(t, j, c, slot)

        @pl.when(last)
        def _():
            for c in range(chunks):
                mix(t, j, c, slot)

        @pl.when(wrap)
        def _():
            finish(t)

        return t2, j2, jnp.where(wrap, block_count(t2), count)

    items = jnp.int32(0)
    for t in range(TILES):
        items = items + block_count(t)
    for c in range(chunks):
        put(0, 0, c, 0, "both")

    def pair(i, state):
        state = step(*state, 0, 2 * i + 1 == items)

        def second(state):
            return step(*state, 1, 2 * i + 2 == items)

        return lax.cond(2 * i + 1 < items, second, lambda s: s, state)

    lax.fori_loop(0, (items + 1) // 2, pair, (jnp.int32(0), jnp.int32(0), block_count(0)))
    for t in range(TILES):
        o_copy(t).wait()


def prefill_call(prompt_len, q, keys, values):
    return pl.pallas_call(
        prefill_kernel,
        name="prefill",
        in_specs=[pl.BlockSpec(memory_space=pltpu.SMEM)] + [pl.BlockSpec(memory_space=pltpu.VMEM)] * 3,
        out_specs=pl.BlockSpec(memory_space=pl.ANY),
        out_shape=jax.ShapeDtypeStruct(q.shape, jnp.bfloat16),
        scratch_shapes=[
            pltpu.VMEM((TILES * TILE, HD), jnp.bfloat16),
            pltpu.VMEM((TILES, HD, TILE), jnp.float32),
            pltpu.VMEM((TILES, 8, TILE), jnp.float32),
            pltpu.VMEM((2, KB, TILE), jnp.bfloat16),
            pltpu.SemaphoreType.DMA((TILES,)),
        ],
        compiler_params=pltpu.CompilerParams(vmem_limit_bytes=VMEM),
        cost_estimate=pl.CostEstimate(
            flops=4 * 8192 * 2304 * 128, bytes_accessed=8 << 20, transcendentals=8192 * 2304
        ),
    )(prompt_len, q, keys, values)


def on_device(
    prefill_q,
    prefill_k,
    prefill_v,
    prompt_len,
    page_map,
    cache_k,
    cache_v,
    cache_len,
    decode_q,
    decode_k,
    decode_v,
):
    def chip_shift(x, chips):
        return lax.ppermute(x, "seq", [(j, (j + 2 * chips) % SEQ) for j in range(SEQ)])

    def core_swap(x):
        return lax.ppermute(x, "seq", [(j, j ^ 1) for j in range(SEQ)])

    q = prefill_q[0].reshape(ROWS * HEADS, HD)
    steps, slots = decode_q.shape[1], decode_q.shape[2]
    own = prepare_call(prefill_k[0, :, 0], prefill_v[0, :, 0])
    right = chip_shift(own, 1)
    left = chip_shift(own, -1)
    far = chip_shift(own, 2)
    pair = core_swap(own)
    decode_out = decode_call(
        cache_len,
        decode_q[0],
        cache_k[0, :, :, 0],
        cache_v[0, :, :, 0],
        decode_k[0, :, :, 0].reshape(steps * slots, HD),
        decode_v[0, :, :, 0].reshape(steps * slots, HD),
    )
    right, left, decode_out = lax.optimization_barrier((right, left, decode_out))
    right_swap, left_swap = core_swap(right), core_swap(left)
    pieces = (own, pair, right, right_swap, left, left_swap, far, core_swap(far))
    keys, values, pk, pv = gather_call(prompt_len, page_map, pieces)
    page_k = lax.ppermute(pk, "pool", [(0, 1), (1, 0)])
    page_v = lax.ppermute(pv, "pool", [(0, 1), (1, 0)])
    prefill_out = prefill_call(prompt_len, q, keys, values)
    return (
        prefill_out.reshape(prefill_q.shape),
        page_k.reshape(1, PAGES_DEV, PAGE, 1, HD),
        page_v.reshape(1, PAGES_DEV, PAGE, 1, HD),
        decode_out[None],
    )


def solution(mesh):
    placed = (
        P("pool", "seq", "mp", None),
        P("pool", "seq", "mp", None),
        P("pool", "seq", "mp", None),
        P(),
        P(),
        P("pool", "seq", None, "mp", None),
        P("pool", "seq", None, "mp", None),
        P("pool", "seq"),
        P("pool", None, "seq", "mp", None),
        P("pool", None, "seq", "mp", None),
        P("pool", None, "seq", "mp", None),
    )
    return jax.shard_map(
        on_device,
        mesh=mesh,
        in_specs=placed,
        out_specs=(
            P("pool", "seq", "mp", None),
            P("pool", "seq", None, "mp", None),
            P("pool", "seq", None, "mp", None),
            P("pool", None, "seq", "mp", None),
        ),
        check_vma=False,
    )
```

```python
import functools

import jax
import jax.numpy as jnp
from jax import lax
from jax.experimental import pallas as pl
from jax.experimental.pallas import tpu as pltpu
from jax.sharding import PartitionSpec as P

PAGE = 128
PAGES_DEV = 6
NPROMPT = 8
NPAGES = 48
SEQ = 8
ROWS = 512
HEADS = 16
HD = 128
SPAN = SEQ * ROWS
BLOCKS = ROWS // PAGE
PAD_BLOCKS = 4
KB = 512
TILE_POS = 128
TILE = TILE_POS * HEADS
TILES = ROWS // TILE_POS
CHUNK = 256
SLOW_CHUNK = 256
DEC_BLOCK = 4
DEC_VMEM = 56 * 1024 * 1024
PLACES = ((0, False), (0, True), (-1, False), (-1, True), (1, False), (1, True))
NEG = -1e30
SCALE = HD ** -0.5
SCALE2 = SCALE * 1.4426950408889634
LOW = 2.0 ** -80
HIGH = 2.0 ** 100
VMEM = 36 * 1024 * 1024
CUT_VMEM = 16 * 1024 * 1024

dot_nt = functools.partial(
    lax.dot_general, dimension_numbers=(((1,), (1,)), ((), ())), preferred_element_type=jnp.float32
)
dot_nn = functools.partial(jnp.dot, preferred_element_type=jnp.float32)


def decode_kernel(start, len_ref, q_ref, ck_ref, cv_ref, nk_ref, nv_ref, *refs):
    o_ref = refs[-1]
    steps, block = q_ref.shape[0], q_ref.shape[1]
    cache = ck_ref.shape[1]
    slots = nk_ref.shape[0] // steps
    rows = steps * HEADS
    first = start + pl.program_id(0) * block
    new_keys = nk_ref[...]
    new_values = nv_ref[...]
    lane = lax.broadcasted_iota(jnp.int32, (rows, cache), 1)
    new_lane = lax.broadcasted_iota(jnp.int32, (rows, steps * slots), 1)
    step = lax.broadcasted_iota(jnp.int32, (rows, steps * slots), 0) // HEADS
    each = range(block)
    queries = [q_ref[:, i].reshape(rows, HD) for i in each]
    old = [dot_nt(queries[i], ck_ref[i]) * SCALE for i in each]
    new = [dot_nt(queries[i], new_keys) * SCALE for i in each]
    old_w, new_w, total = [], [], []
    for i in each:
        old_i = jnp.where(lane < len_ref[0, first + i], old[i], NEG)
        new_ok = (new_lane % slots == first + i) & (new_lane // slots <= step)
        new_i = jnp.where(new_ok, new[i], NEG)
        top = jnp.maximum(
            jnp.max(old_i, axis=1, keepdims=True), jnp.max(new_i, axis=1, keepdims=True)
        )
        old_e = jnp.exp(old_i - top)
        new_e = jnp.exp(new_i - top)
        total.append(jnp.sum(old_e, axis=1, keepdims=True) + jnp.sum(new_e, axis=1, keepdims=True))
        old_w.append(old_e.astype(jnp.bfloat16))
        new_w.append(new_e.astype(jnp.bfloat16))
    for i in each:
        mixed = dot_nn(old_w[i], cv_ref[i]) + dot_nn(new_w[i], new_values)
        o_ref[:, i] = (mixed / total[i]).astype(jnp.bfloat16).reshape(steps, HEADS, HD)


def decode_call(start, count, lengths, q, ck, cv, nk, nv, *before):
    steps, slots = q.shape[0], q.shape[1]
    cache = ck.shape[1]
    skip = start // DEC_BLOCK
    return pl.pallas_call(
        functools.partial(decode_kernel, start),
        name="decode",
        grid=(count // DEC_BLOCK,),
        in_specs=[
            pl.BlockSpec(memory_space=pltpu.SMEM),
            pl.BlockSpec((steps, DEC_BLOCK, HEADS, HD), lambda i: (0, i + skip, 0, 0)),
            pl.BlockSpec((DEC_BLOCK, cache, HD), lambda i: (i + skip, 0, 0)),
            pl.BlockSpec((DEC_BLOCK, cache, HD), lambda i: (i + skip, 0, 0)),
            pl.BlockSpec((steps * slots, HD), lambda i: (0, 0)),
            pl.BlockSpec((steps * slots, HD), lambda i: (0, 0)),
        ]
        + [pl.BlockSpec(memory_space=pl.ANY)] * len(before),
        out_specs=pl.BlockSpec((steps, DEC_BLOCK, HEADS, HD), lambda i: (0, i + skip, 0, 0)),
        out_shape=jax.ShapeDtypeStruct(q.shape, jnp.bfloat16),
        input_output_aliases={6: 0} if before else {},
        compiler_params=pltpu.CompilerParams(vmem_limit_bytes=DEC_VMEM),
        cost_estimate=pl.CostEstimate(
            flops=4 * 64 * 1088 * 128 * count,
            bytes_accessed=count << 19,
            transcendentals=64 * 1088 * count,
        ),
    )(lengths, q, ck, cv, nk, nv, *before)


def prepare_kernel(k_ref, v_ref, o_ref):
    o_ref[:BLOCKS] = k_ref[...].reshape(BLOCKS, PAGE, HD)
    for i in range(BLOCKS):
        values = v_ref[i * PAGE : (i + 1) * PAGE, :].astype(jnp.float32)
        o_ref[BLOCKS + i] = values.T.astype(jnp.bfloat16)


def prepare_call(keys, values):
    return pl.pallas_call(
        prepare_kernel,
        name="prepare",
        out_shape=jax.ShapeDtypeStruct((2 * BLOCKS, PAGE, HD), jnp.bfloat16),
        cost_estimate=pl.CostEstimate(flops=0, bytes_accessed=1 << 19, transcendentals=0),
    )(keys, values)


def piece_seq(me, chips, swapped):
    core = me ^ 1 if swapped else me
    return (core + 2 * chips + SEQ) % SEQ


def gather_kernel(len_ref, map_ref, *refs):
    pieces = refs[: len(PLACES)]
    far, refs = refs[len(PLACES) : len(PLACES) + 4], refs[len(PLACES) + 4 :]
    k_buf, v_buf, page_ref, slot_of = refs
    me = lax.axis_index("seq")
    own = lax.axis_index("pool")
    k_buf[:PAD_BLOCKS] = jnp.zeros((PAD_BLOCKS, PAGE, HD), jnp.bfloat16)
    v_buf[:PAD_BLOCKS] = jnp.zeros((PAD_BLOCKS, PAGE, HD), jnp.bfloat16)
    for (chips, swapped), piece in zip(PLACES, pieces):
        at = pl.ds(piece_seq(me, chips, swapped) * BLOCKS + PAD_BLOCKS, BLOCKS)
        k_buf[at] = piece[:BLOCKS]
        v_buf[at] = piece[BLOCKS:]
    for swapped, keys, values in ((False, far[0], far[1]), (True, far[2], far[3])):
        at = pl.ds(piece_seq(me, 2, swapped) * BLOCKS + PAD_BLOCKS, BLOCKS)
        k_buf[at] = keys[...]
        v_buf[at] = values[...]

    def place(b, _):
        page = map_ref[own, b]

        @pl.when(page // PAGES_DEV == me)
        def _():
            slot_of[page % PAGES_DEV] = b

        return 0

    lax.fori_loop(0, NPAGES, place, 0)
    window = 2 * PAGE
    row = lax.broadcasted_iota(jnp.int32, (PAGE, window), 0)
    col = lax.broadcasted_iota(jnp.int32, (PAGE, window), 1)
    for i in range(PAGES_DEV):
        b = slot_of[i]
        first = jnp.int32(0)
        start = jnp.int32(0)
        source = jnp.int32(0)
        count = jnp.int32(0)
        for prompt in range(NPROMPT):
            length = len_ref[own, prompt]
            blocks = (length + PAGE - 1) // PAGE
            inside = (b >= first) & (b < first + blocks)
            offset = (b - first) * PAGE
            source = jnp.where(inside, start + offset, source)
            count = jnp.where(inside, jnp.minimum(length - offset, PAGE), count)
            first = first + blocks
            start = start + length
        low = jnp.minimum(source // PAGE, SPAN // PAGE - 2)
        hit = ((low * PAGE + col) == (source + row)) & (row < count)
        pick = jnp.where(hit, 1.0, 0.0).astype(jnp.bfloat16)
        here = slice(i * PAGE, (i + 1) * PAGE)
        at = low + PAD_BLOCKS
        keys = k_buf[pl.ds(at, 2)].reshape(window, HD)
        values = jnp.concatenate([v_buf[at], v_buf[at + 1]], axis=1)
        page_ref[0, here, :] = dot_nn(pick, keys).astype(jnp.bfloat16)
        page_ref[1, here, :] = dot_nt(pick, values).astype(jnp.bfloat16)


def gather_call(prompt_len, page_map, pieces):
    rows = PAGES_DEV * PAGE
    return pl.pallas_call(
        gather_kernel,
        name="cut_pages",
        in_specs=[pl.BlockSpec(memory_space=pltpu.SMEM)] * 2
        + [pl.BlockSpec(memory_space=pltpu.VMEM)] * len(pieces),
        out_specs=[pl.BlockSpec(memory_space=pltpu.VMEM)] * 3,
        out_shape=[jax.ShapeDtypeStruct((PAD_BLOCKS + SEQ * BLOCKS, PAGE, HD), jnp.bfloat16)] * 2
        + [jax.ShapeDtypeStruct((2, rows, HD), jnp.bfloat16)],
        scratch_shapes=[pltpu.SMEM((PAGES_DEV,), jnp.int32)],
        compiler_params=pltpu.CompilerParams(vmem_limit_bytes=CUT_VMEM),
        cost_estimate=pl.CostEstimate(
            flops=12 * 2 * 128 * 256 * 128, bytes_accessed=5 << 20, transcendentals=0
        ),
    )(prompt_len, page_map, *pieces)


def emit_kernel(page_ref, k_hbm, v_hbm, sem):
    copies = [
        pltpu.make_async_copy(page_ref.at[i], out, sem.at[i]) for i, out in enumerate((k_hbm, v_hbm))
    ]
    for copy in copies:
        copy.start()
    for copy in copies:
        copy.wait()


def emit_call(pages):
    return pl.pallas_call(
        emit_kernel,
        name="emit_pages",
        in_specs=[pl.BlockSpec(memory_space=pl.ANY)],
        out_specs=[pl.BlockSpec(memory_space=pl.ANY)] * 2,
        out_shape=[jax.ShapeDtypeStruct(pages.shape[1:], jnp.bfloat16)] * 2,
        scratch_shapes=[pltpu.SemaphoreType.DMA((2,))],
        cost_estimate=pl.CostEstimate(flops=0, bytes_accessed=1 << 20, transcendentals=0),
    )(pages)


def prefill_kernel(len_ref, q_ref, k_buf, v_buf, o_hbm, o_ref, acc, total, weights, o_sem):
    me = lax.axis_index("seq")
    own = lax.axis_index("pool")
    chunks = TILE // CHUNK

    def tile_at(t):
        return pl.ds(pl.multiple_of(t * TILE, TILE), TILE)

    def o_copy(t):
        return pltpu.make_async_copy(o_ref.at[tile_at(t)], o_hbm.at[tile_at(t)], o_sem.at[t])

    acc[...] = jnp.zeros_like(acc)
    total[...] = jnp.zeros_like(total)

    def segment_start(position):
        start = jnp.int32(0)
        end = jnp.int32(0)
        for prompt in range(NPROMPT):
            end = end + len_ref[own, prompt]
            start = jnp.where(end <= position, end, start)
        return start

    def first_position(t):
        return me * ROWS + t * TILE_POS

    def tile_end(t):
        return first_position(t) + TILE_POS

    def tile_low(t):
        return segment_start(first_position(t))

    def block_count(t):
        return (tile_end(t) - tile_low(t) + KB - 1) // KB

    def block_start(t, j):
        return tile_end(t) - (j + 1) * KB

    def keys_at(start):
        at = pl.ds(start // PAGE + PAD_BLOCKS, KB // PAGE)
        return k_buf[at].reshape(KB, HD)

    def values_at(start):
        block = start // PAGE + PAD_BLOCKS
        return jnp.concatenate([v_buf[block + i] for i in range(KB // PAGE)], axis=1)

    def scores(start, t, c, width):
        at = pl.ds(pl.multiple_of(t * TILE + c * width, width), width)
        return dot_nt(keys_at(start), q_ref[at, :]) * SCALE2

    def allowed(start, t, c, width):
        lane = lax.broadcasted_iota(jnp.int32, (1, width), 1)
        high = first_position(t) + c * (width // HEADS) + lane // HEADS
        low = segment_start(high)
        k_pos = start + lax.broadcasted_iota(jnp.int32, (KB, width), 0)
        return (k_pos >= low) & (k_pos <= high)

    def put(t, j, c, slot, mode):
        at = slice(c * CHUNK, (c + 1) * CHUNK)
        start = block_start(t, j)
        if mode == "half":
            half = KB // 2
            blocks = half // PAGE
            keys = k_buf[pl.ds((start + half) // PAGE + PAD_BLOCKS, blocks)].reshape(half, HD)
            q_at = pl.ds(pl.multiple_of(t * TILE + c * CHUNK, CHUNK), CHUNK)
            terms = jnp.exp2(dot_nt(keys, q_ref[q_at, :]) * SCALE2)
            low = row_limits(t, c)[0] - (start + half)
            k_pos = lax.broadcasted_iota(jnp.int32, (half, CHUNK), 0)
            terms = jnp.where(k_pos >= low, terms, 0.0)
            weights[slot, :half, at] = jnp.zeros((half, CHUNK), jnp.bfloat16)
            weights[slot, half:, at] = terms.astype(jnp.bfloat16)
            total[t, :, at] += jnp.sum(terms.reshape(half // 8, 8, CHUNK), axis=0)
            return
        terms = jnp.exp2(scores(start, t, c, CHUNK))
        if mode != "none":
            terms = clear(terms, start, t, c, mode)
        weights[slot, :, at] = terms.astype(jnp.bfloat16)
        total[t, :, at] += jnp.sum(terms.reshape(KB // 8, 8, CHUNK), axis=0)

    def mix(t, j, c, slot):
        at = slice(c * CHUNK, (c + 1) * CHUNK)
        acc[t, :, at] += dot_nn(values_at(block_start(t, j)), weights[slot, :, at])

    def row_limits(t, c):
        lane = lax.broadcasted_iota(jnp.int32, (1, CHUNK), 1)
        high = first_position(t) + c * (CHUNK // HEADS) + lane // HEADS
        return segment_start(high), high

    def clear(terms, start, t, c, mode):
        low, high = row_limits(t, c)
        if mode == "both":
            low = low - start
            terms = jnp.where(lax.broadcasted_iota(jnp.int32, (KB, CHUNK), 0) >= low, terms, 0.0)
        cut = KB - TILE_POS
        k_pos = lax.broadcasted_iota(jnp.int32, (TILE_POS, CHUNK), 0)
        end = jnp.where(k_pos <= high - (start + cut), terms[cut:], 0.0)
        return jnp.concatenate([terms[:cut], end], axis=0)

    def slow_tile(t):
        width = SLOW_CHUNK

        def one(c, _):
            def block(j, carried):
                top, below, mixed = carried
                start = block_start(t, j)
                ok = allowed(start, t, c, width)
                here = jnp.where(ok, scores(start, t, c, width), NEG)
                new_top = jnp.maximum(top, jnp.max(here, axis=0, keepdims=True))
                terms = jnp.where(ok, jnp.exp2(here - new_top), 0.0)
                scale = jnp.exp2(top - new_top)
                below = below * scale + jnp.sum(terms, axis=0, keepdims=True)
                mixed = mixed * scale + dot_nn(values_at(start), terms.astype(jnp.bfloat16))
                return new_top, below, mixed

            _, below, mixed = lax.fori_loop(
                0,
                block_count(t),
                block,
                (
                    jnp.full((1, width), NEG, jnp.float32),
                    jnp.zeros((1, width), jnp.float32),
                    jnp.zeros((HD, width), jnp.float32),
                ),
            )
            at = pl.ds(pl.multiple_of(t * TILE + c * width, width), width)
            o_ref[at, :] = (mixed / below).T.astype(jnp.bfloat16)
            return 0

        lax.fori_loop(0, TILE // width, one, 0)

    def finish(t):
        below = jnp.sum(total[t], axis=0, keepdims=True)
        o_ref[tile_at(t), :] = (acc[t] / below).T.astype(jnp.bfloat16)
        bad = jnp.max(jnp.where((below >= LOW) & (below <= HIGH), 0.0, 1.0))

        @pl.when(bad > 0.0)
        def _():
            slow_tile(t)

        o_copy(t).start()

    def step(t, j, count, slot, last):
        wrap = j + 1 == count
        t2 = jnp.where(wrap, t + 1, t)
        j2 = jnp.where(wrap, 0, j + 1)
        t2 = jnp.minimum(t2, TILES - 1)
        start = block_start(t2, j2)
        bounded = segment_start(tile_end(t2) - 1) > start
        half = (j2 > 0) & (tile_low(t2) >= start + KB // 2)
        both = bounded & jnp.logical_not(half)
        edge = (j2 == 0) & jnp.logical_not(bounded)
        inner = (j2 > 0) & jnp.logical_not(bounded)

        for mode, chosen in (("both", both), ("half", half), ("edge", edge), ("none", inner)):

            @pl.when(chosen & jnp.logical_not(last))
            def _():
                for c in range(chunks):
                    put(t2, j2, c, 1 - slot, mode)
                    mix(t, j, c, slot)

        @pl.when(last)
        def _():
            for c in range(chunks):
                mix(t, j, c, slot)

        @pl.when(wrap)
        def _():
            finish(t)

        return t2, j2, jnp.where(wrap, block_count(t2), count)

    items = jnp.int32(0)
    for t in range(TILES):
        items = items + block_count(t)
    for c in range(chunks):
        put(0, 0, c, 0, "both")

    def pair(i, state):
        state = step(*state, 0, 2 * i + 1 == items)

        def second(state):
            return step(*state, 1, 2 * i + 2 == items)

        return lax.cond(2 * i + 1 < items, second, lambda s: s, state)

    lax.fori_loop(0, (items + 1) // 2, pair, (jnp.int32(0), jnp.int32(0), block_count(0)))
    for t in range(TILES):
        o_copy(t).wait()


def prefill_call(prompt_len, q, keys, values):
    return pl.pallas_call(
        prefill_kernel,
        name="prefill",
        in_specs=[pl.BlockSpec(memory_space=pltpu.SMEM)] + [pl.BlockSpec(memory_space=pltpu.VMEM)] * 3,
        out_specs=pl.BlockSpec(memory_space=pl.ANY),
        out_shape=jax.ShapeDtypeStruct(q.shape, jnp.bfloat16),
        scratch_shapes=[
            pltpu.VMEM((TILES * TILE, HD), jnp.bfloat16),
            pltpu.VMEM((TILES, HD, TILE), jnp.float32),
            pltpu.VMEM((TILES, 8, TILE), jnp.float32),
            pltpu.VMEM((2, KB, TILE), jnp.bfloat16),
            pltpu.SemaphoreType.DMA((TILES,)),
        ],
        compiler_params=pltpu.CompilerParams(vmem_limit_bytes=VMEM),
        cost_estimate=pl.CostEstimate(
            flops=4 * 8192 * 2304 * 128, bytes_accessed=8 << 20, transcendentals=8192 * 2304
        ),
    )(prompt_len, q, keys, values)


def on_device(
    prefill_q,
    prefill_k,
    prefill_v,
    prompt_len,
    page_map,
    cache_k,
    cache_v,
    cache_len,
    decode_q,
    decode_k,
    decode_v,
):
    def chip_shift(x, chips):
        return lax.ppermute(x, "seq", [(j, (j + 2 * chips) % SEQ) for j in range(SEQ)])

    def core_swap(x):
        return lax.ppermute(x, "seq", [(j, j ^ 1) for j in range(SEQ)])

    q = prefill_q[0].reshape(ROWS * HEADS, HD)
    steps, slots = decode_q.shape[1], decode_q.shape[2]
    own = prepare_call(prefill_k[0, :, 0], prefill_v[0, :, 0])
    right = chip_shift(own, 1)
    left = chip_shift(own, -1)
    pair = core_swap(own)
    requests = (
        cache_len,
        decode_q[0],
        cache_k[0, :, :, 0],
        cache_v[0, :, :, 0],
        decode_k[0, :, :, 0].reshape(steps * slots, HD),
        decode_v[0, :, :, 0].reshape(steps * slots, HD),
    )
    first_half = decode_call(0, slots // 2, *requests)
    right, left, first_half = lax.optimization_barrier((right, left, first_half))
    far_keys = chip_shift(right[:BLOCKS], 1)
    far_values = chip_shift(left[BLOCKS:], -1)
    right_swap, left_swap = core_swap(right), core_swap(left)
    decode_out = decode_call(slots // 2, slots // 2, *requests, first_half)
    far_keys, far_values, decode_out = lax.optimization_barrier((far_keys, far_values, decode_out))
    pieces = (
        own,
        pair,
        right,
        right_swap,
        left,
        left_swap,
        far_keys,
        far_values,
        core_swap(far_keys),
        core_swap(far_values),
    )
    keys, values, pages = gather_call(prompt_len, page_map, pieces)
    pages = lax.ppermute(pages, "pool", [(0, 1), (1, 0)])
    prefill_out = prefill_call(prompt_len, q, keys, values)
    prefill_out, pages = lax.optimization_barrier((prefill_out, pages))
    page_k, page_v = emit_call(pages)
    return (
        prefill_out.reshape(prefill_q.shape),
        page_k.reshape(1, PAGES_DEV, PAGE, 1, HD),
        page_v.reshape(1, PAGES_DEV, PAGE, 1, HD),
        decode_out[None],
    )


def solution(mesh):
    placed = (
        P("pool", "seq", "mp", None),
        P("pool", "seq", "mp", None),
        P("pool", "seq", "mp", None),
        P(),
        P(),
        P("pool", "seq", None, "mp", None),
        P("pool", "seq", None, "mp", None),
        P("pool", "seq"),
        P("pool", None, "seq", "mp", None),
        P("pool", None, "seq", "mp", None),
        P("pool", None, "seq", "mp", None),
    )
    return jax.shard_map(
        on_device,
        mesh=mesh,
        in_specs=placed,
        out_specs=(
            P("pool", "seq", "mp", None),
            P("pool", "seq", None, "mp", None),
            P("pool", "seq", None, "mp", None),
            P("pool", None, "seq", "mp", None),
        ),
        check_vma=False,
    )
```

```python
import functools

import jax
import jax.numpy as jnp
from jax import lax
from jax.experimental import pallas as pl
from jax.experimental.pallas import tpu as pltpu
from jax.sharding import PartitionSpec as P

PAGE = 128
PAGES_DEV = 6
NPROMPT = 8
NPAGES = 48
SEQ = 8
ROWS = 512
HEADS = 16
HD = 128
SPAN = SEQ * ROWS
BLOCKS = ROWS // PAGE
PAD_BLOCKS = 4
KB = 512
TILE_POS = 128
TILE = TILE_POS * HEADS
TILES = ROWS // TILE_POS
CHUNK = 256
SLOW_CHUNK = 256
DEC_BLOCK = 4
DEC_VMEM = 56 * 1024 * 1024
PLACES = ((0, False), (0, True), (-1, False), (-1, True), (1, False), (1, True))
NEG = -1e30
SCALE = HD ** -0.5
SCALE2 = SCALE * 1.4426950408889634
LOW = 2.0 ** -80
HIGH = 2.0 ** 100
VMEM = 36 * 1024 * 1024
CUT_VMEM = 16 * 1024 * 1024

dot_nt = functools.partial(
    lax.dot_general, dimension_numbers=(((1,), (1,)), ((), ())), preferred_element_type=jnp.float32
)
dot_nn = functools.partial(jnp.dot, preferred_element_type=jnp.float32)


def decode_kernel(start, len_ref, q_ref, ck_ref, cv_ref, nk_ref, nv_ref, *refs):
    o_ref = refs[-1]
    steps, block = q_ref.shape[0], q_ref.shape[1]
    cache = ck_ref.shape[1]
    slots = nk_ref.shape[0] // steps
    rows = steps * HEADS
    first = start + pl.program_id(0) * block
    new_keys = nk_ref[...]
    new_values = nv_ref[...]
    lane = lax.broadcasted_iota(jnp.int32, (rows, cache), 1)
    new_lane = lax.broadcasted_iota(jnp.int32, (rows, steps * slots), 1)
    step = lax.broadcasted_iota(jnp.int32, (rows, steps * slots), 0) // HEADS
    each = range(block)
    queries = [q_ref[:, i].reshape(rows, HD) for i in each]
    old = [dot_nt(queries[i], ck_ref[i]) * SCALE for i in each]
    new = [dot_nt(queries[i], new_keys) * SCALE for i in each]
    old_w, new_w, total = [], [], []
    for i in each:
        old_i = jnp.where(lane < len_ref[0, first + i], old[i], NEG)
        new_ok = (new_lane % slots == first + i) & (new_lane // slots <= step)
        new_i = jnp.where(new_ok, new[i], NEG)
        top = jnp.maximum(
            jnp.max(old_i, axis=1, keepdims=True), jnp.max(new_i, axis=1, keepdims=True)
        )
        old_e = jnp.exp(old_i - top)
        new_e = jnp.exp(new_i - top)
        total.append(jnp.sum(old_e, axis=1, keepdims=True) + jnp.sum(new_e, axis=1, keepdims=True))
        old_w.append(old_e.astype(jnp.bfloat16))
        new_w.append(new_e.astype(jnp.bfloat16))
    for i in each:
        mixed = dot_nn(old_w[i], cv_ref[i]) + dot_nn(new_w[i], new_values)
        o_ref[:, i] = (mixed / total[i]).astype(jnp.bfloat16).reshape(steps, HEADS, HD)


def decode_call(start, count, lengths, q, ck, cv, nk, nv, *before):
    steps, slots = q.shape[0], q.shape[1]
    cache = ck.shape[1]
    skip = start // DEC_BLOCK
    return pl.pallas_call(
        functools.partial(decode_kernel, start),
        name="decode",
        grid=(count // DEC_BLOCK,),
        in_specs=[
            pl.BlockSpec(memory_space=pltpu.SMEM),
            pl.BlockSpec((steps, DEC_BLOCK, HEADS, HD), lambda i: (0, i + skip, 0, 0)),
            pl.BlockSpec((DEC_BLOCK, cache, HD), lambda i: (i + skip, 0, 0)),
            pl.BlockSpec((DEC_BLOCK, cache, HD), lambda i: (i + skip, 0, 0)),
            pl.BlockSpec((steps * slots, HD), lambda i: (0, 0)),
            pl.BlockSpec((steps * slots, HD), lambda i: (0, 0)),
        ]
        + [pl.BlockSpec(memory_space=pl.ANY)] * len(before),
        out_specs=pl.BlockSpec((steps, DEC_BLOCK, HEADS, HD), lambda i: (0, i + skip, 0, 0)),
        out_shape=jax.ShapeDtypeStruct(q.shape, jnp.bfloat16),
        input_output_aliases={6: 0} if before else {},
        compiler_params=pltpu.CompilerParams(vmem_limit_bytes=DEC_VMEM),
        cost_estimate=pl.CostEstimate(
            flops=4 * 64 * 1088 * 128 * count,
            bytes_accessed=count << 19,
            transcendentals=64 * 1088 * count,
        ),
    )(lengths, q, ck, cv, nk, nv, *before)


def prepare_kernel(k_ref, v_ref, o_ref):
    o_ref[:BLOCKS] = k_ref[...].reshape(BLOCKS, PAGE, HD)
    for i in range(BLOCKS):
        values = v_ref[i * PAGE : (i + 1) * PAGE, :].astype(jnp.float32)
        o_ref[BLOCKS + i] = values.T.astype(jnp.bfloat16)


def prepare_call(keys, values):
    return pl.pallas_call(
        prepare_kernel,
        name="prepare",
        out_shape=jax.ShapeDtypeStruct((2 * BLOCKS, PAGE, HD), jnp.bfloat16),
        cost_estimate=pl.CostEstimate(flops=0, bytes_accessed=1 << 19, transcendentals=0),
    )(keys, values)


def piece_seq(me, chips, swapped):
    core = me ^ 1 if swapped else me
    return (core + 2 * chips + SEQ) % SEQ


def gather_kernel(len_ref, map_ref, *refs):
    pieces = refs[: len(PLACES)]
    far, refs = refs[len(PLACES) : len(PLACES) + 4], refs[len(PLACES) + 4 :]
    k_buf, v_buf, page_ref, slot_of = refs
    me = lax.axis_index("seq")
    own = lax.axis_index("pool")
    k_buf[:PAD_BLOCKS] = jnp.zeros((PAD_BLOCKS, PAGE, HD), jnp.bfloat16)
    v_buf[:PAD_BLOCKS] = jnp.zeros((PAD_BLOCKS, PAGE, HD), jnp.bfloat16)
    for (chips, swapped), piece in zip(PLACES, pieces):
        at = pl.ds(piece_seq(me, chips, swapped) * BLOCKS + PAD_BLOCKS, BLOCKS)
        k_buf[at] = piece[:BLOCKS]
        v_buf[at] = piece[BLOCKS:]
    for swapped, keys, values in ((False, far[0], far[1]), (True, far[2], far[3])):
        at = pl.ds(piece_seq(me, 2, swapped) * BLOCKS + PAD_BLOCKS, BLOCKS)
        k_buf[at] = keys[...]
        v_buf[at] = values[...]

    def place(b, _):
        page = map_ref[own, b]

        @pl.when(page // PAGES_DEV == me)
        def _():
            slot_of[page % PAGES_DEV] = b

        return 0

    lax.fori_loop(0, NPAGES, place, 0)
    window = 2 * PAGE
    row = lax.broadcasted_iota(jnp.int32, (PAGE, window), 0)
    col = lax.broadcasted_iota(jnp.int32, (PAGE, window), 1)
    for i in range(PAGES_DEV):
        b = slot_of[i]
        first = jnp.int32(0)
        start = jnp.int32(0)
        source = jnp.int32(0)
        count = jnp.int32(0)
        for prompt in range(NPROMPT):
            length = len_ref[own, prompt]
            blocks = (length + PAGE - 1) // PAGE
            inside = (b >= first) & (b < first + blocks)
            offset = (b - first) * PAGE
            source = jnp.where(inside, start + offset, source)
            count = jnp.where(inside, jnp.minimum(length - offset, PAGE), count)
            first = first + blocks
            start = start + length
        low = jnp.minimum(source // PAGE, SPAN // PAGE - 2)
        hit = ((low * PAGE + col) == (source + row)) & (row < count)
        pick = jnp.where(hit, 1.0, 0.0).astype(jnp.bfloat16)
        here = slice(i * PAGE, (i + 1) * PAGE)
        at = low + PAD_BLOCKS
        keys = k_buf[pl.ds(at, 2)].reshape(window, HD)
        values = jnp.concatenate([v_buf[at], v_buf[at + 1]], axis=1)
        page_ref[0, here, :] = dot_nn(pick, keys).astype(jnp.bfloat16)
        page_ref[1, here, :] = dot_nt(pick, values).astype(jnp.bfloat16)


def gather_call(prompt_len, page_map, pieces):
    rows = PAGES_DEV * PAGE
    return pl.pallas_call(
        gather_kernel,
        name="cut_pages",
        in_specs=[pl.BlockSpec(memory_space=pltpu.SMEM)] * 2
        + [pl.BlockSpec(memory_space=pltpu.VMEM)] * len(pieces),
        out_specs=[pl.BlockSpec(memory_space=pltpu.VMEM)] * 3,
        out_shape=[jax.ShapeDtypeStruct((PAD_BLOCKS + SEQ * BLOCKS, PAGE, HD), jnp.bfloat16)] * 2
        + [jax.ShapeDtypeStruct((2, rows, HD), jnp.bfloat16)],
        scratch_shapes=[pltpu.SMEM((PAGES_DEV,), jnp.int32)],
        compiler_params=pltpu.CompilerParams(vmem_limit_bytes=CUT_VMEM),
        cost_estimate=pl.CostEstimate(
            flops=12 * 2 * 128 * 256 * 128, bytes_accessed=5 << 20, transcendentals=0
        ),
    )(prompt_len, page_map, *pieces)


def emit_kernel(page_ref, k_ref, v_ref):
    k_ref[...] = page_ref[0]
    v_ref[...] = page_ref[1]


def emit_call(pages):
    return pl.pallas_call(
        emit_kernel,
        name="emit_pages",
        out_shape=[jax.ShapeDtypeStruct(pages.shape[1:], jnp.bfloat16)] * 2,
        cost_estimate=pl.CostEstimate(flops=0, bytes_accessed=1 << 20, transcendentals=0),
    )(pages)


def prefill_kernel(len_ref, q_ref, k_buf, v_buf, o_hbm, o_ref, acc, total, weights, o_sem):
    me = lax.axis_index("seq")
    own = lax.axis_index("pool")
    chunks = TILE // CHUNK

    def tile_at(t):
        return pl.ds(pl.multiple_of(t * TILE, TILE), TILE)

    def o_copy(t):
        return pltpu.make_async_copy(o_ref.at[tile_at(t)], o_hbm.at[tile_at(t)], o_sem.at[t])

    acc[...] = jnp.zeros_like(acc)
    total[...] = jnp.zeros_like(total)

    def segment_start(position):
        start = jnp.int32(0)
        end = jnp.int32(0)
        for prompt in range(NPROMPT):
            end = end + len_ref[own, prompt]
            start = jnp.where(end <= position, end, start)
        return start

    def first_position(t):
        return me * ROWS + t * TILE_POS

    def tile_end(t):
        return first_position(t) + TILE_POS

    def tile_low(t):
        return segment_start(first_position(t))

    def block_count(t):
        return (tile_end(t) - tile_low(t) + KB - 1) // KB

    def block_start(t, j):
        return tile_end(t) - (j + 1) * KB

    def keys_at(start):
        at = pl.ds(start // PAGE + PAD_BLOCKS, KB // PAGE)
        return k_buf[at].reshape(KB, HD)

    def values_at(start):
        block = start // PAGE + PAD_BLOCKS
        return jnp.concatenate([v_buf[block + i] for i in range(KB // PAGE)], axis=1)

    def scores(start, t, c, width):
        at = pl.ds(pl.multiple_of(t * TILE + c * width, width), width)
        return dot_nt(keys_at(start), q_ref[at, :]) * SCALE2

    def allowed(start, t, c, width):
        lane = lax.broadcasted_iota(jnp.int32, (1, width), 1)
        high = first_position(t) + c * (width // HEADS) + lane // HEADS
        low = segment_start(high)
        k_pos = start + lax.broadcasted_iota(jnp.int32, (KB, width), 0)
        return (k_pos >= low) & (k_pos <= high)

    def put(t, j, c, slot, mode):
        at = slice(c * CHUNK, (c + 1) * CHUNK)
        start = block_start(t, j)
        if mode == "half":
            half = KB // 2
            blocks = half // PAGE
            keys = k_buf[pl.ds((start + half) // PAGE + PAD_BLOCKS, blocks)].reshape(half, HD)
            q_at = pl.ds(pl.multiple_of(t * TILE + c * CHUNK, CHUNK), CHUNK)
            terms = jnp.exp2(dot_nt(keys, q_ref[q_at, :]) * SCALE2)
            low = row_limits(t, c)[0] - (start + half)
            k_pos = lax.broadcasted_iota(jnp.int32, (half, CHUNK), 0)
            terms = jnp.where(k_pos >= low, terms, 0.0)
            weights[slot, :half, at] = jnp.zeros((half, CHUNK), jnp.bfloat16)
            weights[slot, half:, at] = terms.astype(jnp.bfloat16)
            total[t, :, at] += jnp.sum(terms.reshape(half // 8, 8, CHUNK), axis=0)
            return
        terms = jnp.exp2(scores(start, t, c, CHUNK))
        if mode != "none":
            terms = clear(terms, start, t, c, mode)
        weights[slot, :, at] = terms.astype(jnp.bfloat16)
        total[t, :, at] += jnp.sum(terms.reshape(KB // 8, 8, CHUNK), axis=0)

    def mix(t, j, c, slot):
        at = slice(c * CHUNK, (c + 1) * CHUNK)
        acc[t, :, at] += dot_nn(values_at(block_start(t, j)), weights[slot, :, at])

    def row_limits(t, c):
        lane = lax.broadcasted_iota(jnp.int32, (1, CHUNK), 1)
        high = first_position(t) + c * (CHUNK // HEADS) + lane // HEADS
        return segment_start(high), high

    def clear(terms, start, t, c, mode):
        low, high = row_limits(t, c)
        if mode == "both":
            low = low - start
            terms = jnp.where(lax.broadcasted_iota(jnp.int32, (KB, CHUNK), 0) >= low, terms, 0.0)
        cut = KB - TILE_POS
        k_pos = lax.broadcasted_iota(jnp.int32, (TILE_POS, CHUNK), 0)
        end = jnp.where(k_pos <= high - (start + cut), terms[cut:], 0.0)
        return jnp.concatenate([terms[:cut], end], axis=0)

    def slow_tile(t):
        width = SLOW_CHUNK

        def one(c, _):
            def block(j, carried):
                top, below, mixed = carried
                start = block_start(t, j)
                ok = allowed(start, t, c, width)
                here = jnp.where(ok, scores(start, t, c, width), NEG)
                new_top = jnp.maximum(top, jnp.max(here, axis=0, keepdims=True))
                terms = jnp.where(ok, jnp.exp2(here - new_top), 0.0)
                scale = jnp.exp2(top - new_top)
                below = below * scale + jnp.sum(terms, axis=0, keepdims=True)
                mixed = mixed * scale + dot_nn(values_at(start), terms.astype(jnp.bfloat16))
                return new_top, below, mixed

            _, below, mixed = lax.fori_loop(
                0,
                block_count(t),
                block,
                (
                    jnp.full((1, width), NEG, jnp.float32),
                    jnp.zeros((1, width), jnp.float32),
                    jnp.zeros((HD, width), jnp.float32),
                ),
            )
            at = pl.ds(pl.multiple_of(t * TILE + c * width, width), width)
            o_ref[at, :] = (mixed / below).T.astype(jnp.bfloat16)
            return 0

        lax.fori_loop(0, TILE // width, one, 0)

    def finish(t):
        below = jnp.sum(total[t], axis=0, keepdims=True)
        o_ref[tile_at(t), :] = (acc[t] / below).T.astype(jnp.bfloat16)
        bad = jnp.max(jnp.where((below >= LOW) & (below <= HIGH), 0.0, 1.0))

        @pl.when(bad > 0.0)
        def _():
            slow_tile(t)

        o_copy(t).start()

    def step(t, j, count, slot, last):
        wrap = j + 1 == count
        t2 = jnp.where(wrap, t + 1, t)
        j2 = jnp.where(wrap, 0, j + 1)
        t2 = jnp.minimum(t2, TILES - 1)
        start = block_start(t2, j2)
        bounded = segment_start(tile_end(t2) - 1) > start
        half = (j2 > 0) & (tile_low(t2) >= start + KB // 2)
        both = bounded & jnp.logical_not(half)
        edge = (j2 == 0) & jnp.logical_not(bounded)
        inner = (j2 > 0) & jnp.logical_not(bounded)

        for mode, chosen in (("both", both), ("half", half), ("edge", edge), ("none", inner)):

            @pl.when(chosen & jnp.logical_not(last))
            def _():
                for c in range(chunks):
                    put(t2, j2, c, 1 - slot, mode)
                    mix(t, j, c, slot)

        @pl.when(last)
        def _():
            for c in range(chunks):
                mix(t, j, c, slot)

        @pl.when(wrap)
        def _():
            finish(t)

        return t2, j2, jnp.where(wrap, block_count(t2), count)

    items = jnp.int32(0)
    for t in range(TILES):
        items = items + block_count(t)
    for c in range(chunks):
        put(0, 0, c, 0, "both")

    def pair(i, state):
        state = step(*state, 0, 2 * i + 1 == items)

        def second(state):
            return step(*state, 1, 2 * i + 2 == items)

        return lax.cond(2 * i + 1 < items, second, lambda s: s, state)

    lax.fori_loop(0, (items + 1) // 2, pair, (jnp.int32(0), jnp.int32(0), block_count(0)))
    for t in range(TILES):
        o_copy(t).wait()


def prefill_call(prompt_len, q, keys, values):
    return pl.pallas_call(
        prefill_kernel,
        name="prefill",
        in_specs=[pl.BlockSpec(memory_space=pltpu.SMEM)] + [pl.BlockSpec(memory_space=pltpu.VMEM)] * 3,
        out_specs=pl.BlockSpec(memory_space=pl.ANY),
        out_shape=jax.ShapeDtypeStruct(q.shape, jnp.bfloat16),
        scratch_shapes=[
            pltpu.VMEM((TILES * TILE, HD), jnp.bfloat16),
            pltpu.VMEM((TILES, HD, TILE), jnp.float32),
            pltpu.VMEM((TILES, 8, TILE), jnp.float32),
            pltpu.VMEM((2, KB, TILE), jnp.bfloat16),
            pltpu.SemaphoreType.DMA((TILES,)),
        ],
        compiler_params=pltpu.CompilerParams(vmem_limit_bytes=VMEM),
        cost_estimate=pl.CostEstimate(
            flops=4 * 8192 * 2304 * 128, bytes_accessed=8 << 20, transcendentals=8192 * 2304
        ),
    )(prompt_len, q, keys, values)


def on_device(
    prefill_q,
    prefill_k,
    prefill_v,
    prompt_len,
    page_map,
    cache_k,
    cache_v,
    cache_len,
    decode_q,
    decode_k,
    decode_v,
):
    def chip_shift(x, chips):
        return lax.ppermute(x, "seq", [(j, (j + 2 * chips) % SEQ) for j in range(SEQ)])

    def core_swap(x):
        return lax.ppermute(x, "seq", [(j, j ^ 1) for j in range(SEQ)])

    q = prefill_q[0].reshape(ROWS * HEADS, HD)
    steps, slots = decode_q.shape[1], decode_q.shape[2]
    own = prepare_call(prefill_k[0, :, 0], prefill_v[0, :, 0])
    right = chip_shift(own, 1)
    left = chip_shift(own, -1)
    pair = core_swap(own)
    requests = (
        cache_len,
        decode_q[0],
        cache_k[0, :, :, 0],
        cache_v[0, :, :, 0],
        decode_k[0, :, :, 0].reshape(steps * slots, HD),
        decode_v[0, :, :, 0].reshape(steps * slots, HD),
    )
    first_half = decode_call(0, slots // 2, *requests)
    right, left, pair, first_half = lax.optimization_barrier((right, left, pair, first_half))
    far_keys = chip_shift(right[:BLOCKS], 1)
    far_values = chip_shift(left[BLOCKS:], -1)
    right_swap, left_swap = core_swap(right), core_swap(left)
    decode_out = decode_call(slots // 2, slots // 2, *requests, first_half)
    far_keys, far_values, decode_out = lax.optimization_barrier((far_keys, far_values, decode_out))
    pieces = (
        own,
        pair,
        right,
        right_swap,
        left,
        left_swap,
        far_keys,
        far_values,
        core_swap(far_keys),
        core_swap(far_values),
    )
    keys, values, pages = gather_call(prompt_len, page_map, pieces)
    pages = lax.ppermute(pages, "pool", [(0, 1), (1, 0)])
    prefill_out = prefill_call(prompt_len, q, keys, values)
    prefill_out, pages = lax.optimization_barrier((prefill_out, pages))
    page_k, page_v = emit_call(pages)
    return (
        prefill_out.reshape(prefill_q.shape),
        page_k.reshape(1, PAGES_DEV, PAGE, 1, HD),
        page_v.reshape(1, PAGES_DEV, PAGE, 1, HD),
        decode_out[None],
    )


def solution(mesh):
    placed = (
        P("pool", "seq", "mp", None),
        P("pool", "seq", "mp", None),
        P("pool", "seq", "mp", None),
        P(),
        P(),
        P("pool", "seq", None, "mp", None),
        P("pool", "seq", None, "mp", None),
        P("pool", "seq"),
        P("pool", None, "seq", "mp", None),
        P("pool", None, "seq", "mp", None),
        P("pool", None, "seq", "mp", None),
    )
    return jax.shard_map(
        on_device,
        mesh=mesh,
        in_specs=placed,
        out_specs=(
            P("pool", "seq", "mp", None),
            P("pool", "seq", None, "mp", None),
            P("pool", "seq", None, "mp", None),
            P("pool", None, "seq", "mp", None),
        ),
        check_vma=False,
    )
```

```python
import functools

import jax
import jax.numpy as jnp
from jax import lax
from jax.experimental import pallas as pl
from jax.experimental.pallas import tpu as pltpu
from jax.sharding import PartitionSpec as P

PAGE = 128
PAGES_DEV = 6
NPROMPT = 8
NPAGES = 48
WINDOW = 2 * PAGE
SEQ = 8
ROWS = 512
HEADS = 16
HD = 128
SPAN = SEQ * ROWS
BLOCKS = ROWS // PAGE
PAD_BLOCKS = 4
KB = 512
TILE_POS = 128
TILE = TILE_POS * HEADS
TILES = ROWS // TILE_POS
CHUNK = 256
SLOW_CHUNK = 256
DEC_BLOCK = 4
DEC_VMEM = 56 * 1024 * 1024
PLACES = ((0, False), (0, True), (-1, False), (-1, True), (1, False), (1, True), (2, False), (2, True))
PIECES = PLACES
NEG = -1e30
SCALE = HD ** -0.5
SCALE2 = SCALE * 1.4426950408889634
LOW = 2.0 ** -80
HIGH = 2.0 ** 100
VMEM = 36 * 1024 * 1024
CUT_VMEM = 16 * 1024 * 1024

dot_nt = functools.partial(
    lax.dot_general, dimension_numbers=(((1,), (1,)), ((), ())), preferred_element_type=jnp.float32
)
dot_nn = functools.partial(jnp.dot, preferred_element_type=jnp.float32)


def decode_kernel(len_ref, q_ref, ck_ref, cv_ref, nk_ref, nv_ref, o_ref):
    steps, block = q_ref.shape[0], q_ref.shape[1]
    cache = ck_ref.shape[1]
    slots = nk_ref.shape[0] // steps
    rows = steps * HEADS
    first = pl.program_id(0) * block
    new_keys = nk_ref[...]
    new_values = nv_ref[...]
    lane = lax.broadcasted_iota(jnp.int32, (rows, cache), 1)
    new_lane = lax.broadcasted_iota(jnp.int32, (rows, steps * slots), 1)
    step = lax.broadcasted_iota(jnp.int32, (rows, steps * slots), 0) // HEADS
    each = range(block)
    queries = [q_ref[:, i].reshape(rows, HD) for i in each]
    old = [dot_nt(queries[i], ck_ref[i]) * SCALE for i in each]
    new = [dot_nt(queries[i], new_keys) * SCALE for i in each]
    old_w, new_w, total = [], [], []
    for i in each:
        old_i = jnp.where(lane < len_ref[0, first + i], old[i], NEG)
        new_ok = (new_lane % slots == first + i) & (new_lane // slots <= step)
        new_i = jnp.where(new_ok, new[i], NEG)
        top = jnp.maximum(
            jnp.max(old_i, axis=1, keepdims=True), jnp.max(new_i, axis=1, keepdims=True)
        )
        old_e = jnp.exp(old_i - top)
        new_e = jnp.exp(new_i - top)
        total.append(jnp.sum(old_e, axis=1, keepdims=True) + jnp.sum(new_e, axis=1, keepdims=True))
        old_w.append(old_e.astype(jnp.bfloat16))
        new_w.append(new_e.astype(jnp.bfloat16))
    for i in each:
        mixed = dot_nn(old_w[i], cv_ref[i]) + dot_nn(new_w[i], new_values)
        o_ref[:, i] = (mixed / total[i]).astype(jnp.bfloat16).reshape(steps, HEADS, HD)


def decode_call(lengths, q, ck, cv, nk, nv):
    steps, slots = q.shape[0], q.shape[1]
    cache = ck.shape[1]
    return pl.pallas_call(
        decode_kernel,
        name="decode",
        grid=(slots // DEC_BLOCK,),
        in_specs=[
            pl.BlockSpec(memory_space=pltpu.SMEM),
            pl.BlockSpec((steps, DEC_BLOCK, HEADS, HD), lambda i: (0, i, 0, 0)),
            pl.BlockSpec((DEC_BLOCK, cache, HD), lambda i: (i, 0, 0)),
            pl.BlockSpec((DEC_BLOCK, cache, HD), lambda i: (i, 0, 0)),
            pl.BlockSpec((steps * slots, HD), lambda i: (0, 0)),
            pl.BlockSpec((steps * slots, HD), lambda i: (0, 0)),
        ],
        out_specs=pl.BlockSpec((steps, DEC_BLOCK, HEADS, HD), lambda i: (0, i, 0, 0)),
        out_shape=jax.ShapeDtypeStruct(q.shape, jnp.bfloat16),
        compiler_params=pltpu.CompilerParams(vmem_limit_bytes=DEC_VMEM),
        cost_estimate=pl.CostEstimate(
            flops=4 * 64 * 1088 * 128 * 16, bytes_accessed=9 << 20, transcendentals=64 * 1088 * 16
        ),
    )(lengths, q, ck, cv, nk, nv)


def prepare_kernel(k_ref, v_ref, o_ref):
    o_ref[:BLOCKS] = k_ref[...].reshape(BLOCKS, PAGE, HD)
    for i in range(BLOCKS):
        values = v_ref[i * PAGE : (i + 1) * PAGE, :].astype(jnp.float32)
        o_ref[BLOCKS + i] = values.T.astype(jnp.bfloat16)


def prepare_call(keys, values):
    return pl.pallas_call(
        prepare_kernel,
        name="prepare",
        out_shape=jax.ShapeDtypeStruct((2 * BLOCKS, PAGE, HD), jnp.bfloat16),
        cost_estimate=pl.CostEstimate(flops=0, bytes_accessed=1 << 19, transcendentals=0),
    )(keys, values)


def piece_seq(me, chips, swapped):
    core = me ^ 1 if swapped else me
    return (core + 2 * chips + SEQ) % SEQ


def plan_kernel(len_ref, map_ref, low_ref, pick_ref, slot_of):
    me = lax.axis_index("seq")
    own = lax.axis_index("pool")

    def place(b, _):
        page = map_ref[own, b]

        @pl.when(page // PAGES_DEV == me)
        def _():
            slot_of[page % PAGES_DEV] = b

        return 0

    lax.fori_loop(0, NPAGES, place, 0)
    row = lax.broadcasted_iota(jnp.int32, (PAGE, WINDOW), 0)
    col = lax.broadcasted_iota(jnp.int32, (PAGE, WINDOW), 1)
    for i in range(PAGES_DEV):
        b = slot_of[i]
        first = jnp.int32(0)
        start = jnp.int32(0)
        source = jnp.int32(0)
        count = jnp.int32(0)
        for prompt in range(NPROMPT):
            length = len_ref[own, prompt]
            blocks = (length + PAGE - 1) // PAGE
            inside = (b >= first) & (b < first + blocks)
            offset = (b - first) * PAGE
            source = jnp.where(inside, start + offset, source)
            count = jnp.where(inside, jnp.minimum(length - offset, PAGE), count)
            first = first + blocks
            start = start + length
        low = jnp.minimum(source // PAGE, SPAN // PAGE - 2)
        hit = ((low * PAGE + col) == (source + row)) & (row < count)
        pick_ref[i] = jnp.where(hit, 1.0, 0.0).astype(jnp.bfloat16)
        low_ref[i] = low


def plan_call(prompt_len, page_map):
    return pl.pallas_call(
        plan_kernel,
        name="plan_pages",
        in_specs=[pl.BlockSpec(memory_space=pltpu.SMEM)] * 2,
        out_specs=[pl.BlockSpec(memory_space=pltpu.SMEM), pl.BlockSpec(memory_space=pltpu.VMEM)],
        out_shape=[
            jax.ShapeDtypeStruct((PAGES_DEV,), jnp.int32),
            jax.ShapeDtypeStruct((PAGES_DEV, PAGE, WINDOW), jnp.bfloat16),
        ],
        scratch_shapes=[pltpu.SMEM((PAGES_DEV,), jnp.int32)],
        cost_estimate=pl.CostEstimate(flops=1 << 20, bytes_accessed=1 << 19, transcendentals=0),
    )(prompt_len, page_map)


def gather_kernel(low_ref, pick_ref, *refs):
    pieces = refs[: len(PIECES)]
    k_buf, v_buf, pk_ref, pv_ref = refs[len(PIECES) :]
    me = lax.axis_index("seq")
    k_buf[:PAD_BLOCKS] = jnp.zeros((PAD_BLOCKS, PAGE, HD), jnp.bfloat16)
    v_buf[:PAD_BLOCKS] = jnp.zeros((PAD_BLOCKS, PAGE, HD), jnp.bfloat16)
    for (chips, swapped), piece in zip(PIECES, pieces):
        at = pl.ds(piece_seq(me, chips, swapped) * BLOCKS + PAD_BLOCKS, BLOCKS)
        k_buf[at] = piece[:BLOCKS]
        v_buf[at] = piece[BLOCKS:]
    new_keys, new_values = [], []
    for i in range(PAGES_DEV):
        at = low_ref[i] + PAD_BLOCKS
        keys = k_buf[pl.ds(at, 2)].reshape(WINDOW, HD)
        values = jnp.concatenate([v_buf[at], v_buf[at + 1]], axis=1)
        new_keys.append(dot_nn(pick_ref[i], keys).astype(jnp.bfloat16))
        new_values.append(dot_nt(pick_ref[i], values).astype(jnp.bfloat16))
    for i in range(PAGES_DEV):
        here = slice(i * PAGE, (i + 1) * PAGE)
        pk_ref[here, :] = new_keys[i]
        pv_ref[here, :] = new_values[i]


def gather_call(lows, picks, pieces):
    rows = PAGES_DEV * PAGE
    return pl.pallas_call(
        gather_kernel,
        name="cut_pages",
        in_specs=[pl.BlockSpec(memory_space=pltpu.SMEM)]
        + [pl.BlockSpec(memory_space=pltpu.VMEM)] * (1 + len(PIECES)),
        out_specs=[pl.BlockSpec(memory_space=pltpu.VMEM)] * 4,
        out_shape=[jax.ShapeDtypeStruct((PAD_BLOCKS + SEQ * BLOCKS, PAGE, HD), jnp.bfloat16)] * 2
        + [jax.ShapeDtypeStruct((rows, HD), jnp.bfloat16)] * 2,
        compiler_params=pltpu.CompilerParams(vmem_limit_bytes=CUT_VMEM),
        cost_estimate=pl.CostEstimate(
            flops=12 * 2 * 128 * 256 * 128, bytes_accessed=5 << 20, transcendentals=0
        ),
    )(lows, picks, *pieces)


def prefill_kernel(len_ref, q_ref, k_buf, v_buf, o_hbm, o_ref, acc, total, weights, o_sem):
    me = lax.axis_index("seq")
    own = lax.axis_index("pool")
    chunks = TILE // CHUNK

    def tile_at(t):
        return pl.ds(pl.multiple_of(t * TILE, TILE), TILE)

    def o_copy(t):
        return pltpu.make_async_copy(o_ref.at[tile_at(t)], o_hbm.at[tile_at(t)], o_sem.at[t])

    acc[...] = jnp.zeros_like(acc)
    total[...] = jnp.zeros_like(total)

    def segment_start(position):
        start = jnp.int32(0)
        end = jnp.int32(0)
        for prompt in range(NPROMPT):
            end = end + len_ref[own, prompt]
            start = jnp.where(end <= position, end, start)
        return start

    def first_position(t):
        return me * ROWS + t * TILE_POS

    def tile_end(t):
        return first_position(t) + TILE_POS

    def tile_low(t):
        return segment_start(first_position(t))

    def block_count(t):
        return (tile_end(t) - tile_low(t) + KB - 1) // KB

    def block_start(t, j):
        return tile_end(t) - (j + 1) * KB

    def keys_at(start):
        at = pl.ds(start // PAGE + PAD_BLOCKS, KB // PAGE)
        return k_buf[at].reshape(KB, HD)

    def values_at(start):
        block = start // PAGE + PAD_BLOCKS
        return jnp.concatenate([v_buf[block + i] for i in range(KB // PAGE)], axis=1)

    def scores(start, t, c, width):
        at = pl.ds(pl.multiple_of(t * TILE + c * width, width), width)
        return dot_nt(keys_at(start), q_ref[at, :]) * SCALE2

    def allowed(start, t, c, width):
        lane = lax.broadcasted_iota(jnp.int32, (1, width), 1)
        high = first_position(t) + c * (width // HEADS) + lane // HEADS
        low = segment_start(high)
        k_pos = start + lax.broadcasted_iota(jnp.int32, (KB, width), 0)
        return (k_pos >= low) & (k_pos <= high)

    def put(t, j, c, slot, mode):
        at = slice(c * CHUNK, (c + 1) * CHUNK)
        start = block_start(t, j)
        if mode == "half":
            half = KB // 2
            blocks = half // PAGE
            keys = k_buf[pl.ds((start + half) // PAGE + PAD_BLOCKS, blocks)].reshape(half, HD)
            q_at = pl.ds(pl.multiple_of(t * TILE + c * CHUNK, CHUNK), CHUNK)
            terms = jnp.exp2(dot_nt(keys, q_ref[q_at, :]) * SCALE2)
            low = row_limits(t, c)[0] - (start + half)
            k_pos = lax.broadcasted_iota(jnp.int32, (half, CHUNK), 0)
            terms = jnp.where(k_pos >= low, terms, 0.0)
            weights[slot, :half, at] = jnp.zeros((half, CHUNK), jnp.bfloat16)
            weights[slot, half:, at] = terms.astype(jnp.bfloat16)
            total[t, :, at] += jnp.sum(terms.reshape(half // 8, 8, CHUNK), axis=0)
            return
        terms = jnp.exp2(scores(start, t, c, CHUNK))
        if mode != "none":
            terms = clear(terms, start, t, c, mode)
        weights[slot, :, at] = terms.astype(jnp.bfloat16)
        total[t, :, at] += jnp.sum(terms.reshape(KB // 8, 8, CHUNK), axis=0)

    def mix(t, j, c, slot):
        at = slice(c * CHUNK, (c + 1) * CHUNK)
        acc[t, :, at] += dot_nn(values_at(block_start(t, j)), weights[slot, :, at])

    def row_limits(t, c):
        lane = lax.broadcasted_iota(jnp.int32, (1, CHUNK), 1)
        high = first_position(t) + c * (CHUNK // HEADS) + lane // HEADS
        return segment_start(high), high

    def clear(terms, start, t, c, mode):
        low, high = row_limits(t, c)
        if mode == "both":
            low = low - start
            terms = jnp.where(lax.broadcasted_iota(jnp.int32, (KB, CHUNK), 0) >= low, terms, 0.0)
        cut = KB - TILE_POS
        k_pos = lax.broadcasted_iota(jnp.int32, (TILE_POS, CHUNK), 0)
        end = jnp.where(k_pos <= high - (start + cut), terms[cut:], 0.0)
        return jnp.concatenate([terms[:cut], end], axis=0)

    def slow_tile(t):
        width = SLOW_CHUNK

        def one(c, _):
            def block(j, carried):
                top, below, mixed = carried
                start = block_start(t, j)
                ok = allowed(start, t, c, width)
                here = jnp.where(ok, scores(start, t, c, width), NEG)
                new_top = jnp.maximum(top, jnp.max(here, axis=0, keepdims=True))
                terms = jnp.where(ok, jnp.exp2(here - new_top), 0.0)
                scale = jnp.exp2(top - new_top)
                below = below * scale + jnp.sum(terms, axis=0, keepdims=True)
                mixed = mixed * scale + dot_nn(values_at(start), terms.astype(jnp.bfloat16))
                return new_top, below, mixed

            _, below, mixed = lax.fori_loop(
                0,
                block_count(t),
                block,
                (
                    jnp.full((1, width), NEG, jnp.float32),
                    jnp.zeros((1, width), jnp.float32),
                    jnp.zeros((HD, width), jnp.float32),
                ),
            )
            at = pl.ds(pl.multiple_of(t * TILE + c * width, width), width)
            o_ref[at, :] = (mixed / below).T.astype(jnp.bfloat16)
            return 0

        lax.fori_loop(0, TILE // width, one, 0)

    def finish(t):
        below = jnp.sum(total[t], axis=0, keepdims=True)
        o_ref[tile_at(t), :] = (acc[t] / below).T.astype(jnp.bfloat16)
        bad = jnp.max(jnp.where((below >= LOW) & (below <= HIGH), 0.0, 1.0))

        @pl.when(bad > 0.0)
        def _():
            slow_tile(t)

        o_copy(t).start()

    def step(t, j, count, slot, last):
        wrap = j + 1 == count
        t2 = jnp.where(wrap, t + 1, t)
        j2 = jnp.where(wrap, 0, j + 1)
        t2 = jnp.minimum(t2, TILES - 1)
        start = block_start(t2, j2)
        bounded = segment_start(tile_end(t2) - 1) > start
        half = (j2 > 0) & (tile_low(t2) >= start + KB // 2)
        both = bounded & jnp.logical_not(half)
        edge = (j2 == 0) & jnp.logical_not(bounded)
        inner = (j2 > 0) & jnp.logical_not(bounded)

        for mode, chosen in (("both", both), ("half", half), ("edge", edge), ("none", inner)):

            @pl.when(chosen & jnp.logical_not(last))
            def _():
                for c in range(chunks):
                    put(t2, j2, c, 1 - slot, mode)
                    mix(t, j, c, slot)

        @pl.when(last)
        def _():
            for c in range(chunks):
                mix(t, j, c, slot)

        @pl.when(wrap)
        def _():
            finish(t)

        return t2, j2, jnp.where(wrap, block_count(t2), count)

    items = jnp.int32(0)
    for t in range(TILES):
        items = items + block_count(t)
    for c in range(chunks):
        put(0, 0, c, 0, "both")

    def pair(i, state):
        state = step(*state, 0, 2 * i + 1 == items)

        def second(state):
            return step(*state, 1, 2 * i + 2 == items)

        return lax.cond(2 * i + 1 < items, second, lambda s: s, state)

    lax.fori_loop(0, (items + 1) // 2, pair, (jnp.int32(0), jnp.int32(0), block_count(0)))
    for t in range(TILES):
        o_copy(t).wait()


def prefill_call(prompt_len, q, keys, values):
    return pl.pallas_call(
        prefill_kernel,
        name="prefill",
        in_specs=[pl.BlockSpec(memory_space=pltpu.SMEM)] + [pl.BlockSpec(memory_space=pltpu.VMEM)] * 3,
        out_specs=pl.BlockSpec(memory_space=pl.ANY),
        out_shape=jax.ShapeDtypeStruct(q.shape, jnp.bfloat16),
        scratch_shapes=[
            pltpu.VMEM((TILES * TILE, HD), jnp.bfloat16),
            pltpu.VMEM((TILES, HD, TILE), jnp.float32),
            pltpu.VMEM((TILES, 8, TILE), jnp.float32),
            pltpu.VMEM((2, KB, TILE), jnp.bfloat16),
            pltpu.SemaphoreType.DMA((TILES,)),
        ],
        compiler_params=pltpu.CompilerParams(vmem_limit_bytes=VMEM),
        cost_estimate=pl.CostEstimate(
            flops=4 * 8192 * 2304 * 128, bytes_accessed=8 << 20, transcendentals=8192 * 2304
        ),
    )(prompt_len, q, keys, values)


def on_device(
    prefill_q,
    prefill_k,
    prefill_v,
    prompt_len,
    page_map,
    cache_k,
    cache_v,
    cache_len,
    decode_q,
    decode_k,
    decode_v,
):
    def chip_shift(x, chips):
        return lax.ppermute(x, "seq", [(j, (j + 2 * chips) % SEQ) for j in range(SEQ)])

    def core_swap(x):
        return lax.ppermute(x, "seq", [(j, j ^ 1) for j in range(SEQ)])

    q = prefill_q[0].reshape(ROWS * HEADS, HD)
    steps, slots = decode_q.shape[1], decode_q.shape[2]
    own = prepare_call(prefill_k[0, :, 0], prefill_v[0, :, 0])
    right = chip_shift(own, 1)
    left = chip_shift(own, -1)
    far = chip_shift(own, 2)
    pair = core_swap(own)
    decode_out = decode_call(
        cache_len,
        decode_q[0],
        cache_k[0, :, :, 0],
        cache_v[0, :, :, 0],
        decode_k[0, :, :, 0].reshape(steps * slots, HD),
        decode_v[0, :, :, 0].reshape(steps * slots, HD),
    )
    lows, picks = plan_call(prompt_len, page_map)
    right, left, far, decode_out, lows, picks = lax.optimization_barrier(
        (right, left, far, decode_out, lows, picks)
    )
    right_swap, left_swap = core_swap(right), core_swap(left)
    pieces = (own, pair, right, right_swap, left, left_swap, far, core_swap(far))
    keys, values, pk, pv = gather_call(lows, picks, pieces)
    page_k = lax.ppermute(pk, "pool", [(0, 1), (1, 0)])
    page_v = lax.ppermute(pv, "pool", [(0, 1), (1, 0)])
    prefill_out = prefill_call(prompt_len, q, keys, values)
    return (
        prefill_out.reshape(prefill_q.shape),
        page_k.reshape(1, PAGES_DEV, PAGE, 1, HD),
        page_v.reshape(1, PAGES_DEV, PAGE, 1, HD),
        decode_out[None],
    )


def solution(mesh):
    placed = (
        P("pool", "seq", "mp", None),
        P("pool", "seq", "mp", None),
        P("pool", "seq", "mp", None),
        P(),
        P(),
        P("pool", "seq", None, "mp", None),
        P("pool", "seq", None, "mp", None),
        P("pool", "seq"),
        P("pool", None, "seq", "mp", None),
        P("pool", None, "seq", "mp", None),
        P("pool", None, "seq", "mp", None),
    )
    return jax.shard_map(
        on_device,
        mesh=mesh,
        in_specs=placed,
        out_specs=(
            P("pool", "seq", "mp", None),
            P("pool", "seq", None, "mp", None),
            P("pool", "seq", None, "mp", None),
            P("pool", None, "seq", "mp", None),
        ),
        check_vma=False,
    )
```

```python
import functools

import jax
import jax.numpy as jnp
from jax import lax
from jax.experimental import pallas as pl
from jax.experimental.pallas import tpu as pltpu
from jax.sharding import PartitionSpec as P

PAGE = 128
PAGES_DEV = 6
NPROMPT = 8
NPAGES = 48
WINDOW = 2 * PAGE
SEQ = 8
ROWS = 512
HEADS = 16
HD = 128
SPAN = SEQ * ROWS
BLOCKS = ROWS // PAGE
PAD_BLOCKS = 4
KB = 512
TILE_POS = 128
TILE = TILE_POS * HEADS
TILES = ROWS // TILE_POS
CHUNK = 256
SLOW_CHUNK = 256
DEC_BLOCK = 4
DEC_VMEM = 56 * 1024 * 1024
PLACES = ((0, False), (0, True), (-1, False), (-1, True), (1, False), (1, True), (2, False), (2, True))
PIECES = PLACES
NEG = -1e30
SCALE = HD ** -0.5
SCALE2 = SCALE * 1.4426950408889634
LOW = 2.0 ** -80
HIGH = 2.0 ** 100
VMEM = 36 * 1024 * 1024
CUT_VMEM = 16 * 1024 * 1024

dot_nt = functools.partial(
    lax.dot_general, dimension_numbers=(((1,), (1,)), ((), ())), preferred_element_type=jnp.float32
)
dot_nn = functools.partial(jnp.dot, preferred_element_type=jnp.float32)


def decode_kernel(len_ref, q_ref, ck_ref, cv_ref, nk_ref, nv_ref, o_ref):
    steps, block = q_ref.shape[0], q_ref.shape[1]
    cache = ck_ref.shape[1]
    slots = nk_ref.shape[0] // steps
    rows = steps * HEADS
    first = pl.program_id(0) * block
    new_keys = nk_ref[...]
    new_values = nv_ref[...]
    lane = lax.broadcasted_iota(jnp.int32, (rows, cache), 1)
    new_lane = lax.broadcasted_iota(jnp.int32, (rows, steps * slots), 1)
    step = lax.broadcasted_iota(jnp.int32, (rows, steps * slots), 0) // HEADS
    each = range(block)
    queries = [q_ref[:, i].reshape(rows, HD) for i in each]
    old = [dot_nt(queries[i], ck_ref[i]) * SCALE for i in each]
    new = [dot_nt(queries[i], new_keys) * SCALE for i in each]
    old_w, new_w, total = [], [], []
    for i in each:
        old_i = jnp.where(lane < len_ref[0, first + i], old[i], NEG)
        new_ok = (new_lane % slots == first + i) & (new_lane // slots <= step)
        new_i = jnp.where(new_ok, new[i], NEG)
        top = jnp.maximum(
            jnp.max(old_i, axis=1, keepdims=True), jnp.max(new_i, axis=1, keepdims=True)
        )
        old_e = jnp.exp(old_i - top)
        new_e = jnp.exp(new_i - top)
        total.append(jnp.sum(old_e, axis=1, keepdims=True) + jnp.sum(new_e, axis=1, keepdims=True))
        old_w.append(old_e.astype(jnp.bfloat16))
        new_w.append(new_e.astype(jnp.bfloat16))
    for i in each:
        mixed = dot_nn(old_w[i], cv_ref[i]) + dot_nn(new_w[i], new_values)
        o_ref[:, i] = (mixed / total[i]).astype(jnp.bfloat16).reshape(steps, HEADS, HD)


def decode_call(lengths, q, ck, cv, nk, nv):
    steps, slots = q.shape[0], q.shape[1]
    cache = ck.shape[1]
    return pl.pallas_call(
        decode_kernel,
        name="decode",
        grid=(slots // DEC_BLOCK,),
        in_specs=[
            pl.BlockSpec(memory_space=pltpu.SMEM),
            pl.BlockSpec((steps, DEC_BLOCK, HEADS, HD), lambda i: (0, i, 0, 0)),
            pl.BlockSpec((DEC_BLOCK, cache, HD), lambda i: (i, 0, 0)),
            pl.BlockSpec((DEC_BLOCK, cache, HD), lambda i: (i, 0, 0)),
            pl.BlockSpec((steps * slots, HD), lambda i: (0, 0)),
            pl.BlockSpec((steps * slots, HD), lambda i: (0, 0)),
        ],
        out_specs=pl.BlockSpec((steps, DEC_BLOCK, HEADS, HD), lambda i: (0, i, 0, 0)),
        out_shape=jax.ShapeDtypeStruct(q.shape, jnp.bfloat16),
        compiler_params=pltpu.CompilerParams(vmem_limit_bytes=DEC_VMEM),
        cost_estimate=pl.CostEstimate(
            flops=4 * 64 * 1088 * 128 * 16, bytes_accessed=9 << 20, transcendentals=64 * 1088 * 16
        ),
    )(lengths, q, ck, cv, nk, nv)


def prepare_kernel(k_ref, v_ref, o_ref):
    o_ref[:BLOCKS] = k_ref[...].reshape(BLOCKS, PAGE, HD)
    for i in range(BLOCKS):
        values = v_ref[i * PAGE : (i + 1) * PAGE, :].astype(jnp.float32)
        o_ref[BLOCKS + i] = values.T.astype(jnp.bfloat16)


def prepare_call(keys, values):
    return pl.pallas_call(
        prepare_kernel,
        name="prepare",
        out_shape=jax.ShapeDtypeStruct((2 * BLOCKS, PAGE, HD), jnp.bfloat16),
        cost_estimate=pl.CostEstimate(flops=0, bytes_accessed=1 << 19, transcendentals=0),
    )(keys, values)


def piece_seq(me, chips, swapped):
    core = me ^ 1 if swapped else me
    return (core + 2 * chips + SEQ) % SEQ


def plan_kernel(len_ref, map_ref, low_ref, pick_ref, slot_of):
    me = lax.axis_index("seq")
    own = lax.axis_index("pool")

    def place(b, _):
        page = map_ref[own, b]

        @pl.when(page // PAGES_DEV == me)
        def _():
            slot_of[page % PAGES_DEV] = b

        return 0

    lax.fori_loop(0, NPAGES, place, 0)
    row = lax.broadcasted_iota(jnp.int32, (PAGE, WINDOW), 0)
    col = lax.broadcasted_iota(jnp.int32, (PAGE, WINDOW), 1)
    for i in range(PAGES_DEV):
        b = slot_of[i]
        first = jnp.int32(0)
        start = jnp.int32(0)
        source = jnp.int32(0)
        count = jnp.int32(0)
        for prompt in range(NPROMPT):
            length = len_ref[own, prompt]
            blocks = (length + PAGE - 1) // PAGE
            inside = (b >= first) & (b < first + blocks)
            offset = (b - first) * PAGE
            source = jnp.where(inside, start + offset, source)
            count = jnp.where(inside, jnp.minimum(length - offset, PAGE), count)
            first = first + blocks
            start = start + length
        low = jnp.minimum(source // PAGE, SPAN // PAGE - 2)
        hit = ((low * PAGE + col) == (source + row)) & (row < count)
        pick_ref[i] = jnp.where(hit, 1.0, 0.0).astype(jnp.bfloat16)
        low_ref[i] = low


def plan_call(prompt_len, page_map):
    return pl.pallas_call(
        plan_kernel,
        name="plan_pages",
        in_specs=[pl.BlockSpec(memory_space=pltpu.SMEM)] * 2,
        out_specs=[pl.BlockSpec(memory_space=pltpu.SMEM), pl.BlockSpec(memory_space=pltpu.VMEM)],
        out_shape=[
            jax.ShapeDtypeStruct((PAGES_DEV,), jnp.int32),
            jax.ShapeDtypeStruct((PAGES_DEV, PAGE, WINDOW), jnp.bfloat16),
        ],
        scratch_shapes=[pltpu.SMEM((PAGES_DEV,), jnp.int32)],
        cost_estimate=pl.CostEstimate(flops=1 << 20, bytes_accessed=1 << 19, transcendentals=0),
    )(prompt_len, page_map)


def gather_kernel(low_ref, pick_ref, *refs):
    pieces = refs[: len(PIECES)]
    k_buf, v_buf, pk_ref, pv_ref = refs[len(PIECES) :]
    me = lax.axis_index("seq")
    k_buf[:PAD_BLOCKS] = jnp.zeros((PAD_BLOCKS, PAGE, HD), jnp.bfloat16)
    v_buf[:PAD_BLOCKS] = jnp.zeros((PAD_BLOCKS, PAGE, HD), jnp.bfloat16)
    for (chips, swapped), piece in zip(PIECES, pieces):
        at = pl.ds(piece_seq(me, chips, swapped) * BLOCKS + PAD_BLOCKS, BLOCKS)
        k_buf[at] = piece[:BLOCKS]
        v_buf[at] = piece[BLOCKS:]
    new_keys, new_values = [], []
    for i in range(PAGES_DEV):
        at = low_ref[i] + PAD_BLOCKS
        keys = k_buf[pl.ds(at, 2)].reshape(WINDOW, HD)
        values = jnp.concatenate([v_buf[at], v_buf[at + 1]], axis=1)
        new_keys.append(dot_nn(pick_ref[i], keys).astype(jnp.bfloat16))
        new_values.append(dot_nt(pick_ref[i], values).astype(jnp.bfloat16))
    for i in range(PAGES_DEV):
        here = slice(i * PAGE, (i + 1) * PAGE)
        pk_ref[here, :] = new_keys[i]
        pv_ref[here, :] = new_values[i]


def gather_call(lows, picks, pieces):
    rows = PAGES_DEV * PAGE
    return pl.pallas_call(
        gather_kernel,
        name="cut_pages",
        in_specs=[pl.BlockSpec(memory_space=pltpu.SMEM)]
        + [pl.BlockSpec(memory_space=pltpu.VMEM)] * (1 + len(PIECES)),
        out_specs=[pl.BlockSpec(memory_space=pltpu.VMEM)] * 4,
        out_shape=[jax.ShapeDtypeStruct((PAD_BLOCKS + SEQ * BLOCKS, PAGE, HD), jnp.bfloat16)] * 2
        + [jax.ShapeDtypeStruct((rows, HD), jnp.bfloat16)] * 2,
        compiler_params=pltpu.CompilerParams(vmem_limit_bytes=CUT_VMEM),
        cost_estimate=pl.CostEstimate(
            flops=12 * 2 * 128 * 256 * 128, bytes_accessed=5 << 20, transcendentals=0
        ),
    )(lows, picks, *pieces)


def prefill_kernel(len_ref, q_ref, k_buf, v_buf, o_hbm, o_ref, acc, total, weights, table, o_sem):
    me = lax.axis_index("seq")
    own = lax.axis_index("pool")
    chunks = TILE // CHUNK

    def tile_at(t):
        return pl.ds(pl.multiple_of(t * TILE, TILE), TILE)

    def o_copy(t):
        return pltpu.make_async_copy(o_ref.at[tile_at(t)], o_hbm.at[tile_at(t)], o_sem.at[t])

    acc[...] = jnp.zeros_like(acc)
    total[...] = jnp.zeros_like(total)

    def segment_start(position):
        start = jnp.int32(0)
        end = jnp.int32(0)
        for prompt in range(NPROMPT):
            end = end + len_ref[own, prompt]
            start = jnp.where(end <= position, end, start)
        return start

    def first_position(t):
        return me * ROWS + t * TILE_POS

    def tile_end(t):
        return first_position(t) + TILE_POS

    def tile_low(t):
        return segment_start(first_position(t))

    def block_count(t):
        return (tile_end(t) - tile_low(t) + KB - 1) // KB

    def block_start(t, j):
        return tile_end(t) - (j + 1) * KB

    def keys_at(start):
        at = pl.ds(start // PAGE + PAD_BLOCKS, KB // PAGE)
        return k_buf[at].reshape(KB, HD)

    def values_at(start):
        block = start // PAGE + PAD_BLOCKS
        return jnp.concatenate([v_buf[block + i] for i in range(KB // PAGE)], axis=1)

    def scores(start, t, c, width):
        at = pl.ds(pl.multiple_of(t * TILE + c * width, width), width)
        return dot_nt(keys_at(start), q_ref[at, :]) * SCALE2

    def allowed(start, t, c, width):
        lane = lax.broadcasted_iota(jnp.int32, (1, width), 1)
        high = first_position(t) + c * (width // HEADS) + lane // HEADS
        low = segment_start(high)
        k_pos = start + lax.broadcasted_iota(jnp.int32, (KB, width), 0)
        return (k_pos >= low) & (k_pos <= high)

    def put(t, j, c, slot, mode):
        at = slice(c * CHUNK, (c + 1) * CHUNK)
        start = block_start(t, j)
        if mode == "half":
            half = KB // 2
            blocks = half // PAGE
            keys = k_buf[pl.ds((start + half) // PAGE + PAD_BLOCKS, blocks)].reshape(half, HD)
            q_at = pl.ds(pl.multiple_of(t * TILE + c * CHUNK, CHUNK), CHUNK)
            terms = jnp.exp2(dot_nt(keys, q_ref[q_at, :]) * SCALE2)
            low = row_limits(t, c)[0] - (start + half)
            k_pos = lax.broadcasted_iota(jnp.int32, (half, CHUNK), 0)
            terms = jnp.where(k_pos >= low, terms, 0.0)
            weights[slot, :half, at] = jnp.zeros((half, CHUNK), jnp.bfloat16)
            weights[slot, half:, at] = terms.astype(jnp.bfloat16)
            total[t, :, at] += jnp.sum(terms.reshape(half // 8, 8, CHUNK), axis=0)
            return
        terms = jnp.exp2(scores(start, t, c, CHUNK))
        if mode != "none":
            terms = clear(terms, start, t, c, mode)
        weights[slot, :, at] = terms.astype(jnp.bfloat16)
        total[t, :, at] += jnp.sum(terms.reshape(KB // 8, 8, CHUNK), axis=0)

    def mix(t, j, c, slot):
        at = slice(c * CHUNK, (c + 1) * CHUNK)
        acc[t, :, at] += dot_nn(values_at(block_start(t, j)), weights[slot, :, at])

    def row_limits(t, c):
        lane = lax.broadcasted_iota(jnp.int32, (1, CHUNK), 1)
        high = first_position(t) + c * (CHUNK // HEADS) + lane // HEADS
        return segment_start(high), high

    def clear(terms, start, t, c, mode):
        low, high = row_limits(t, c)
        if mode == "both":
            low = low - start
            terms = jnp.where(lax.broadcasted_iota(jnp.int32, (KB, CHUNK), 0) >= low, terms, 0.0)
        cut = KB - TILE_POS
        k_pos = lax.broadcasted_iota(jnp.int32, (TILE_POS, CHUNK), 0)
        end = jnp.where(k_pos <= high - (start + cut), terms[cut:], 0.0)
        return jnp.concatenate([terms[:cut], end], axis=0)

    def slow_tile(t):
        width = SLOW_CHUNK

        def one(c, _):
            def block(j, carried):
                top, below, mixed = carried
                start = block_start(t, j)
                ok = allowed(start, t, c, width)
                here = jnp.where(ok, scores(start, t, c, width), NEG)
                new_top = jnp.maximum(top, jnp.max(here, axis=0, keepdims=True))
                terms = jnp.where(ok, jnp.exp2(here - new_top), 0.0)
                scale = jnp.exp2(top - new_top)
                below = below * scale + jnp.sum(terms, axis=0, keepdims=True)
                mixed = mixed * scale + dot_nn(values_at(start), terms.astype(jnp.bfloat16))
                return new_top, below, mixed

            _, below, mixed = lax.fori_loop(
                0,
                block_count(t),
                block,
                (
                    jnp.full((1, width), NEG, jnp.float32),
                    jnp.zeros((1, width), jnp.float32),
                    jnp.zeros((HD, width), jnp.float32),
                ),
            )
            at = pl.ds(pl.multiple_of(t * TILE + c * width, width), width)
            o_ref[at, :] = (mixed / below).T.astype(jnp.bfloat16)
            return 0

        lax.fori_loop(0, TILE // width, one, 0)

    def finish(t):
        below = jnp.sum(total[t], axis=0, keepdims=True)
        o_ref[tile_at(t), :] = (acc[t] / below).T.astype(jnp.bfloat16)
        bad = jnp.max(jnp.where((below >= LOW) & (below <= HIGH), 0.0, 1.0))

        @pl.when(bad > 0.0)
        def _():
            slow_tile(t)

        o_copy(t).start()

    def step(t, j, count, slot, last):
        wrap = j + 1 == count
        t2 = jnp.where(wrap, t + 1, t)
        j2 = jnp.where(wrap, 0, j + 1)
        t2 = jnp.minimum(t2, TILES - 1)
        start = block_start(t2, j2)
        bounded = table[1, t2] > start
        half = (j2 > 0) & (table[0, t2] >= start + KB // 2)
        both = bounded & jnp.logical_not(half)
        edge = (j2 == 0) & jnp.logical_not(bounded)
        inner = (j2 > 0) & jnp.logical_not(bounded)

        for mode, chosen in (("both", both), ("half", half), ("edge", edge), ("none", inner)):

            @pl.when(chosen & jnp.logical_not(last))
            def _():
                for c in range(chunks):
                    put(t2, j2, c, 1 - slot, mode)
                    mix(t, j, c, slot)

        @pl.when(last)
        def _():
            for c in range(chunks):
                mix(t, j, c, slot)

        @pl.when(wrap)
        def _():
            finish(t)

        return t2, j2, jnp.where(wrap, table[2, t2], count)

    items = jnp.int32(0)
    for t in range(TILES):
        blocks = block_count(t)
        table[0, t] = tile_low(t)
        table[1, t] = segment_start(tile_end(t) - 1)
        table[2, t] = blocks
        items = items + blocks
    for c in range(chunks):
        put(0, 0, c, 0, "both")

    def pair(i, state):
        state = step(*state, 0, 2 * i + 1 == items)

        def second(state):
            return step(*state, 1, 2 * i + 2 == items)

        return lax.cond(2 * i + 1 < items, second, lambda s: s, state)

    lax.fori_loop(0, (items + 1) // 2, pair, (jnp.int32(0), jnp.int32(0), table[2, 0]))
    for t in range(TILES):
        o_copy(t).wait()


def prefill_call(prompt_len, q, keys, values):
    return pl.pallas_call(
        prefill_kernel,
        name="prefill",
        in_specs=[pl.BlockSpec(memory_space=pltpu.SMEM)] + [pl.BlockSpec(memory_space=pltpu.VMEM)] * 3,
        out_specs=pl.BlockSpec(memory_space=pl.ANY),
        out_shape=jax.ShapeDtypeStruct(q.shape, jnp.bfloat16),
        scratch_shapes=[
            pltpu.VMEM((TILES * TILE, HD), jnp.bfloat16),
            pltpu.VMEM((TILES, HD, TILE), jnp.float32),
            pltpu.VMEM((TILES, 8, TILE), jnp.float32),
            pltpu.VMEM((2, KB, TILE), jnp.bfloat16),
            pltpu.SMEM((3, TILES), jnp.int32),
            pltpu.SemaphoreType.DMA((TILES,)),
        ],
        compiler_params=pltpu.CompilerParams(vmem_limit_bytes=VMEM),
        cost_estimate=pl.CostEstimate(
            flops=4 * 8192 * 2304 * 128, bytes_accessed=8 << 20, transcendentals=8192 * 2304
        ),
    )(prompt_len, q, keys, values)


def on_device(
    prefill_q,
    prefill_k,
    prefill_v,
    prompt_len,
    page_map,
    cache_k,
    cache_v,
    cache_len,
    decode_q,
    decode_k,
    decode_v,
):
    def chip_shift(x, chips):
        return lax.ppermute(x, "seq", [(j, (j + 2 * chips) % SEQ) for j in range(SEQ)])

    def core_swap(x):
        return lax.ppermute(x, "seq", [(j, j ^ 1) for j in range(SEQ)])

    q = prefill_q[0].reshape(ROWS * HEADS, HD)
    steps, slots = decode_q.shape[1], decode_q.shape[2]
    own = prepare_call(prefill_k[0, :, 0], prefill_v[0, :, 0])
    right = chip_shift(own, 1)
    left = chip_shift(own, -1)
    far = chip_shift(own, 2)
    pair = core_swap(own)
    decode_out = decode_call(
        cache_len,
        decode_q[0],
        cache_k[0, :, :, 0],
        cache_v[0, :, :, 0],
        decode_k[0, :, :, 0].reshape(steps * slots, HD),
        decode_v[0, :, :, 0].reshape(steps * slots, HD),
    )
    lows, picks = plan_call(prompt_len, page_map)
    right, left, far, decode_out, lows, picks = lax.optimization_barrier(
        (right, left, far, decode_out, lows, picks)
    )
    right_swap, left_swap = core_swap(right), core_swap(left)
    pieces = (own, pair, right, right_swap, left, left_swap, far, core_swap(far))
    keys, values, pk, pv = gather_call(lows, picks, pieces)
    page_k = lax.ppermute(pk, "pool", [(0, 1), (1, 0)])
    page_v = lax.ppermute(pv, "pool", [(0, 1), (1, 0)])
    prefill_out = prefill_call(prompt_len, q, keys, values)
    return (
        prefill_out.reshape(prefill_q.shape),
        page_k.reshape(1, PAGES_DEV, PAGE, 1, HD),
        page_v.reshape(1, PAGES_DEV, PAGE, 1, HD),
        decode_out[None],
    )


def solution(mesh):
    placed = (
        P("pool", "seq", "mp", None),
        P("pool", "seq", "mp", None),
        P("pool", "seq", "mp", None),
        P(),
        P(),
        P("pool", "seq", None, "mp", None),
        P("pool", "seq", None, "mp", None),
        P("pool", "seq"),
        P("pool", None, "seq", "mp", None),
        P("pool", None, "seq", "mp", None),
        P("pool", None, "seq", "mp", None),
    )
    return jax.shard_map(
        on_device,
        mesh=mesh,
        in_specs=placed,
        out_specs=(
            P("pool", "seq", "mp", None),
            P("pool", "seq", None, "mp", None),
            P("pool", "seq", None, "mp", None),
            P("pool", None, "seq", "mp", None),
        ),
        check_vma=False,
    )
```

```python
import functools

import jax
import jax.numpy as jnp
from jax import lax
from jax.experimental import pallas as pl
from jax.experimental.pallas import tpu as pltpu
from jax.sharding import PartitionSpec as P

PAGE = 128
PAGES_DEV = 6
NPROMPT = 8
NPAGES = 48
WINDOW = 2 * PAGE
SEQ = 8
ROWS = 512
HEADS = 16
HD = 128
SPAN = SEQ * ROWS
BLOCKS = ROWS // PAGE
PAD_BLOCKS = 4
KB = 512
TILE_POS = 128
TILE = TILE_POS * HEADS
TILES = ROWS // TILE_POS
CHUNK = 256
SLOW_CHUNK = 256
DEC_BLOCK = 4
DEC_VMEM = 56 * 1024 * 1024
PLACES = ((0, False), (0, True), (-1, False), (-1, True), (1, False), (1, True), (2, False), (2, True))
PIECES = PLACES
NEG = -1e30
SCALE = HD ** -0.5
SCALE2 = SCALE * 1.4426950408889634
LOW = 2.0 ** -80
HIGH = 2.0 ** 100
VMEM = 36 * 1024 * 1024
CUT_VMEM = 16 * 1024 * 1024

dot_nt = functools.partial(
    lax.dot_general, dimension_numbers=(((1,), (1,)), ((), ())), preferred_element_type=jnp.float32
)
dot_nn = functools.partial(jnp.dot, preferred_element_type=jnp.float32)


def decode_kernel(len_ref, q_ref, ck_ref, cv_ref, nk_ref, nv_ref, o_ref):
    steps, block = q_ref.shape[0], q_ref.shape[1]
    cache = ck_ref.shape[1]
    slots = nk_ref.shape[0] // steps
    rows = steps * HEADS
    first = pl.program_id(0) * block
    new_keys = nk_ref[...]
    new_values = nv_ref[...]
    lane = lax.broadcasted_iota(jnp.int32, (rows, cache), 1)
    new_lane = lax.broadcasted_iota(jnp.int32, (rows, steps * slots), 1)
    step = lax.broadcasted_iota(jnp.int32, (rows, steps * slots), 0) // HEADS
    each = range(block)
    queries = [q_ref[:, i].reshape(rows, HD) for i in each]
    old = [dot_nt(queries[i], ck_ref[i]) * SCALE for i in each]
    new = [dot_nt(queries[i], new_keys) * SCALE for i in each]
    old_w, new_w, total = [], [], []
    for i in each:
        old_i = jnp.where(lane < len_ref[0, first + i], old[i], NEG)
        new_ok = (new_lane % slots == first + i) & (new_lane // slots <= step)
        new_i = jnp.where(new_ok, new[i], NEG)
        top = jnp.maximum(
            jnp.max(old_i, axis=1, keepdims=True), jnp.max(new_i, axis=1, keepdims=True)
        )
        old_e = jnp.exp(old_i - top)
        new_e = jnp.exp(new_i - top)
        total.append(jnp.sum(old_e, axis=1, keepdims=True) + jnp.sum(new_e, axis=1, keepdims=True))
        old_w.append(old_e.astype(jnp.bfloat16))
        new_w.append(new_e.astype(jnp.bfloat16))
    for i in each:
        mixed = dot_nn(old_w[i], cv_ref[i]) + dot_nn(new_w[i], new_values)
        o_ref[:, i] = (mixed / total[i]).astype(jnp.bfloat16).reshape(steps, HEADS, HD)


def decode_call(lengths, q, ck, cv, nk, nv):
    steps, slots = q.shape[0], q.shape[1]
    cache = ck.shape[1]
    return pl.pallas_call(
        decode_kernel,
        name="decode",
        grid=(slots // DEC_BLOCK,),
        in_specs=[
            pl.BlockSpec(memory_space=pltpu.SMEM),
            pl.BlockSpec((steps, DEC_BLOCK, HEADS, HD), lambda i: (0, i, 0, 0)),
            pl.BlockSpec((DEC_BLOCK, cache, HD), lambda i: (i, 0, 0)),
            pl.BlockSpec((DEC_BLOCK, cache, HD), lambda i: (i, 0, 0)),
            pl.BlockSpec((steps * slots, HD), lambda i: (0, 0)),
            pl.BlockSpec((steps * slots, HD), lambda i: (0, 0)),
        ],
        out_specs=pl.BlockSpec((steps, DEC_BLOCK, HEADS, HD), lambda i: (0, i, 0, 0)),
        out_shape=jax.ShapeDtypeStruct(q.shape, jnp.bfloat16),
        compiler_params=pltpu.CompilerParams(vmem_limit_bytes=DEC_VMEM),
        cost_estimate=pl.CostEstimate(
            flops=4 * 64 * 1088 * 128 * 16, bytes_accessed=9 << 20, transcendentals=64 * 1088 * 16
        ),
    )(lengths, q, ck, cv, nk, nv)


def prepare_kernel(k_ref, v_ref, o_ref):
    o_ref[:BLOCKS] = k_ref[...].reshape(BLOCKS, PAGE, HD)
    for i in range(BLOCKS):
        values = v_ref[i * PAGE : (i + 1) * PAGE, :].astype(jnp.float32)
        o_ref[BLOCKS + i] = values.T.astype(jnp.bfloat16)


def prepare_call(keys, values):
    return pl.pallas_call(
        prepare_kernel,
        name="prepare",
        out_shape=jax.ShapeDtypeStruct((2 * BLOCKS, PAGE, HD), jnp.bfloat16),
        cost_estimate=pl.CostEstimate(flops=0, bytes_accessed=1 << 19, transcendentals=0),
    )(keys, values)


def piece_seq(me, chips, swapped):
    core = me ^ 1 if swapped else me
    return (core + 2 * chips + SEQ) % SEQ


def plan_kernel(len_ref, map_ref, low_ref, pick_ref, slot_of):
    me = lax.axis_index("seq")
    own = lax.axis_index("pool")

    def place(b, _):
        page = map_ref[own, b]

        @pl.when(page // PAGES_DEV == me)
        def _():
            slot_of[page % PAGES_DEV] = b

        return 0

    lax.fori_loop(0, NPAGES, place, 0)
    row = lax.broadcasted_iota(jnp.int32, (PAGE, WINDOW), 0)
    col = lax.broadcasted_iota(jnp.int32, (PAGE, WINDOW), 1)
    for i in range(PAGES_DEV):
        b = slot_of[i]
        first = jnp.int32(0)
        start = jnp.int32(0)
        source = jnp.int32(0)
        count = jnp.int32(0)
        for prompt in range(NPROMPT):
            length = len_ref[own, prompt]
            blocks = (length + PAGE - 1) // PAGE
            inside = (b >= first) & (b < first + blocks)
            offset = (b - first) * PAGE
            source = jnp.where(inside, start + offset, source)
            count = jnp.where(inside, jnp.minimum(length - offset, PAGE), count)
            first = first + blocks
            start = start + length
        low = jnp.minimum(source // PAGE, SPAN // PAGE - 2)
        hit = ((low * PAGE + col) == (source + row)) & (row < count)
        pick_ref[i] = jnp.where(hit, 1.0, 0.0).astype(jnp.bfloat16)
        low_ref[i] = low


def plan_call(prompt_len, page_map):
    return pl.pallas_call(
        plan_kernel,
        name="plan_pages",
        in_specs=[pl.BlockSpec(memory_space=pltpu.SMEM)] * 2,
        out_specs=[pl.BlockSpec(memory_space=pltpu.SMEM), pl.BlockSpec(memory_space=pltpu.VMEM)],
        out_shape=[
            jax.ShapeDtypeStruct((PAGES_DEV,), jnp.int32),
            jax.ShapeDtypeStruct((PAGES_DEV, PAGE, WINDOW), jnp.bfloat16),
        ],
        scratch_shapes=[pltpu.SMEM((PAGES_DEV,), jnp.int32)],
        cost_estimate=pl.CostEstimate(flops=1 << 20, bytes_accessed=1 << 19, transcendentals=0),
    )(prompt_len, page_map)


def gather_kernel(low_ref, pick_ref, *refs):
    pieces = refs[: len(PIECES)]
    k_buf, v_buf, pk_ref, pv_ref = refs[len(PIECES) :]
    me = lax.axis_index("seq")
    k_buf[:PAD_BLOCKS] = jnp.zeros((PAD_BLOCKS, PAGE, HD), jnp.bfloat16)
    v_buf[:PAD_BLOCKS] = jnp.zeros((PAD_BLOCKS, PAGE, HD), jnp.bfloat16)
    for (chips, swapped), piece in zip(PIECES, pieces):
        at = pl.ds(piece_seq(me, chips, swapped) * BLOCKS + PAD_BLOCKS, BLOCKS)
        k_buf[at] = piece[:BLOCKS]
        v_buf[at] = piece[BLOCKS:]
    new_keys, new_values = [], []
    for i in range(PAGES_DEV):
        at = low_ref[i] + PAD_BLOCKS
        keys = k_buf[pl.ds(at, 2)].reshape(WINDOW, HD)
        values = jnp.concatenate([v_buf[at], v_buf[at + 1]], axis=1)
        new_keys.append(dot_nn(pick_ref[i], keys).astype(jnp.bfloat16))
        new_values.append(dot_nt(pick_ref[i], values).astype(jnp.bfloat16))
    for i in range(PAGES_DEV):
        here = slice(i * PAGE, (i + 1) * PAGE)
        pk_ref[here, :] = new_keys[i]
        pv_ref[here, :] = new_values[i]


def gather_call(lows, picks, pieces):
    rows = PAGES_DEV * PAGE
    return pl.pallas_call(
        gather_kernel,
        name="cut_pages",
        in_specs=[pl.BlockSpec(memory_space=pltpu.SMEM)]
        + [pl.BlockSpec(memory_space=pltpu.VMEM)] * (1 + len(PIECES)),
        out_specs=[pl.BlockSpec(memory_space=pltpu.VMEM)] * 4,
        out_shape=[jax.ShapeDtypeStruct((PAD_BLOCKS + SEQ * BLOCKS, PAGE, HD), jnp.bfloat16)] * 2
        + [jax.ShapeDtypeStruct((rows, HD), jnp.bfloat16)] * 2,
        compiler_params=pltpu.CompilerParams(vmem_limit_bytes=CUT_VMEM),
        cost_estimate=pl.CostEstimate(
            flops=12 * 2 * 128 * 256 * 128, bytes_accessed=5 << 20, transcendentals=0
        ),
    )(lows, picks, *pieces)


def prefill_kernel(len_ref, q_ref, k_buf, v_buf, o_hbm, o_ref, acc, total, weights, table, o_sem):
    me = lax.axis_index("seq")
    own = lax.axis_index("pool")
    chunks = TILE // CHUNK

    def tile_at(t):
        return pl.ds(pl.multiple_of(t * TILE, TILE), TILE)

    def o_copy(t):
        return pltpu.make_async_copy(o_ref.at[tile_at(t)], o_hbm.at[tile_at(t)], o_sem.at[t])

    acc[...] = jnp.zeros_like(acc)
    total[...] = jnp.zeros_like(total)

    def segment_start(position):
        start = jnp.int32(0)
        end = jnp.int32(0)
        for prompt in range(NPROMPT):
            end = end + len_ref[own, prompt]
            start = jnp.where(end <= position, end, start)
        return start

    def first_position(t):
        return me * ROWS + t * TILE_POS

    def tile_end(t):
        return first_position(t) + TILE_POS

    def tile_low(t):
        return segment_start(first_position(t))

    def block_count(t):
        return (tile_end(t) - tile_low(t) + KB - 1) // KB

    def block_start(t, j):
        return tile_end(t) - (j + 1) * KB

    def keys_at(start):
        at = pl.ds(start // PAGE + PAD_BLOCKS, KB // PAGE)
        return k_buf[at].reshape(KB, HD)

    def values_at(start):
        block = start // PAGE + PAD_BLOCKS
        return jnp.concatenate([v_buf[block + i] for i in range(KB // PAGE)], axis=1)

    def scores(start, t, c, width):
        at = pl.ds(pl.multiple_of(t * TILE + c * width, width), width)
        return dot_nt(keys_at(start), q_ref[at, :]) * SCALE2

    def allowed(start, t, c, width):
        lane = lax.broadcasted_iota(jnp.int32, (1, width), 1)
        high = first_position(t) + c * (width // HEADS) + lane // HEADS
        low = segment_start(high)
        k_pos = start + lax.broadcasted_iota(jnp.int32, (KB, width), 0)
        return (k_pos >= low) & (k_pos <= high)

    def put(t, j, c, slot, mode):
        at = slice(c * CHUNK, (c + 1) * CHUNK)
        start = block_start(t, j)
        if mode == "half":
            half = KB // 2
            blocks = half // PAGE
            keys = k_buf[pl.ds((start + half) // PAGE + PAD_BLOCKS, blocks)].reshape(half, HD)
            q_at = pl.ds(pl.multiple_of(t * TILE + c * CHUNK, CHUNK), CHUNK)
            terms = jnp.exp2(dot_nt(keys, q_ref[q_at, :]) * SCALE2)
            low = row_limits(t, c)[0] - (start + half)
            k_pos = lax.broadcasted_iota(jnp.int32, (half, CHUNK), 0)
            terms = jnp.where(k_pos >= low, terms, 0.0)
            weights[slot, :half, at] = jnp.zeros((half, CHUNK), jnp.bfloat16)
            weights[slot, half:, at] = terms.astype(jnp.bfloat16)
            total[t, :, at] += jnp.sum(terms.reshape(half // 8, 8, CHUNK), axis=0)
            return
        terms = jnp.exp2(scores(start, t, c, CHUNK))
        if mode != "none":
            terms = clear(terms, start, t, c, mode)
        weights[slot, :, at] = terms.astype(jnp.bfloat16)
        total[t, :, at] += jnp.sum(terms.reshape(KB // 8, 8, CHUNK), axis=0)

    def mix(t, j, c, slot):
        at = slice(c * CHUNK, (c + 1) * CHUNK)
        acc[t, :, at] += dot_nn(values_at(block_start(t, j)), weights[slot, :, at])

    def row_limits(t, c):
        lane = lax.broadcasted_iota(jnp.int32, (1, CHUNK), 1)
        high = first_position(t) + c * (CHUNK // HEADS) + lane // HEADS
        return segment_start(high), high

    def clear(terms, start, t, c, mode):
        low, high = row_limits(t, c)
        if mode == "both":
            low = low - start
            terms = jnp.where(lax.broadcasted_iota(jnp.int32, (KB, CHUNK), 0) >= low, terms, 0.0)
        cut = KB - TILE_POS
        k_pos = lax.broadcasted_iota(jnp.int32, (TILE_POS, CHUNK), 0)
        end = jnp.where(k_pos <= high - (start + cut), terms[cut:], 0.0)
        return jnp.concatenate([terms[:cut], end], axis=0)

    def slow_tile(t):
        width = SLOW_CHUNK

        def one(c, _):
            def block(j, carried):
                top, below, mixed = carried
                start = block_start(t, j)
                ok = allowed(start, t, c, width)
                here = jnp.where(ok, scores(start, t, c, width), NEG)
                new_top = jnp.maximum(top, jnp.max(here, axis=0, keepdims=True))
                terms = jnp.where(ok, jnp.exp2(here - new_top), 0.0)
                scale = jnp.exp2(top - new_top)
                below = below * scale + jnp.sum(terms, axis=0, keepdims=True)
                mixed = mixed * scale + dot_nn(values_at(start), terms.astype(jnp.bfloat16))
                return new_top, below, mixed

            _, below, mixed = lax.fori_loop(
                0,
                block_count(t),
                block,
                (
                    jnp.full((1, width), NEG, jnp.float32),
                    jnp.zeros((1, width), jnp.float32),
                    jnp.zeros((HD, width), jnp.float32),
                ),
            )
            at = pl.ds(pl.multiple_of(t * TILE + c * width, width), width)
            o_ref[at, :] = (mixed / below).T.astype(jnp.bfloat16)
            return 0

        lax.fori_loop(0, TILE // width, one, 0)

    def finish(t):
        below = jnp.sum(total[t], axis=0, keepdims=True)
        o_ref[tile_at(t), :] = (acc[t] / below).T.astype(jnp.bfloat16)
        bad = jnp.max(jnp.where((below >= LOW) & (below <= HIGH), 0.0, 1.0))

        @pl.when(bad > 0.0)
        def _():
            slow_tile(t)

        o_copy(t).start()

    def step(t, j, count, slot, last):
        wrap = j + 1 == count
        t2 = jnp.where(wrap, t + 1, t)
        j2 = jnp.where(wrap, 0, j + 1)
        t2 = jnp.minimum(t2, TILES - 1)
        start = block_start(t2, j2)
        bounded = table[1, t2] > start
        half = (j2 > 0) & (table[0, t2] >= start + KB // 2)
        both = bounded & jnp.logical_not(half)
        edge = (j2 == 0) & jnp.logical_not(bounded)
        inner = (j2 > 0) & jnp.logical_not(bounded)

        for mode, chosen in (("both", both), ("half", half), ("edge", edge), ("none", inner)):

            @pl.when(chosen & jnp.logical_not(last))
            def _():
                for c in range(chunks):
                    put(t2, j2, c, 1 - slot, mode)
                    mix(t, j, c, slot)

        @pl.when(last)
        def _():
            for c in range(chunks):
                mix(t, j, c, slot)

        @pl.when(wrap)
        def _():
            finish(t)

        return t2, j2, jnp.where(wrap, table[2, t2], count)

    items = jnp.int32(0)
    for t in range(TILES):
        blocks = block_count(t)
        table[0, t] = tile_low(t)
        table[1, t] = segment_start(tile_end(t) - 1)
        table[2, t] = blocks
        items = items + blocks
    for c in range(chunks):
        put(0, 0, c, 0, "both")

    def pair(i, state):
        state = step(*state, 0, 2 * i + 1 == items)

        def second(state):
            return step(*state, 1, 2 * i + 2 == items)

        return lax.cond(2 * i + 1 < items, second, lambda s: s, state)

    lax.fori_loop(0, (items + 1) // 2, pair, (jnp.int32(0), jnp.int32(0), table[2, 0]))
    for t in range(TILES):
        o_copy(t).wait()


def prefill_call(prompt_len, q, keys, values):
    return pl.pallas_call(
        prefill_kernel,
        name="prefill",
        in_specs=[pl.BlockSpec(memory_space=pltpu.SMEM)] + [pl.BlockSpec(memory_space=pltpu.VMEM)] * 3,
        out_specs=pl.BlockSpec(memory_space=pl.ANY),
        out_shape=jax.ShapeDtypeStruct(q.shape, jnp.bfloat16),
        scratch_shapes=[
            pltpu.VMEM((TILES * TILE, HD), jnp.bfloat16),
            pltpu.VMEM((TILES, HD, TILE), jnp.float32),
            pltpu.VMEM((TILES, 8, TILE), jnp.float32),
            pltpu.VMEM((2, KB, TILE), jnp.bfloat16),
            pltpu.SMEM((3, TILES), jnp.int32),
            pltpu.SemaphoreType.DMA((TILES,)),
        ],
        compiler_params=pltpu.CompilerParams(vmem_limit_bytes=VMEM),
        cost_estimate=pl.CostEstimate(
            flops=4 * 8192 * 2304 * 128, bytes_accessed=8 << 20, transcendentals=8192 * 2304
        ),
    )(prompt_len, q, keys, values)


def on_device(
    prefill_q,
    prefill_k,
    prefill_v,
    prompt_len,
    page_map,
    cache_k,
    cache_v,
    cache_len,
    decode_q,
    decode_k,
    decode_v,
):
    def chip_shift(x, chips):
        return lax.ppermute(x, "seq", [(j, (j + 2 * chips) % SEQ) for j in range(SEQ)])

    def core_swap(x):
        return lax.ppermute(x, "seq", [(j, j ^ 1) for j in range(SEQ)])

    q = prefill_q[0].reshape(ROWS * HEADS, HD)
    steps, slots = decode_q.shape[1], decode_q.shape[2]
    own = prepare_call(prefill_k[0, :, 0], prefill_v[0, :, 0])
    right = chip_shift(own, 1)
    left = chip_shift(own, -1)
    far = chip_shift(own, 2)
    pair = core_swap(own)
    decode_out = decode_call(
        cache_len,
        decode_q[0],
        cache_k[0, :, :, 0],
        cache_v[0, :, :, 0],
        decode_k[0, :, :, 0].reshape(steps * slots, HD),
        decode_v[0, :, :, 0].reshape(steps * slots, HD),
    )
    lows, picks = plan_call(prompt_len, page_map)
    right, left, decode_out, lows, picks = lax.optimization_barrier(
        (right, left, decode_out, lows, picks)
    )
    right_swap, left_swap = core_swap(right), core_swap(left)
    pieces = (own, pair, right, right_swap, left, left_swap, far, core_swap(far))
    keys, values, pk, pv = gather_call(lows, picks, pieces)
    page_k = lax.ppermute(pk, "pool", [(0, 1), (1, 0)])
    page_v = lax.ppermute(pv, "pool", [(0, 1), (1, 0)])
    prefill_out = prefill_call(prompt_len, q, keys, values)
    return (
        prefill_out.reshape(prefill_q.shape),
        page_k.reshape(1, PAGES_DEV, PAGE, 1, HD),
        page_v.reshape(1, PAGES_DEV, PAGE, 1, HD),
        decode_out[None],
    )


def solution(mesh):
    placed = (
        P("pool", "seq", "mp", None),
        P("pool", "seq", "mp", None),
        P("pool", "seq", "mp", None),
        P(),
        P(),
        P("pool", "seq", None, "mp", None),
        P("pool", "seq", None, "mp", None),
        P("pool", "seq"),
        P("pool", None, "seq", "mp", None),
        P("pool", None, "seq", "mp", None),
        P("pool", None, "seq", "mp", None),
    )
    return jax.shard_map(
        on_device,
        mesh=mesh,
        in_specs=placed,
        out_specs=(
            P("pool", "seq", "mp", None),
            P("pool", "seq", None, "mp", None),
            P("pool", "seq", None, "mp", None),
            P("pool", None, "seq", "mp", None),
        ),
        check_vma=False,
    )
```

```python
import functools

import jax
import jax.numpy as jnp
from jax import lax
from jax.experimental import pallas as pl
from jax.experimental.pallas import tpu as pltpu
from jax.sharding import PartitionSpec as P

PAGE = 128
PAGES_DEV = 6
NPROMPT = 8
NPAGES = 48
WINDOW = 2 * PAGE
SEQ = 8
ROWS = 512
HEADS = 16
HD = 128
SPAN = SEQ * ROWS
BLOCKS = ROWS // PAGE
PAD_BLOCKS = 4
KB = 512
TILE_POS = 128
TILE = TILE_POS * HEADS
TILES = ROWS // TILE_POS
CHUNK = 256
SLOW_CHUNK = 256
DEC_BLOCK = 4
DEC_VMEM = 56 * 1024 * 1024
PLACES = ((0, False), (0, True), (-1, False), (-1, True), (1, False), (1, True), (2, False), (2, True))
PIECES = PLACES
NEG = -1e30
SCALE = HD ** -0.5
SCALE2 = SCALE * 1.4426950408889634
LOW = 2.0 ** -80
HIGH = 2.0 ** 100
VMEM = 36 * 1024 * 1024
CUT_VMEM = 16 * 1024 * 1024

dot_nt = functools.partial(
    lax.dot_general, dimension_numbers=(((1,), (1,)), ((), ())), preferred_element_type=jnp.float32
)
dot_nn = functools.partial(jnp.dot, preferred_element_type=jnp.float32)


def decode_kernel(len_ref, q_ref, ck_ref, cv_ref, nk_ref, nv_ref, o_ref):
    steps, block = q_ref.shape[0], q_ref.shape[1]
    cache = ck_ref.shape[1]
    slots = nk_ref.shape[0] // steps
    rows = steps * HEADS
    first = pl.program_id(0) * block
    new_keys = nk_ref[...]
    new_values = nv_ref[...]
    lane = lax.broadcasted_iota(jnp.int32, (rows, cache), 1)
    new_lane = lax.broadcasted_iota(jnp.int32, (rows, steps * slots), 1)
    step = lax.broadcasted_iota(jnp.int32, (rows, steps * slots), 0) // HEADS
    each = range(block)
    queries = [q_ref[:, i].reshape(rows, HD) for i in each]
    old = [dot_nt(queries[i], ck_ref[i]) * SCALE for i in each]
    new = [dot_nt(queries[i], new_keys) * SCALE for i in each]
    old_w, new_w, total = [], [], []
    for i in each:
        old_i = jnp.where(lane < len_ref[0, first + i], old[i], NEG)
        new_ok = (new_lane % slots == first + i) & (new_lane // slots <= step)
        new_i = jnp.where(new_ok, new[i], NEG)
        top = jnp.maximum(
            jnp.max(old_i, axis=1, keepdims=True), jnp.max(new_i, axis=1, keepdims=True)
        )
        old_e = jnp.exp(old_i - top)
        new_e = jnp.exp(new_i - top)
        total.append(jnp.sum(old_e, axis=1, keepdims=True) + jnp.sum(new_e, axis=1, keepdims=True))
        old_w.append(old_e.astype(jnp.bfloat16))
        new_w.append(new_e.astype(jnp.bfloat16))
    for i in each:
        mixed = dot_nn(old_w[i], cv_ref[i]) + dot_nn(new_w[i], new_values)
        o_ref[:, i] = (mixed / total[i]).astype(jnp.bfloat16).reshape(steps, HEADS, HD)


def decode_call(lengths, q, ck, cv, nk, nv):
    steps, slots = q.shape[0], q.shape[1]
    cache = ck.shape[1]
    return pl.pallas_call(
        decode_kernel,
        name="decode",
        grid=(slots // DEC_BLOCK,),
        in_specs=[
            pl.BlockSpec(memory_space=pltpu.SMEM),
            pl.BlockSpec((steps, DEC_BLOCK, HEADS, HD), lambda i: (0, i, 0, 0)),
            pl.BlockSpec((DEC_BLOCK, cache, HD), lambda i: (i, 0, 0)),
            pl.BlockSpec((DEC_BLOCK, cache, HD), lambda i: (i, 0, 0)),
            pl.BlockSpec((steps * slots, HD), lambda i: (0, 0)),
            pl.BlockSpec((steps * slots, HD), lambda i: (0, 0)),
        ],
        out_specs=pl.BlockSpec((steps, DEC_BLOCK, HEADS, HD), lambda i: (0, i, 0, 0)),
        out_shape=jax.ShapeDtypeStruct(q.shape, jnp.bfloat16),
        compiler_params=pltpu.CompilerParams(vmem_limit_bytes=DEC_VMEM),
        cost_estimate=pl.CostEstimate(
            flops=4 * 64 * 1088 * 128 * 16, bytes_accessed=9 << 20, transcendentals=64 * 1088 * 16
        ),
    )(lengths, q, ck, cv, nk, nv)


def prepare_kernel(k_ref, v_ref, o_ref):
    o_ref[:BLOCKS] = k_ref[...].reshape(BLOCKS, PAGE, HD)
    for i in range(BLOCKS):
        o_ref[BLOCKS + i] = v_ref[i * PAGE : (i + 1) * PAGE, :].T


def prepare_call(keys, values):
    return pl.pallas_call(
        prepare_kernel,
        name="prepare",
        out_shape=jax.ShapeDtypeStruct((2 * BLOCKS, PAGE, HD), jnp.bfloat16),
        cost_estimate=pl.CostEstimate(flops=0, bytes_accessed=1 << 19, transcendentals=0),
    )(keys, values)


def piece_seq(me, chips, swapped):
    core = me ^ 1 if swapped else me
    return (core + 2 * chips + SEQ) % SEQ


def plan_kernel(len_ref, map_ref, low_ref, pick_ref, slot_of):
    me = lax.axis_index("seq")
    own = lax.axis_index("pool")

    def place(b, _):
        page = map_ref[own, b]

        @pl.when(page // PAGES_DEV == me)
        def _():
            slot_of[page % PAGES_DEV] = b

        return 0

    lax.fori_loop(0, NPAGES, place, 0)
    row = lax.broadcasted_iota(jnp.int32, (PAGE, WINDOW), 0)
    col = lax.broadcasted_iota(jnp.int32, (PAGE, WINDOW), 1)
    for i in range(PAGES_DEV):
        b = slot_of[i]
        first = jnp.int32(0)
        start = jnp.int32(0)
        source = jnp.int32(0)
        count = jnp.int32(0)
        for prompt in range(NPROMPT):
            length = len_ref[own, prompt]
            blocks = (length + PAGE - 1) // PAGE
            inside = (b >= first) & (b < first + blocks)
            offset = (b - first) * PAGE
            source = jnp.where(inside, start + offset, source)
            count = jnp.where(inside, jnp.minimum(length - offset, PAGE), count)
            first = first + blocks
            start = start + length
        low = jnp.minimum(source // PAGE, SPAN // PAGE - 2)
        hit = ((low * PAGE + col) == (source + row)) & (row < count)
        pick_ref[i] = jnp.where(hit, 1.0, 0.0).astype(jnp.bfloat16)
        low_ref[i] = low


def plan_call(prompt_len, page_map):
    return pl.pallas_call(
        plan_kernel,
        name="plan_pages",
        in_specs=[pl.BlockSpec(memory_space=pltpu.SMEM)] * 2,
        out_specs=[pl.BlockSpec(memory_space=pltpu.SMEM), pl.BlockSpec(memory_space=pltpu.VMEM)],
        out_shape=[
            jax.ShapeDtypeStruct((PAGES_DEV,), jnp.int32),
            jax.ShapeDtypeStruct((PAGES_DEV, PAGE, WINDOW), jnp.bfloat16),
        ],
        scratch_shapes=[pltpu.SMEM((PAGES_DEV,), jnp.int32)],
        cost_estimate=pl.CostEstimate(flops=1 << 20, bytes_accessed=1 << 19, transcendentals=0),
    )(prompt_len, page_map)


def gather_kernel(low_ref, pick_ref, *refs):
    pieces = refs[: len(PIECES)]
    k_buf, v_buf, pk_ref, pv_ref = refs[len(PIECES) :]
    me = lax.axis_index("seq")
    k_buf[:PAD_BLOCKS] = jnp.zeros((PAD_BLOCKS, PAGE, HD), jnp.bfloat16)
    v_buf[:PAD_BLOCKS] = jnp.zeros((PAD_BLOCKS, PAGE, HD), jnp.bfloat16)
    for (chips, swapped), piece in zip(PIECES, pieces):
        at = pl.ds(piece_seq(me, chips, swapped) * BLOCKS + PAD_BLOCKS, BLOCKS)
        k_buf[at] = piece[:BLOCKS]
        v_buf[at] = piece[BLOCKS:]
    new_keys, new_values = [], []
    for i in range(PAGES_DEV):
        at = low_ref[i] + PAD_BLOCKS
        keys = k_buf[pl.ds(at, 2)].reshape(WINDOW, HD)
        values = jnp.concatenate([v_buf[at], v_buf[at + 1]], axis=1)
        new_keys.append(dot_nn(pick_ref[i], keys).astype(jnp.bfloat16))
        new_values.append(dot_nt(pick_ref[i], values).astype(jnp.bfloat16))
    for i in range(PAGES_DEV):
        here = slice(i * PAGE, (i + 1) * PAGE)
        pk_ref[here, :] = new_keys[i]
        pv_ref[here, :] = new_values[i]


def gather_call(lows, picks, pieces):
    rows = PAGES_DEV * PAGE
    return pl.pallas_call(
        gather_kernel,
        name="cut_pages",
        in_specs=[pl.BlockSpec(memory_space=pltpu.SMEM)]
        + [pl.BlockSpec(memory_space=pltpu.VMEM)] * (1 + len(PIECES)),
        out_specs=[pl.BlockSpec(memory_space=pltpu.VMEM)] * 4,
        out_shape=[jax.ShapeDtypeStruct((PAD_BLOCKS + SEQ * BLOCKS, PAGE, HD), jnp.bfloat16)] * 2
        + [jax.ShapeDtypeStruct((rows, HD), jnp.bfloat16)] * 2,
        compiler_params=pltpu.CompilerParams(vmem_limit_bytes=CUT_VMEM),
        cost_estimate=pl.CostEstimate(
            flops=12 * 2 * 128 * 256 * 128, bytes_accessed=5 << 20, transcendentals=0
        ),
    )(lows, picks, *pieces)


def prefill_kernel(len_ref, q_ref, k_buf, v_buf, o_hbm, o_ref, acc, total, weights, table, o_sem):
    me = lax.axis_index("seq")
    own = lax.axis_index("pool")
    chunks = TILE // CHUNK

    def tile_at(t):
        return pl.ds(pl.multiple_of(t * TILE, TILE), TILE)

    def o_copy(t):
        return pltpu.make_async_copy(o_ref.at[tile_at(t)], o_hbm.at[tile_at(t)], o_sem.at[t])

    acc[...] = jnp.zeros_like(acc)
    total[...] = jnp.zeros_like(total)

    def segment_start(position):
        start = jnp.int32(0)
        end = jnp.int32(0)
        for prompt in range(NPROMPT):
            end = end + len_ref[own, prompt]
            start = jnp.where(end <= position, end, start)
        return start

    def first_position(t):
        return me * ROWS + t * TILE_POS

    def tile_end(t):
        return first_position(t) + TILE_POS

    def tile_low(t):
        return segment_start(first_position(t))

    def block_count(t):
        return (tile_end(t) - tile_low(t) + KB - 1) // KB

    def block_start(t, j):
        return tile_end(t) - (j + 1) * KB

    def keys_at(start):
        at = pl.ds(start // PAGE + PAD_BLOCKS, KB // PAGE)
        return k_buf[at].reshape(KB, HD)

    def values_at(start):
        block = start // PAGE + PAD_BLOCKS
        return jnp.concatenate([v_buf[block + i] for i in range(KB // PAGE)], axis=1)

    def scores(start, t, c, width):
        at = pl.ds(pl.multiple_of(t * TILE + c * width, width), width)
        return dot_nt(keys_at(start), q_ref[at, :]) * SCALE2

    def allowed(start, t, c, width):
        lane = lax.broadcasted_iota(jnp.int32, (1, width), 1)
        high = first_position(t) + c * (width // HEADS) + lane // HEADS
        low = segment_start(high)
        k_pos = start + lax.broadcasted_iota(jnp.int32, (KB, width), 0)
        return (k_pos >= low) & (k_pos <= high)

    def put(t, j, c, slot, mode):
        at = slice(c * CHUNK, (c + 1) * CHUNK)
        start = block_start(t, j)
        if mode == "half":
            half = KB // 2
            blocks = half // PAGE
            keys = k_buf[pl.ds((start + half) // PAGE + PAD_BLOCKS, blocks)].reshape(half, HD)
            q_at = pl.ds(pl.multiple_of(t * TILE + c * CHUNK, CHUNK), CHUNK)
            terms = jnp.exp2(dot_nt(keys, q_ref[q_at, :]) * SCALE2)
            low = row_limits(t, c)[0] - (start + half)
            k_pos = lax.broadcasted_iota(jnp.int32, (half, CHUNK), 0)
            terms = jnp.where(k_pos >= low, terms, 0.0)
            weights[slot, :half, at] = jnp.zeros((half, CHUNK), jnp.bfloat16)
            weights[slot, half:, at] = terms.astype(jnp.bfloat16)
            total[t, :, at] += jnp.sum(terms.reshape(half // 8, 8, CHUNK), axis=0)
            return
        terms = jnp.exp2(scores(start, t, c, CHUNK))
        if mode != "none":
            terms = clear(terms, start, t, c, mode)
        weights[slot, :, at] = terms.astype(jnp.bfloat16)
        total[t, :, at] += jnp.sum(terms.reshape(KB // 8, 8, CHUNK), axis=0)

    def mix(t, j, c, slot):
        at = slice(c * CHUNK, (c + 1) * CHUNK)
        acc[t, :, at] += dot_nn(values_at(block_start(t, j)), weights[slot, :, at])

    def row_limits(t, c):
        lane = lax.broadcasted_iota(jnp.int32, (1, CHUNK), 1)
        high = first_position(t) + c * (CHUNK // HEADS) + lane // HEADS
        return segment_start(high), high

    def clear(terms, start, t, c, mode):
        low, high = row_limits(t, c)
        if mode == "both":
            low = low - start
            terms = jnp.where(lax.broadcasted_iota(jnp.int32, (KB, CHUNK), 0) >= low, terms, 0.0)
        cut = KB - TILE_POS
        k_pos = lax.broadcasted_iota(jnp.int32, (TILE_POS, CHUNK), 0)
        end = jnp.where(k_pos <= high - (start + cut), terms[cut:], 0.0)
        return jnp.concatenate([terms[:cut], end], axis=0)

    def slow_tile(t):
        width = SLOW_CHUNK

        def one(c, _):
            def block(j, carried):
                top, below, mixed = carried
                start = block_start(t, j)
                ok = allowed(start, t, c, width)
                here = jnp.where(ok, scores(start, t, c, width), NEG)
                new_top = jnp.maximum(top, jnp.max(here, axis=0, keepdims=True))
                terms = jnp.where(ok, jnp.exp2(here - new_top), 0.0)
                scale = jnp.exp2(top - new_top)
                below = below * scale + jnp.sum(terms, axis=0, keepdims=True)
                mixed = mixed * scale + dot_nn(values_at(start), terms.astype(jnp.bfloat16))
                return new_top, below, mixed

            _, below, mixed = lax.fori_loop(
                0,
                block_count(t),
                block,
                (
                    jnp.full((1, width), NEG, jnp.float32),
                    jnp.zeros((1, width), jnp.float32),
                    jnp.zeros((HD, width), jnp.float32),
                ),
            )
            at = pl.ds(pl.multiple_of(t * TILE + c * width, width), width)
            o_ref[at, :] = (mixed / below).T.astype(jnp.bfloat16)
            return 0

        lax.fori_loop(0, TILE // width, one, 0)

    def finish(t):
        below = jnp.sum(total[t], axis=0, keepdims=True)
        o_ref[tile_at(t), :] = (acc[t] / below).T.astype(jnp.bfloat16)
        bad = jnp.max(jnp.where((below >= LOW) & (below <= HIGH), 0.0, 1.0))

        @pl.when(bad > 0.0)
        def _():
            slow_tile(t)

        o_copy(t).start()

    def step(t, j, count, slot, last):
        wrap = j + 1 == count
        t2 = jnp.where(wrap, t + 1, t)
        j2 = jnp.where(wrap, 0, j + 1)
        t2 = jnp.minimum(t2, TILES - 1)
        start = block_start(t2, j2)
        bounded = table[1, t2] > start
        half = (j2 > 0) & (table[0, t2] >= start + KB // 2)
        both = bounded & jnp.logical_not(half)
        edge = (j2 == 0) & jnp.logical_not(bounded)
        inner = (j2 > 0) & jnp.logical_not(bounded)

        for mode, chosen in (("both", both), ("half", half), ("edge", edge), ("none", inner)):

            @pl.when(chosen & jnp.logical_not(last))
            def _():
                for c in range(chunks):
                    put(t2, j2, c, 1 - slot, mode)
                    mix(t, j, c, slot)

        @pl.when(last)
        def _():
            for c in range(chunks):
                mix(t, j, c, slot)

        @pl.when(wrap)
        def _():
            finish(t)

        return t2, j2, jnp.where(wrap, table[2, t2], count)

    items = jnp.int32(0)
    for t in range(TILES):
        blocks = block_count(t)
        table[0, t] = tile_low(t)
        table[1, t] = segment_start(tile_end(t) - 1)
        table[2, t] = blocks
        items = items + blocks
    for c in range(chunks):
        put(0, 0, c, 0, "both")

    def pair(i, state):
        state = step(*state, 0, 2 * i + 1 == items)

        def second(state):
            return step(*state, 1, 2 * i + 2 == items)

        return lax.cond(2 * i + 1 < items, second, lambda s: s, state)

    lax.fori_loop(0, (items + 1) // 2, pair, (jnp.int32(0), jnp.int32(0), table[2, 0]))
    for t in range(TILES):
        o_copy(t).wait()


def prefill_call(prompt_len, q, keys, values):
    return pl.pallas_call(
        prefill_kernel,
        name="prefill",
        in_specs=[pl.BlockSpec(memory_space=pltpu.SMEM)] + [pl.BlockSpec(memory_space=pltpu.VMEM)] * 3,
        out_specs=pl.BlockSpec(memory_space=pl.ANY),
        out_shape=jax.ShapeDtypeStruct(q.shape, jnp.bfloat16),
        scratch_shapes=[
            pltpu.VMEM((TILES * TILE, HD), jnp.bfloat16),
            pltpu.VMEM((TILES, HD, TILE), jnp.float32),
            pltpu.VMEM((TILES, 8, TILE), jnp.float32),
            pltpu.VMEM((2, KB, TILE), jnp.bfloat16),
            pltpu.SMEM((3, TILES), jnp.int32),
            pltpu.SemaphoreType.DMA((TILES,)),
        ],
        compiler_params=pltpu.CompilerParams(vmem_limit_bytes=VMEM),
        cost_estimate=pl.CostEstimate(
            flops=4 * 8192 * 2304 * 128, bytes_accessed=8 << 20, transcendentals=8192 * 2304
        ),
    )(prompt_len, q, keys, values)


def on_device(
    prefill_q,
    prefill_k,
    prefill_v,
    prompt_len,
    page_map,
    cache_k,
    cache_v,
    cache_len,
    decode_q,
    decode_k,
    decode_v,
):
    def chip_shift(x, chips):
        return lax.ppermute(x, "seq", [(j, (j + 2 * chips) % SEQ) for j in range(SEQ)])

    def core_swap(x):
        return lax.ppermute(x, "seq", [(j, j ^ 1) for j in range(SEQ)])

    q = prefill_q[0].reshape(ROWS * HEADS, HD)
    steps, slots = decode_q.shape[1], decode_q.shape[2]
    own = prepare_call(prefill_k[0, :, 0], prefill_v[0, :, 0])
    right = chip_shift(own, 1)
    left = chip_shift(own, -1)
    far = chip_shift(own, 2)
    pair = core_swap(own)
    decode_out = decode_call(
        cache_len,
        decode_q[0],
        cache_k[0, :, :, 0],
        cache_v[0, :, :, 0],
        decode_k[0, :, :, 0].reshape(steps * slots, HD),
        decode_v[0, :, :, 0].reshape(steps * slots, HD),
    )
    lows, picks = plan_call(prompt_len, page_map)
    right, left, decode_out, lows, picks = lax.optimization_barrier(
        (right, left, decode_out, lows, picks)
    )
    right_swap, left_swap = core_swap(right), core_swap(left)
    pieces = (own, pair, right, right_swap, left, left_swap, far, core_swap(far))
    keys, values, pk, pv = gather_call(lows, picks, pieces)
    page_k = lax.ppermute(pk, "pool", [(0, 1), (1, 0)])
    page_v = lax.ppermute(pv, "pool", [(0, 1), (1, 0)])
    prefill_out = prefill_call(prompt_len, q, keys, values)
    return (
        prefill_out.reshape(prefill_q.shape),
        page_k.reshape(1, PAGES_DEV, PAGE, 1, HD),
        page_v.reshape(1, PAGES_DEV, PAGE, 1, HD),
        decode_out[None],
    )


def solution(mesh):
    placed = (
        P("pool", "seq", "mp", None),
        P("pool", "seq", "mp", None),
        P("pool", "seq", "mp", None),
        P(),
        P(),
        P("pool", "seq", None, "mp", None),
        P("pool", "seq", None, "mp", None),
        P("pool", "seq"),
        P("pool", None, "seq", "mp", None),
        P("pool", None, "seq", "mp", None),
        P("pool", None, "seq", "mp", None),
    )
    return jax.shard_map(
        on_device,
        mesh=mesh,
        in_specs=placed,
        out_specs=(
            P("pool", "seq", "mp", None),
            P("pool", "seq", None, "mp", None),
            P("pool", "seq", None, "mp", None),
            P("pool", None, "seq", "mp", None),
        ),
        check_vma=False,
    )
```
